256 devices in a mesh: blk: 16 (over y_hi, x, core), col: 16 (over z, y_lo).
Axes of the slice: x: 4, y: 4 (y_hi: 2, y_lo: 2; y = y_hi * 2 + y_lo), z: 8, core: 2. Of those that a mesh axis runs over, the one named last changes fastest.
Arguments:
- queries: bfloat16 [128, 256, 1152], P('blk', 'col'), may hold values from -200 to 200
- key_states: bfloat16 [32, 64, 1152], P('blk', 'col'), may hold values from -6 to 6
- values: bfloat16 [32, 64, 1152], P('blk', 'col'), may hold values from -6 to 6
- saved_out: bfloat16 [128, 256, 1152], P('blk', 'col'), may hold values from -6 to 6
- grad_out: bfloat16 [128, 256, 1152], P('blk', 'col'), may hold values from -96 to 96
- w_qkv: bfloat16 [1152, 3456], replicated, may hold values from -0.1875 to 0.1875
- w_patch: bfloat16 [256, 1152], replicated, may hold values from -0.375 to 0.375
Outputs:
- grad_image: float32 [1024, 2048], P('blk', 'col')
The draws below stay inside these ranges and needn't reach their ends.
All inputs are finite; a program needn't handle non-finite values.
Results may differ from the reference program's by a relative error of at most 0.0055.
Values may be sent and summed in bfloat16 or wider, within the bound.
No kernel may reach another device: no remote copies, remote signals or barrier semaphores. Data moves between devices by JAX's collectives and lax.ppermute only.
A program may use at most 64 MiB of HBM per device.

```python
import jax
import jax.numpy as jnp
from jax import lax

D = 1152
HEADS = 16
KERNEL = 16
POOL = 4
GR = 128
GC = 256


def base_pair(key):
    pooled_count = GR // POOL * (GC // POOL)
    keys_base = jax.random.truncated_normal(jax.random.fold_in(key, 21), -6.0, 6.0, (pooled_count, D), jnp.float32)
    query_base = jax.random.truncated_normal(jax.random.fold_in(key, 22), -6.0, 6.0, (GR * GC, D), jnp.float32)
    return (keys_base, query_base)


def draw_key_states(key, part):
    keys_base, query_base = base_pair(key)
    result = keys_base
    return result.reshape(GR // POOL, GC // POOL, D).astype(jnp.bfloat16)


def draw_queries(key, part):
    keys_base, query_base = base_pair(key)
    result = query_base
    return result.reshape(GR, GC, D).astype(jnp.bfloat16)


def level_of(rng, extent, pieces, smallest, high):
    level = 1.0
    for axis_at, parts in pieces:
        heights = jax.random.uniform(jax.random.fold_in(jax.random.fold_in(rng, 6), axis_at), (parts,), jnp.float32, smallest / len(pieces), high / len(pieces))
        level = level * jnp.repeat(jnp.exp(heights), extent[axis_at] // parts).reshape((-1,) + (1,) * (len(extent) - 1 - axis_at))
    return level


def scatter_about(stream_key, shape, scale, most, cuts=(), dtype=jnp.bfloat16):
    gain = level_of(stream_key, shape, cuts, -0.22, 0.18) if cuts else 1.0
    entries = jax.random.normal(stream_key, shape, jnp.float32) * scale * gain
    return jnp.minimum(jnp.maximum(entries, -most), most).astype(dtype)


def setup_inputs(seed: int = 0) -> dict:
    splits = jax.random.split(jax.random.key(seed), 8)
    queries = draw_queries(jax.random.fold_in(splits[7], 71), 0)
    key_states = draw_key_states(jax.random.fold_in(splits[7], 71), 0)
    values = scatter_about(splits[2], (GR // POOL, GC // POOL, D), 1.0, 6.0, ((0, 16), (1, 16)))
    saved_out = scatter_about(splits[3], (GR, GC, D), 1.0, 6.0, ((0, 16), (1, 16)))
    grad_out = scatter_about(splits[4], (GR, GC, D), 16.0, 96.0, ((0, 16), (1, 16)))
    w_qkv = scatter_about(splits[5], (D, 3 * D), D ** -0.5, 0.1875)
    w_patch = scatter_about(splits[6], (KERNEL * KERNEL, D), (KERNEL * KERNEL) ** -0.5, 0.375)
    return {"queries": queries, "key_states": key_states, "values": values, "saved_out": saved_out, "grad_out": grad_out, "w_qkv": w_qkv, "w_patch": w_patch}


def fold_blocks(padded_patch, row_count, col_count):
    total = None
    for row_step in (0, 1):
        for col_step in (0, 1):
            piece = padded_patch[1 - row_step:row_count + 2 - row_step, 1 - col_step:col_count + 2 - col_step, row_step, :, col_step, :]
            total = piece if total is None else total + piece
    return total.transpose(0, 2, 1, 3).reshape(8 * (row_count + 1), 8 * (col_count + 1))


def expand_pooled(pooled):
    spread = jnp.repeat(jnp.repeat(pooled, POOL, axis=0), POOL, axis=1)
    return spread * (1.0 / (POOL * POOL))


def reference(queries, key_states, values, saved_out, grad_out, w_qkv, w_patch):
    head_dim = D // HEADS
    count = GR * GC
    pooled_count = (GR // POOL) * (GC // POOL)
    score_scale = head_dim ** -0.5

    def split_heads(array, rows):
        return array.reshape(rows, HEADS, head_dim).transpose(1, 0, 2)

    def one_head(arrays):
        query_h, key_h, value_h, out_h, grad_h = arrays
        scores = score_scale * jnp.dot(query_h, key_h.T, preferred_element_type=jnp.float32)
        log_norms = jax.nn.logsumexp(scores, axis=1)
        probs = jnp.exp(scores - log_norms[:, None])
        prob_half = probs.astype(jnp.bfloat16)
        grad_probs = jnp.dot(grad_h, value_h.T, preferred_element_type=jnp.float32)
        out_dots = jnp.sum(grad_h.astype(jnp.float32) * out_h.astype(jnp.float32), axis=1)
        grad_scores = (probs * (grad_probs - out_dots[:, None])).astype(jnp.bfloat16)
        grad_query = (score_scale * jnp.dot(grad_scores, key_h, preferred_element_type=jnp.float32)).astype(jnp.bfloat16)
        grad_key = (score_scale * jnp.dot(grad_scores.T, query_h, preferred_element_type=jnp.float32)).astype(jnp.bfloat16)
        grad_value = jnp.dot(prob_half.T, grad_h, preferred_element_type=jnp.float32).astype(jnp.bfloat16)
        return grad_query, grad_key, grad_value

    grad_query, grad_key, grad_value = lax.map(one_head, (split_heads(queries, count), split_heads(key_states, pooled_count), split_heads(values, pooled_count), split_heads(saved_out, count), split_heads(grad_out, count)))
    query_full = grad_query.transpose(1, 0, 2).reshape(GR, GC, D)
    key_full = expand_pooled(grad_key.transpose(1, 0, 2).reshape(GR // POOL, GC // POOL, D))
    value_full = expand_pooled(grad_value.transpose(1, 0, 2).reshape(GR // POOL, GC // POOL, D))
    joined = jnp.concatenate([query_full, key_full, value_full], axis=2).reshape(count, 3 * D)
    grad_embed = jnp.dot(joined, w_qkv.T, preferred_element_type=jnp.float32).astype(jnp.bfloat16)
    grad_patch = jnp.dot(grad_embed, w_patch.T, preferred_element_type=jnp.float32)
    grad_patch = grad_patch.reshape(GR, GC, 2, 8, 2, 8)
    padded = jnp.pad(grad_patch, ((1, 1), (1, 1), (0, 0), (0, 0), (0, 0), (0, 0)))
    canvas = fold_blocks(padded, GR, GC)
    return canvas[4:-4, 4:-4]
```

```python
import math

import jax
import jax.numpy as jnp
from jax import lax
from jax.experimental import pallas as pl
from jax.experimental.pallas import tpu as pltpu
from jax.sharding import Mesh, PartitionSpec as P

D = 1152
HEADS = 16
DH = D // HEADS
POOL = 4
SCALE = DH**-0.5
SCALE2 = SCALE * math.log2(math.e)
ROWS, COLS = 8, 16
TOK = ROWS * COLS
CELLS = TOK // POOL**2
FPAD = 80
KEYS = 2048
HEAD_AXES = ("yh", "x", "yl")
BLK = ("yh", "x", "c")
COL = ("z", "yl")
NT = (((1,), (1,)), ((), ()))
VMEM = 48 * 2**20
bf16, f32 = jnp.bfloat16, jnp.float32


def call(kernel, shapes, scratch=()):
    return pl.pallas_call(
        kernel,
        out_shape=shapes,
        scratch_shapes=scratch,
        compiler_params=pltpu.CompilerParams(vmem_limit_bytes=VMEM),
    )


def pack_kernel(q_ref, g_ref, o_ref, k_ref, v_ref, send_ref):
    q_t = q_ref[...].astype(f32).T
    g_t = g_ref[...].astype(f32).T
    prod = g_t * o_ref[...].astype(f32).T
    keys = k_ref[...].astype(f32)
    vals = v_ref[...].astype(f32)
    row = lax.broadcasted_iota(jnp.int32, (8, TOK), 0)
    lanes = jnp.zeros((CELLS, 128 - DH), f32)
    lane = lax.broadcasted_iota(jnp.int32, (CELLS, 128 - DH), 1)
    ones = jnp.where(lane < 3, 1.0, 0.0).astype(f32)
    for h in range(HEADS):
        part = slice(h * DH, (h + 1) * DH)
        dot = -jnp.sum(prod[part], axis=0, keepdims=True)
        high = dot.astype(bf16).astype(f32)
        mid = (dot - high).astype(bf16).astype(f32)
        low = dot - high - mid
        dots = jnp.where(row == 0, high, jnp.where(row == 1, mid, jnp.where(row == 2, low, 0.0)))
        send_ref[h, 0:FPAD, :] = jnp.concatenate([q_t[part], jnp.zeros((8, TOK), f32)]).astype(bf16)
        send_ref[h, FPAD : 2 * FPAD, :] = jnp.concatenate([g_t[part], dots]).astype(bf16)
        k_h = jnp.concatenate([keys[:, part], lanes], axis=1)
        v_h = jnp.concatenate([vals[:, part], ones], axis=1)
        send_ref[h, 2 * FPAD : 2 * FPAD + 16, :] = jnp.concatenate([k_h, v_h]).astype(bf16)


def attention_kernel(
    qg_ref, kv_own, kv_other, dq_ref, own_ref, other_ref, k_s, v_s, kt_s, e_s, dk_s, dv_s
):
    half = KEYS // 2
    for at, kv_ref in ((0, kv_own), (half, kv_other)):
        kv = kv_ref[...].astype(f32).reshape(8 * HEADS, 2, CELLS, 128)
        keys = kv[:, 0].reshape(half, 128)
        k_s[at : at + half] = keys.astype(bf16)
        kt_s[:, at : at + half] = keys.T.astype(bf16)
        v_s[at : at + half] = kv[:, 1].reshape(half, 128).astype(bf16)
    dk_s[...] = jnp.zeros_like(dk_s)
    dv_s[...] = jnp.zeros_like(dv_s)
    step = 512
    blocks = [slice(at, at + step) for at in range(0, KEYS, step)]

    def tile(t, _):
        q_t = jnp.concatenate([qg_ref[2 * t, 0:FPAD], qg_ref[2 * t + 1, 0:FPAD]], axis=1)
        g_t = jnp.concatenate(
            [qg_ref[2 * t, FPAD : 2 * FPAD], qg_ref[2 * t + 1, FPAD : 2 * FPAD]], axis=1
        )
        top = jnp.full((1, 2 * TOK), -jnp.inf, f32)
        for b in blocks:
            scores = jnp.dot(k_s[b, 0:FPAD], q_t, preferred_element_type=f32)
            e_s[b] = scores
            top = jnp.maximum(top, jnp.max(scores, axis=0, keepdims=True))
        top = top * SCALE2
        total = jnp.zeros((1, 2 * TOK), f32)
        for b in blocks:
            exps = jnp.exp2(e_s[b] * SCALE2 - top)
            e_s[b] = exps
            total = total + jnp.sum(exps, axis=0, keepdims=True)
        inverse = 1.0 / total
        dq = jnp.zeros((FPAD, 2 * TOK), f32)
        for b in blocks:
            probs = e_s[b] * inverse
            half_probs = probs.astype(bf16)
            shifted = jnp.dot(v_s[b, 0:FPAD], g_t, preferred_element_type=f32)
            ds = (probs * shifted).astype(bf16)
            dk_s[b, 0:FPAD] += lax.dot_general(ds, q_t, NT, preferred_element_type=f32)
            dv_s[b, 0:FPAD] += lax.dot_general(half_probs, g_t, NT, preferred_element_type=f32)
            dq = dq + jnp.dot(kt_s[0:FPAD, b], ds, preferred_element_type=f32)
        dq = (dq * SCALE).astype(bf16)
        dq_ref[2 * t] = dq[:, 0:TOK]
        dq_ref[2 * t + 1] = dq[:, TOK:]
        return 0

    lax.fori_loop(0, HEADS // 2, tile, 0)
    dk_t = dk_s[...].T
    dv_t = dv_s[...].T
    for out, at in ((own_ref, 0), (other_ref, half)):
        for b in range(8):
            keys = slice(at + b * 128, at + (b + 1) * 128)
            out[b, 0:DH] = dk_t[0:DH, keys] * SCALE
            out[b, DH : 2 * DH] = dv_t[0:DH, keys]


def pack_back_kernel(dq_ref, mine_ref, came_ref, send_ref):
    total = mine_ref[...] + came_ref[...].astype(f32)
    lanes = jnp.zeros((128, 128 - DH), f32)
    dk = jnp.concatenate([total[0:DH].T, lanes], axis=1)
    dv = jnp.concatenate([total[DH : 2 * DH].T, lanes], axis=1)
    send_ref[:, 0:FPAD, :] = dq_ref[...]
    for a in range(HEADS):
        cells = slice(a * CELLS, (a + 1) * CELLS)
        send_ref[a, FPAD : FPAD + 16, :] = jnp.concatenate([dk[cells], dv[cells]]).astype(bf16)


def embed_kernel(back_ref, q_hi, q_lo, kv_hi, kv_lo, out_ref):
    dq_t = back_ref[:, 0:FPAD, :].reshape(HEADS * FPAD, TOK)
    rows = (((0,), (0,)), ((), ()))
    patch = lax.dot_general(dq_t, q_hi[...], rows, preferred_element_type=f32)
    patch = patch + lax.dot_general(dq_t, q_lo[...], rows, preferred_element_type=f32)
    cell = jnp.zeros((CELLS, 256), f32)
    for h in range(HEADS):
        pooled = back_ref[h, FPAD : FPAD + 16, :].astype(f32)
        for part in (0, 1):
            mine = pooled[part * CELLS : (part + 1) * CELLS].astype(bf16)
            for w in (kv_hi, kv_lo):
                cell = cell + jnp.dot(mine, w[part, h], preferred_element_type=f32)
    cell = cell * (1.0 / POOL**2)
    spread = cell.reshape(CELLS // 4, 4, 1, 256)
    spread = jnp.broadcast_to(spread, (CELLS // 4, 4, POOL, 256)).reshape(CELLS // 4, 1, COLS, 256)
    spread = jnp.broadcast_to(spread, (CELLS // 4, POOL, COLS, 256)).reshape(TOK, 256)
    out_ref[...] = patch + spread


def swapped(x, axis, by):
    peers = lax.axis_size(axis)
    return lax.ppermute(x, axis, [(i, i ^ by) for i in range(peers)])


def fold_blocks(padded_patch, row_count, col_count):
    total = None
    for row_step in (0, 1):
        for col_step in (0, 1):
            piece = padded_patch[
                1 - row_step : row_count + 2 - row_step,
                1 - col_step : col_count + 2 - col_step,
                row_step,
                :,
                col_step,
                :,
            ]
            total = piece if total is None else total + piece
    return total.transpose(0, 2, 1, 3).reshape(8 * (row_count + 1), 8 * (col_count + 1))


def edges_added(canvas, axis, dim):
    count = lax.axis_size(axis)
    size = canvas.shape[dim]
    forward = [(i, i + 1) for i in range(count - 1)]
    backward = [(target, source) for source, target in forward]
    last = lax.ppermute(lax.slice_in_dim(canvas, size - 4, size, axis=dim), axis, forward)
    first = lax.ppermute(lax.slice_in_dim(canvas, 0, 4, axis=dim), axis, backward)
    parts = [
        lax.slice_in_dim(canvas, 4, 8, axis=dim) + last,
        lax.slice_in_dim(canvas, 8, size - 8, axis=dim),
        lax.slice_in_dim(canvas, size - 8, size - 4, axis=dim) + first,
    ]
    return jnp.concatenate(parts, axis=dim)


def combined_weights(w_qkv, w_patch):
    both = lax.dot_general(w_qkv, w_patch, (((0,), (1,)), ((), ())), preferred_element_type=f32)
    both = both.reshape(3, HEADS, DH, 256)
    high = lax.reduce_precision(both, 8, 7)
    low = both - high

    def padded(x, to):
        return jnp.pad(x.astype(bf16), ((0, 0),) * (x.ndim - 2) + ((0, to - DH), (0, 0)))

    return [
        padded(high[0], FPAD).reshape(HEADS * FPAD, 256),
        padded(low[0], FPAD).reshape(HEADS * FPAD, 256),
        padded(high[1:], 128),
        padded(low[1:], 128),
    ]


def on_device(queries, key_states, values, saved_out, grad_out, w_qkv, w_patch):
    weights = combined_weights(w_qkv, w_patch)
    send = call(pack_kernel, jax.ShapeDtypeStruct((HEADS, 2 * FPAD + 16, TOK), bf16))(
        queries.reshape(TOK, D),
        grad_out.reshape(TOK, D),
        saved_out.reshape(TOK, D),
        key_states.reshape(CELLS, D),
        values.reshape(CELLS, D),
    )
    got = lax.all_to_all(send, HEAD_AXES, 0, 0, tiled=True)
    kv = got[:, 2 * FPAD :, :][None]
    for by in (1, 2, 4):
        kv = jnp.concatenate([kv, swapped(kv, "z", by)])
    kv_other = swapped(kv, "c", 1)
    grads = jax.ShapeDtypeStruct((8, 2 * DH, 128), f32)
    dq, own, other = call(
        attention_kernel,
        [jax.ShapeDtypeStruct((HEADS, FPAD, TOK), bf16), grads, grads],
        [
            pltpu.VMEM((KEYS, 128), bf16),
            pltpu.VMEM((KEYS, 128), bf16),
            pltpu.VMEM((128, KEYS), bf16),
            pltpu.VMEM((KEYS, 2 * TOK), f32),
            pltpu.VMEM((KEYS, 128), f32),
            pltpu.VMEM((KEYS, 128), f32),
        ],
    )(got, kv, kv_other)
    mine = own + swapped(other, "c", 1)
    for by in (4, 2):
        mine = mine[:by] + swapped(mine[by:].astype(bf16), "z", by).astype(f32)
    came = swapped(mine[1].astype(bf16), "z", 1)
    send = call(pack_back_kernel, jax.ShapeDtypeStruct((HEADS, FPAD + 16, TOK), bf16))(
        dq, mine[0], came
    )
    back = lax.all_to_all(send, HEAD_AXES, 0, 0, tiled=True)
    patch = call(embed_kernel, jax.ShapeDtypeStruct((TOK, 256), f32))(back, *weights)
    patch = patch.reshape(ROWS, COLS, 2, 8, 2, 8)
    patch = jnp.pad(patch, ((1, 1), (1, 1), (0, 0), (0, 0), (0, 0), (0, 0)))
    canvas = fold_blocks(patch, ROWS, COLS)
    canvas = edges_added(canvas, BLK, 0)
    return edges_added(canvas, COL, 1)


def solution(mesh):
    fine = Mesh(mesh.devices.reshape(2, 4, 2, 8, 2), ("yh", "x", "c", "z", "yl"))
    split = P(BLK, COL, None)
    return jax.shard_map(
        on_device,
        mesh=fine,
        in_specs=(split, split, split, split, split, P(), P()),
        out_specs=P(BLK, COL),
        check_vma=False,
    )
```

```python
import math

import jax
import jax.numpy as jnp
import ml_dtypes
import numpy as np
from jax import lax
from jax.experimental import pallas as pl
from jax.experimental.pallas import tpu as pltpu
from jax.sharding import Mesh, PartitionSpec as P

D = 1152
HEADS = 16
DH = D // HEADS
POOL = 4
SCALE = DH**-0.5
SCALE2 = SCALE * math.log2(math.e)
ROWS, COLS = 8, 16
TOK = ROWS * COLS
CELLS = TOK // POOL**2
FPAD = 80
KEYS = 2048
HEAD_AXES = ("yh", "x", "yl")
BLK = ("yh", "x", "c")
COL = ("z", "yl")
NT = (((1,), (1,)), ((), ()))
VMEM = 48 * 2**20
bf16, f32 = jnp.bfloat16, jnp.float32


def call(kernel, shapes, scratch=()):
    return pl.pallas_call(
        kernel,
        out_shape=shapes,
        scratch_shapes=scratch,
        compiler_params=pltpu.CompilerParams(vmem_limit_bytes=VMEM),
    )


def pack_kernel(q_in, g_in, o_in, k_in, v_in, send_ref, q_ref, g_ref, o_ref, k_ref, v_ref, sems):
    copies = []
    quarter = TOK // 4
    for source, target in ((k_in, k_ref), (v_in, v_ref)):
        copies.append((source, target))
    for source, target in ((q_in, q_ref), (g_in, g_ref), (o_in, o_ref)):
        for at in range(0, TOK, quarter):
            copies.append((source.at[at : at + quarter], target.at[at : at + quarter]))
    copies = [pltpu.make_async_copy(*pair, sems.at[n]) for n, pair in enumerate(copies)]
    for copy in copies:
        copy.start()
    for copy in copies:
        copy.wait()
    q_t = q_ref[...].astype(f32).T
    g_t = g_ref[...].astype(f32).T
    prod = g_t * o_ref[...].astype(f32).T
    keys = jnp.concatenate([k_ref[0].astype(f32), k_ref[1].astype(f32)])
    vals = jnp.concatenate([v_ref[0].astype(f32), v_ref[1].astype(f32)])
    row = lax.broadcasted_iota(jnp.int32, (8, TOK), 0)
    lanes = jnp.zeros((CELLS, 128 - DH), f32)
    for h in range(HEADS):
        part = slice(h * DH, (h + 1) * DH)
        dot = -jnp.sum(prod[part], axis=0, keepdims=True)
        high = dot.astype(bf16).astype(f32)
        mid = (dot - high).astype(bf16).astype(f32)
        low = dot - high - mid
        dots = jnp.where(row == 0, high, jnp.where(row == 1, mid, jnp.where(row == 2, low, 0.0)))
        send_ref[h, 0:FPAD, :] = jnp.concatenate([q_t[part], jnp.zeros((8, TOK), f32)]).astype(bf16)
        send_ref[h, FPAD : 2 * FPAD, :] = jnp.concatenate([g_t[part], dots]).astype(bf16)
        k_h = jnp.concatenate([keys[:, part], lanes], axis=1)
        v_h = jnp.concatenate([vals[:, part], lanes], axis=1)
        send_ref[h, 2 * FPAD : 2 * FPAD + 16, :] = jnp.concatenate([k_h, v_h]).astype(bf16)


def keys_kernel(got_ref, out_ref):
    kv = got_ref[...].astype(f32).reshape(HEADS, 2, CELLS, 128)
    k_t = kv[:, 0].reshape(128, 128).T
    v_t = kv[:, 1].reshape(128, 128).T
    out_ref[...] = jnp.concatenate([k_t[0:DH], v_t[0:DH]]).astype(bf16)


def attention_kernel(
    qg_ref, kv_own, kv_other, dq_ref, own_ref, other_ref, k_s, v_s, kt_s, e_s, dk_s, dv_s
):
    half = KEYS // 2
    lane = lax.broadcasted_iota(jnp.int32, (128, 128), 1)
    pad = jnp.zeros((128 - DH, 128), f32)
    for at, kv_ref in ((0, kv_own), (half, kv_other)):
        for b in range(8):
            kv = kv_ref[b].astype(f32)
            keys = slice(at + b * 128, at + (b + 1) * 128)
            k_t = jnp.concatenate([kv[0:DH], pad])
            kt_s[:, keys] = k_t.astype(bf16)
            k_s[keys] = k_t.T.astype(bf16)
            v = jnp.concatenate([kv[DH:], pad]).T
            v_s[keys] = jnp.where((lane >= DH) & (lane < DH + 3), 1.0, v).astype(bf16)
    dk_s[...] = jnp.zeros_like(dk_s)
    dv_s[...] = jnp.zeros_like(dv_s)
    step = 512
    blocks = [slice(at, at + step) for at in range(0, KEYS, step)]

    def tile(t, _):
        q_t = jnp.concatenate([qg_ref[2 * t, 0:FPAD], qg_ref[2 * t + 1, 0:FPAD]], axis=1)
        g_t = jnp.concatenate(
            [qg_ref[2 * t, FPAD : 2 * FPAD], qg_ref[2 * t + 1, FPAD : 2 * FPAD]], axis=1
        )
        top = jnp.full((1, 2 * TOK), -jnp.inf, f32)
        for b in blocks:
            scores = jnp.dot(k_s[b, 0:FPAD], q_t, preferred_element_type=f32)
            e_s[b] = scores
            top = jnp.maximum(top, jnp.max(scores, axis=0, keepdims=True))
        top = top * SCALE2
        total = jnp.zeros((1, 2 * TOK), f32)
        for b in blocks:
            exps = jnp.exp2(e_s[b] * SCALE2 - top)
            e_s[b] = exps
            total = total + jnp.sum(exps, axis=0, keepdims=True)
        inverse = 1.0 / total
        dq = jnp.zeros((FPAD, 2 * TOK), f32)
        for b in blocks:
            probs = e_s[b] * inverse
            half_probs = probs.astype(bf16)
            shifted = jnp.dot(v_s[b, 0:FPAD], g_t, preferred_element_type=f32)
            ds = (probs * shifted).astype(bf16)
            dk_s[b, 0:FPAD] += lax.dot_general(ds, q_t, NT, preferred_element_type=f32)
            dv_s[b, 0:FPAD] += lax.dot_general(half_probs, g_t, NT, preferred_element_type=f32)
            dq = dq + jnp.dot(kt_s[0:FPAD, b], ds, preferred_element_type=f32)
        dq = (dq * SCALE).astype(bf16)
        dq_ref[2 * t] = dq[:, 0:TOK]
        dq_ref[2 * t + 1] = dq[:, TOK:]
        return 0

    lax.fori_loop(0, HEADS // 2, tile, 0)
    dk_t = dk_s[...].T
    dv_t = dv_s[...].T
    for out, at in ((own_ref, 0), (other_ref, half)):
        for b in range(8):
            keys = slice(at + b * 128, at + (b + 1) * 128)
            out[b, 0:DH] = dk_t[0:DH, keys] * SCALE
            out[b, DH : 2 * DH] = dv_t[0:DH, keys]


def pack_back_kernel(dq_ref, mine_ref, came_ref, send_ref):
    total = mine_ref[...] + came_ref[...].astype(f32)
    lanes = jnp.zeros((128, 128 - DH), f32)
    dk = jnp.concatenate([total[0:DH].T, lanes], axis=1)
    dv = jnp.concatenate([total[DH : 2 * DH].T, lanes], axis=1)
    send_ref[:, 0:FPAD, :] = dq_ref[...]
    for a in range(HEADS):
        cells = slice(a * CELLS, (a + 1) * CELLS)
        send_ref[a, FPAD : FPAD + 16, :] = jnp.concatenate([dk[cells], dv[cells]]).astype(bf16)


def weights_kernel(patch_ref, qkv_ref, high_ref, low_ref):
    both = jnp.dot(patch_ref[...], qkv_ref[...], preferred_element_type=f32)
    high = both.astype(bf16)
    high_ref[...] = high
    low_ref[...] = (both - high.astype(f32)).astype(bf16)


def embed_kernel(core_ref, back_ref, high_ref, low_ref, tile_ref, canvas_ref, core_out, chip_out, joined, sheet):
    cols = (((0,), (0,)), ((), ()))
    cell = lax.broadcasted_iota(jnp.int32, (CELLS, TOK), 0)
    token = lax.broadcasted_iota(jnp.int32, (CELLS, TOK), 1)
    holds = (token // (POOL * COLS) == cell // 4) & (token % COLS // POOL == cell % 4)
    spread = jnp.where(holds, 1.0 / POOL**2, 0.0).astype(bf16)
    for h in range(HEADS):
        mine = back_ref[h].astype(f32)
        rows = slice(h * DH, (h + 1) * DH)
        joined[rows] = mine[0:DH]
        for part in (0, 1):
            at = FPAD + part * CELLS
            pooled = mine[at : at + CELLS].astype(bf16)
            wide = lax.dot_general(pooled, spread, cols, preferred_element_type=f32)
            joined[(part + 1) * D + h * DH : (part + 1) * D + (h + 1) * DH] = wide[0:DH]
    values = joined[...].astype(bf16)
    patch = jnp.dot(high_ref[...], values, preferred_element_type=f32)
    patch = patch + jnp.dot(low_ref[...], values, preferred_element_type=f32)
    patch = jnp.concatenate([patch[0:128].T, patch[128:256].T])
    high = patch.astype(bf16)
    rest = patch - high.astype(f32)
    mid = rest.astype(bf16)
    low = (rest - mid.astype(f32)).astype(bf16)
    lane = lax.broadcasted_iota(jnp.int32, (2 * TOK, 256), 1)
    row = lax.broadcasted_iota(jnp.int32, (2 * TOK, 256), 0)
    here = lane % 128 // 8 == row % COLS
    sheet[...] = jnp.zeros_like(sheet)
    parts = jnp.concatenate([high, mid, low], axis=1)
    for pair in range(8):
        wide = jnp.dot(parts, tile_ref[:, pair * 256 : (pair + 1) * 256], preferred_element_type=f32)
        wide = jnp.where(here, wide, 0.0)
        wide = jnp.sum(wide.reshape(2 * ROWS, COLS, 256), axis=1)
        for k in (0, 1):
            u = 2 * pair + k
            for side in (0, 1):
                piece = wide[side * ROWS : (side + 1) * ROWS, k * 128 : (k + 1) * 128]
                sheet[side, pl.ds(u, ROWS, stride=8), :] += piece
    left = sheet[0]
    right = sheet[1]
    lane = lax.broadcasted_iota(jnp.int32, left.shape, 1)
    center = jnp.where(lane < 124, pltpu.roll(left, 124, 1), 0.0)
    center = center + jnp.where(lane >= 4, pltpu.roll(right, 4, 1), 0.0)
    edges = jnp.where(lane < 4, left, pltpu.roll(right, 8, 1))
    canvas = jnp.concatenate([center, jnp.where(lane < 8, edges, 0.0)], axis=1)
    canvas_ref[...] = canvas
    first = core_ref[0] == 0
    core_out[...] = jnp.where(first, canvas[68:72], canvas[0:4])
    chip_out[...] = jnp.where(first, canvas[0:4], canvas[68:72])


def rows_kernel(at_ref, canvas_ref, core_ref, chip_ref, center_ref, near_out, far_out):
    first = at_ref[0] == 0
    above = jnp.where(first, chip_ref[...], core_ref[...])
    below = jnp.where(first, core_ref[...], chip_ref[...])
    quiet = jnp.zeros((56, 256), f32)
    canvas = canvas_ref[4:68] + jnp.concatenate([above, quiet, below])
    center_ref[...] = canvas[:, 0:128]
    edges = canvas[:, 128:256].T[0:8]
    left, right = edges[0:4], edges[4:8]
    begins = at_ref[1] == 0
    near_out[...] = jnp.where(begins, right, left)
    far_out[...] = jnp.where(begins, left, right)


def cols_kernel(at_ref, center_ref, near_ref, far_ref, out_ref):
    begins = at_ref[1] == 0
    left = jnp.where(begins, far_ref[...], near_ref[...])
    right = jnp.where(begins, near_ref[...], far_ref[...])
    quiet = jnp.zeros((120, 64), f32)
    out_ref[...] = center_ref[...] + jnp.concatenate([left, quiet, right]).T


def swapped(x, axis, by):
    peers = lax.axis_size(axis)
    return lax.ppermute(x, axis, [(i, i ^ by) for i in range(peers)])


def neighbours(x, axis):
    peers = lax.axis_size(axis)
    pairs = [(i, i + 1) for i in range(1, peers - 1, 2)]
    return lax.ppermute(x, axis, pairs + [(target, source) for source, target in pairs])


def tile_matrix():
    rows = np.arange(128)[:, None]
    lanes = np.arange(2048)[None, :]
    tile = (lanes // 128 == rows // 8) & (lanes % 8 == rows % 8)
    return np.concatenate([tile] * 3).astype(ml_dtypes.bfloat16)


def combined_weights(w_qkv, w_patch):
    ordered = w_patch.reshape(16, 2, 8, D).transpose(1, 0, 2, 3).reshape(256, D)
    width = 384
    shape = jax.ShapeDtypeStruct((256, 3 * D), bf16)
    return pl.pallas_call(
        weights_kernel,
        grid=(3 * D // width,),
        in_specs=[pl.BlockSpec((256, D), lambda n: (0, 0)), pl.BlockSpec((D, width), lambda n: (0, n))],
        out_specs=[pl.BlockSpec((256, width), lambda n: (0, n))] * 2,
        out_shape=[shape, shape],
        cost_estimate=pl.CostEstimate(flops=2 * 256 * D * 3 * D, bytes_accessed=6 * D * D, transcendentals=0),
    )(ordered, w_qkv)


def on_device(queries, key_states, values, saved_out, grad_out, w_qkv, w_patch):
    weights = combined_weights(w_qkv, w_patch)
    anywhere = pl.BlockSpec(memory_space=pl.ANY)
    tokens = pltpu.VMEM((TOK, D), bf16)
    cells = pltpu.VMEM((2, 4, D), bf16)
    send = pl.pallas_call(
        pack_kernel,
        in_specs=[anywhere] * 5,
        out_shape=jax.ShapeDtypeStruct((HEADS, 2 * FPAD + 16, TOK), bf16),
        scratch_shapes=[tokens, tokens, tokens, cells, cells, pltpu.SemaphoreType.DMA((14,))],
        compiler_params=pltpu.CompilerParams(vmem_limit_bytes=VMEM),
    )(
        queries.reshape(TOK, D),
        grad_out.reshape(TOK, D),
        saved_out.reshape(TOK, D),
        key_states,
        values,
    )
    got = lax.all_to_all(send, HEAD_AXES, 0, 0, tiled=True)
    kv = pl.pallas_call(
        keys_kernel,
        grid=(1,),
        in_specs=[pl.BlockSpec((HEADS, 16, 128), lambda n: (0, 10, 0))],
        out_specs=pl.BlockSpec((2 * DH, 128), lambda n: (0, 0)),
        out_shape=jax.ShapeDtypeStruct((2 * DH, 128), bf16),
    )(got)[None]
    for by in (4, 2, 1):
        kv = jnp.concatenate([kv, swapped(kv, "z", by)])
    kv_other = swapped(kv, "c", 1)
    kv, kv_other, *weights = lax.optimization_barrier((kv, kv_other, *weights))
    grads = jax.ShapeDtypeStruct((8, 2 * DH, 128), f32)
    dq, own, other = call(
        attention_kernel,
        [jax.ShapeDtypeStruct((HEADS, FPAD, TOK), bf16), grads, grads],
        [
            pltpu.VMEM((KEYS, 128), bf16),
            pltpu.VMEM((KEYS, 128), bf16),
            pltpu.VMEM((128, KEYS), bf16),
            pltpu.VMEM((KEYS, 2 * TOK), f32),
            pltpu.VMEM((KEYS, 128), f32),
            pltpu.VMEM((KEYS, 128), f32),
        ],
    )(got, kv, kv_other)
    mine = own + swapped(other, "c", 1)
    for by, keep in ((1, 4), (2, 2)):
        mine = mine[:keep] + swapped(mine[keep:].astype(bf16), "z", by).astype(f32)
    came = swapped(mine[1].astype(bf16), "z", 4)
    send = call(pack_back_kernel, jax.ShapeDtypeStruct((HEADS, FPAD + 16, TOK), bf16))(
        dq, mine[0], came
    )
    back = lax.all_to_all(send, HEAD_AXES, 0, 0, tiled=True)
    at = jnp.stack([lax.axis_index("c"), lax.axis_index("yl")]).astype(jnp.int32)
    scalars = pl.BlockSpec(memory_space=pltpu.SMEM)
    whole = pl.BlockSpec(memory_space=pltpu.VMEM)
    strip = jax.ShapeDtypeStruct((4, 256), f32)
    canvas, to_core, to_chip = pl.pallas_call(
        embed_kernel,
        in_specs=[scalars] + [whole] * 4,
        out_shape=[jax.ShapeDtypeStruct((72, 256), f32), strip, strip],
        scratch_shapes=[pltpu.VMEM((3 * D, TOK), f32), pltpu.VMEM((2, 72, 128), f32)],
        compiler_params=pltpu.CompilerParams(vmem_limit_bytes=VMEM),
    )(at, back, *weights, tile_matrix())
    strip = jax.ShapeDtypeStruct((4, 64), f32)
    center, to_near, to_far = pl.pallas_call(
        rows_kernel,
        in_specs=[scalars] + [whole] * 3,
        out_shape=[jax.ShapeDtypeStruct((64, 128), f32), strip, strip],
    )(at, canvas, swapped(to_core, "c", 1), neighbours(to_chip, BLK))
    return pl.pallas_call(
        cols_kernel,
        in_specs=[scalars] + [whole] * 3,
        out_shape=jax.ShapeDtypeStruct((64, 128), f32),
    )(at, center, swapped(to_near, "yl", 1), neighbours(to_far, COL))


def solution(mesh):
    fine = Mesh(mesh.devices.reshape(2, 4, 2, 8, 2), ("yh", "x", "c", "z", "yl"))
    split = P(BLK, COL, None)
    return jax.shard_map(
        on_device,
        mesh=fine,
        in_specs=(split, split, split, split, split, P(), P()),
        out_specs=P(BLK, COL),
        check_vma=False,
    )
```

```python
import functools
import math

import jax
import jax.numpy as jnp
from jax import lax
from jax.experimental import pallas as pl
from jax.experimental.pallas import tpu as pltpu
from jax.sharding import Mesh, PartitionSpec as P

D = 1152
HEADS = 16
DH = D // HEADS
POOL = 4
SCALE = DH**-0.5
SCALE2 = SCALE * math.log2(math.e)
ROWS, COLS = 8, 16
TOK = ROWS * COLS
CELLS = TOK // POOL**2
FPAD = 80
KEYS = 2048
HEAD_AXES = ("yh", "x", "yl")
BLK = ("yh", "x", "c")
COL = ("z", "yl")
NT = (((1,), (1,)), ((), ()))
WHOLE = pl.BlockSpec(memory_space=pltpu.VMEM)
ANYWHERE = pl.BlockSpec(memory_space=pl.ANY)
bf16, f32 = jnp.bfloat16, jnp.float32


def call(kernel, out, mib, scratch=(), specs=None, **more):
    if specs is not None:
        more["in_specs"] = specs
    return pl.pallas_call(
        kernel,
        out_shape=out,
        scratch_shapes=scratch,
        compiler_params=pltpu.CompilerParams(vmem_limit_bytes=mib * 2**20 if mib else None),
        **more,
    )


def pack_kernel(q_in, g_in, o_in, k_in, v_in, out_ref, q_ref, g_ref, o_ref, k_ref, v_ref, send_ref, sems, out_sems):
    copies = []
    quarter = TOK // 4
    for source, target in ((k_in, k_ref), (v_in, v_ref)):
        copies.append((source, target))
    for source, target in ((q_in, q_ref), (g_in, g_ref), (o_in, o_ref)):
        for at in range(0, TOK, quarter):
            copies.append((source.at[at : at + quarter], target.at[at : at + quarter]))
    copies = [pltpu.make_async_copy(*pair, sems.at[n]) for n, pair in enumerate(copies)]
    for copy in copies:
        copy.start()
    for copy in copies:
        copy.wait()
    outs = []
    q_t = q_ref[...].astype(f32).T
    g_t = g_ref[...].astype(f32).T
    prod = g_t * o_ref[...].astype(f32).T
    keys = jnp.concatenate([k_ref[0].astype(f32), k_ref[1].astype(f32)])
    vals = jnp.concatenate([v_ref[0].astype(f32), v_ref[1].astype(f32)])
    row = lax.broadcasted_iota(jnp.int32, (8, TOK), 0)
    lanes = jnp.zeros((CELLS, 128 - DH), f32)
    for h in range(HEADS):
        part = slice(h * DH, (h + 1) * DH)
        dot = -jnp.sum(prod[part], axis=0, keepdims=True)
        high = dot.astype(bf16).astype(f32)
        mid = (dot - high).astype(bf16).astype(f32)
        low = dot - high - mid
        dots = jnp.where(row == 0, high, jnp.where(row == 1, mid, jnp.where(row == 2, low, 0.0)))
        send_ref[h, 0:FPAD, :] = jnp.concatenate([q_t[part], jnp.zeros((8, TOK), f32)]).astype(bf16)
        send_ref[h, FPAD : 2 * FPAD, :] = jnp.concatenate([g_t[part], dots]).astype(bf16)
        k_h = jnp.concatenate([keys[:, part], lanes], axis=1)
        v_h = jnp.concatenate([vals[:, part], lanes], axis=1)
        send_ref[h, 2 * FPAD : 2 * FPAD + 16, :] = jnp.concatenate([k_h, v_h]).astype(bf16)
        if h % 4 == 3:
            heads = slice(h - 3, h + 1)
            copy = pltpu.make_async_copy(send_ref.at[heads], out_ref.at[heads], out_sems.at[h // 4])
            copy.start()
            outs.append(copy)
    for copy in outs:
        copy.wait()


def keys_kernel(got_ref, out_ref, kv_ref, sem):
    copy = pltpu.make_async_copy(got_ref.at[:, 2 * FPAD : 2 * FPAD + 16], kv_ref, sem)
    copy.start()
    copy.wait()
    kv = kv_ref[...].astype(f32).reshape(HEADS, 2, CELLS, 128)
    k_t = kv[:, 0].reshape(128, 128).T
    v_t = kv[:, 1].reshape(128, 128).T
    out_ref[...] = jnp.concatenate([k_t[0:DH], v_t[0:DH]]).astype(bf16)


def attention_kernel(
    qg_ref, kv_a, kv_b, kv_c, kv_d, dq_ref, own_ref, other_ref, k_s, v_s, kt_s, e_s, dk_s, dv_s
):
    half = KEYS // 2
    lane = lax.broadcasted_iota(jnp.int32, (128, 128), 1)
    pad = jnp.zeros((128 - DH, 128), f32)
    for at, kv_ref in enumerate((kv_a, kv_b, kv_c, kv_d)):
        for b in range(4):
            kv = kv_ref[b].astype(f32)
            keys = slice((4 * at + b) * 128, (4 * at + b + 1) * 128)
            k_t = jnp.concatenate([kv[0:DH], pad])
            kt_s[:, keys] = k_t.astype(bf16)
            k_s[keys] = k_t.T.astype(bf16)
            v = jnp.concatenate([kv[DH:], pad]).T
            v_s[keys] = jnp.where((lane >= DH) & (lane < DH + 3), 1.0, v).astype(bf16)
    dk_s[...] = jnp.zeros_like(dk_s)
    dv_s[...] = jnp.zeros_like(dv_s)
    step = 512
    blocks = [slice(at, at + step) for at in range(0, KEYS, step)]

    def tile(t, _):
        q_t = jnp.concatenate([qg_ref[2 * t, 0:FPAD], qg_ref[2 * t + 1, 0:FPAD]], axis=1)
        g_t = jnp.concatenate(
            [qg_ref[2 * t, FPAD : 2 * FPAD], qg_ref[2 * t + 1, FPAD : 2 * FPAD]], axis=1
        )
        top = jnp.full((1, 2 * TOK), -jnp.inf, f32)
        for b in blocks:
            scores = jnp.dot(k_s[b, 0:FPAD], q_t, preferred_element_type=f32)
            e_s[b] = scores
            top = jnp.maximum(top, jnp.max(scores, axis=0, keepdims=True))
        top = top * SCALE2
        total = jnp.zeros((1, 2 * TOK), f32)
        for b in blocks:
            exps = jnp.exp2(e_s[b] * SCALE2 - top)
            e_s[b] = exps
            total = total + jnp.sum(exps, axis=0, keepdims=True)
        inverse = 1.0 / total
        dq = jnp.zeros((FPAD, 2 * TOK), f32)
        for b in blocks:
            probs = e_s[b] * inverse
            half_probs = probs.astype(bf16)
            shifted = jnp.dot(v_s[b, 0:FPAD], g_t, preferred_element_type=f32)
            ds = (probs * shifted).astype(bf16)
            dk_s[b, 0:FPAD] += lax.dot_general(ds, q_t, NT, preferred_element_type=f32)
            dv_s[b, 0:FPAD] += lax.dot_general(half_probs, g_t, NT, preferred_element_type=f32)
            dq = dq + jnp.dot(kt_s[0:FPAD, b], ds, preferred_element_type=f32)
        dq = (dq * SCALE).astype(bf16)
        dq_ref[2 * t] = dq[:, 0:TOK]
        dq_ref[2 * t + 1] = dq[:, TOK:]
        return 0

    lax.fori_loop(0, HEADS // 2, tile, 0)
    dk_t = dk_s[...].T
    dv_t = dv_s[...].T
    for out, at in ((own_ref, 0), (other_ref, half)):
        for b in range(8):
            keys = slice(at + b * 128, at + (b + 1) * 128)
            out[b, 0:DH] = dk_t[0:DH, keys] * SCALE
            out[b, DH : 2 * DH] = dv_t[0:DH, keys]


def pack_back_kernel(dq_ref, mine_ref, came_a, came_b, came_c, send_ref):
    total = mine_ref[0]
    for came in (came_a, came_b, came_c):
        total = total + came[...].astype(f32)
    lanes = jnp.zeros((128, 128 - DH), f32)
    dk = jnp.concatenate([total[0:DH].T, lanes], axis=1)
    dv = jnp.concatenate([total[DH : 2 * DH].T, lanes], axis=1)
    send_ref[:, 0:FPAD, :] = dq_ref[...]
    for a in range(HEADS):
        cells = slice(a * CELLS, (a + 1) * CELLS)
        send_ref[a, FPAD : FPAD + 16, :] = jnp.concatenate([dk[cells], dv[cells]]).astype(bf16)


def weights_kernel(part, patch_ref, qkv_ref, high_ref, low_ref, qkv_s, sems):
    step = 128
    copies = []
    for n in range(D // step):
        rows = slice(n * step, (n + 1) * step)
        source = qkv_ref.at[rows, part * D : (part + 1) * D]
        copies.append(pltpu.make_async_copy(source, qkv_s.at[rows], sems.at[n]))
        copies[-1].start()
    for copy in copies:
        copy.wait()
    both = jnp.dot(patch_ref[...], qkv_s[...], preferred_element_type=f32)
    both = both.reshape(16, 2, 8, D)
    both = jnp.concatenate([both[:, 0].reshape(128, D), both[:, 1].reshape(128, D)])
    high = both.astype(bf16)
    high_ref[...] = high
    low_ref[...] = (both - high.astype(f32)).astype(bf16)


def embed_kernel(back_ref, *refs):
    weights, (canvas_ref, core_out, chip_out, joined, sheet) = refs[:6], refs[6:]
    cols = (((0,), (0,)), ((), ()))
    cell = lax.broadcasted_iota(jnp.int32, (CELLS, TOK), 0)
    token = lax.broadcasted_iota(jnp.int32, (CELLS, TOK), 1)
    holds = (token // (POOL * COLS) == cell // 4) & (token % COLS // POOL == cell % 4)
    spread = jnp.where(holds, 1.0 / POOL**2, 0.0).astype(bf16)
    for h in range(HEADS):
        mine = back_ref[h].astype(f32)
        rows = slice(h * DH, (h + 1) * DH)
        joined[rows] = mine[0:DH]
        for part in (0, 1):
            at = FPAD + part * CELLS
            pooled = mine[at : at + CELLS].astype(bf16)
            wide = lax.dot_general(pooled, spread, cols, preferred_element_type=f32)
            joined[(part + 1) * D + h * DH : (part + 1) * D + (h + 1) * DH] = wide[0:DH]
    values = joined[...].astype(bf16)
    patch = jnp.zeros((256, TOK), f32)
    for n, weight in enumerate(weights):
        rows = slice(n // 2 * D, (n // 2 + 1) * D)
        patch = patch + jnp.dot(weight[...], values[rows], preferred_element_type=f32)
    patch = jnp.concatenate([patch[0:128].T, patch[128:256].T])
    high = patch.astype(bf16)
    rest = patch - high.astype(f32)
    mid = rest.astype(bf16)
    low = (rest - mid.astype(f32)).astype(bf16)
    lane = lax.broadcasted_iota(jnp.int32, (2 * TOK, 256), 1)
    row = lax.broadcasted_iota(jnp.int32, (2 * TOK, 256), 0)
    here = lane % 128 // 8 == row % COLS
    sheet[...] = jnp.zeros_like(sheet)
    parts = jnp.concatenate([high, mid, low], axis=1)
    to = lax.broadcasted_iota(jnp.int32, (128, 256), 1)
    at = lax.broadcasted_iota(jnp.int32, (128, 256), 0)
    for pair in range(8):
        tile = (to // 128 + 2 * pair == at // 8) & (to % 8 == at % 8)
        tile = jnp.where(tile, 1.0, 0.0).astype(bf16)
        tile = jnp.concatenate([tile] * 3)
        wide = jnp.dot(parts, tile, preferred_element_type=f32)
        wide = jnp.where(here, wide, 0.0)
        wide = jnp.sum(wide.reshape(2 * ROWS, COLS, 256), axis=1)
        for k in (0, 1):
            u = 2 * pair + k
            for side in (0, 1):
                piece = wide[side * ROWS : (side + 1) * ROWS, k * 128 : (k + 1) * 128]
                sheet[side, pl.ds(u, ROWS, stride=8), :] += piece
    left = sheet[0]
    right = sheet[1]
    lane = lax.broadcasted_iota(jnp.int32, left.shape, 1)
    center = jnp.where(lane < 124, pltpu.roll(left, 124, 1), 0.0)
    center = center + jnp.where(lane >= 4, pltpu.roll(right, 4, 1), 0.0)
    edges = jnp.where(lane < 4, left, pltpu.roll(right, 8, 1))
    canvas = jnp.concatenate([center, jnp.where(lane < 8, edges, 0.0)], axis=1)
    canvas_ref[...] = canvas
    first = lax.axis_index("c") == 0
    core_out[...] = jnp.where(first, canvas[68:72], canvas[0:4])
    chip_out[...] = jnp.where(first, canvas[0:4], canvas[68:72])


def rows_kernel(canvas_ref, core_ref, chip_ref, center_ref, near_out, far_out):
    first = lax.axis_index("c") == 0
    above = jnp.where(first, chip_ref[...], core_ref[...])
    below = jnp.where(first, core_ref[...], chip_ref[...])
    quiet = jnp.zeros((56, 256), f32)
    canvas = canvas_ref[4:68] + jnp.concatenate([above, quiet, below])
    center_ref[...] = canvas[:, 0:128]
    edges = canvas[:, 128:256].T[0:8]
    left, right = edges[0:4], edges[4:8]
    begins = lax.axis_index("yl") == 0
    near_out[...] = jnp.where(begins, right, left)
    far_out[...] = jnp.where(begins, left, right)


def cols_kernel(center_ref, near_ref, far_ref, out_ref):
    begins = lax.axis_index("yl") == 0
    left = jnp.where(begins, far_ref[...], near_ref[...])
    right = jnp.where(begins, near_ref[...], far_ref[...])
    quiet = jnp.zeros((120, 64), f32)
    out_ref[...] = center_ref[...] + jnp.concatenate([left, quiet, right]).T


def swapped(x, axis, by):
    peers = lax.axis_size(axis)
    return lax.ppermute(x, axis, [(i, i ^ by) for i in range(peers)])


def neighbours(x, axis):
    peers = lax.axis_size(axis)
    pairs = [(i, i + 1) for i in range(1, peers - 1, 2)]
    return lax.ppermute(x, axis, pairs + [(target, source) for source, target in pairs])


def combined_weights(w_qkv, w_patch, part):
    shape = jax.ShapeDtypeStruct((256, D), bf16)
    return call(
        functools.partial(weights_kernel, part),
        [shape, shape],
        12,
        [pltpu.VMEM((D, D), bf16), pltpu.SemaphoreType.DMA((D // 128,))],
        [WHOLE, ANYWHERE],
        cost_estimate=pl.CostEstimate(flops=2 * 256 * D * D, bytes_accessed=4 * D * D, transcendentals=0),
    )(w_patch, w_qkv)


def on_device(queries, key_states, values, saved_out, grad_out, w_qkv, w_patch):
    tokens = pltpu.VMEM((TOK, D), bf16)
    cells = pltpu.VMEM((2, 4, D), bf16)
    packed = (HEADS, 2 * FPAD + 16, TOK)
    dma = pltpu.SemaphoreType.DMA
    send = call(
        pack_kernel,
        jax.ShapeDtypeStruct(packed, bf16),
        None,
        [tokens, tokens, tokens, cells, cells, pltpu.VMEM(packed, bf16), dma((14,)), dma((4,))],
        [ANYWHERE] * 5,
        out_specs=ANYWHERE,
    )(
        queries.reshape(TOK, D),
        grad_out.reshape(TOK, D),
        saved_out.reshape(TOK, D),
        key_states,
        values,
    )
    got = lax.all_to_all(send, HEAD_AXES, 0, 0, tiled=True)
    kv = call(
        keys_kernel,
        jax.ShapeDtypeStruct((2 * DH, 128), bf16),
        4,
        [pltpu.VMEM((HEADS, 16, 128), bf16), dma(())],
        [ANYWHERE],
    )(got)
    came = [swapped(kv, "z", by) for by in (2, 4, 6)]
    weights = list(combined_weights(w_qkv, w_patch, 0))
    came, weights = lax.optimization_barrier((came, weights))
    kv_a = jnp.stack([kv] + came)
    kv_b = swapped(kv_a, "z", 1)
    kv_c = swapped(kv_a, "c", 1)
    for part in (1, 2):
        weights += combined_weights(w_qkv, w_patch, part)
    kv_b, kv_c, weights = lax.optimization_barrier((kv_b, kv_c, weights))
    kv_d = swapped(kv_b, "c", 1)
    grads = jax.ShapeDtypeStruct((8, 2 * DH, 128), f32)
    dq, own, other = call(
        attention_kernel,
        [jax.ShapeDtypeStruct((HEADS, FPAD, TOK), bf16), grads, grads],
        32,
        [
            pltpu.VMEM((KEYS, 128), bf16),
            pltpu.VMEM((KEYS, 128), bf16),
            pltpu.VMEM((128, KEYS), bf16),
            pltpu.VMEM((KEYS, 2 * TOK), f32),
            pltpu.VMEM((KEYS, 128), f32),
            pltpu.VMEM((KEYS, 128), f32),
        ],
    )(got, kv_a, kv_b, kv_c, kv_d)
    mine = own + swapped(other, "c", 1)
    mine = mine[:4] + swapped(mine[4:].astype(bf16), "z", 1).astype(f32)
    came = [swapped(mine[n].astype(bf16), "z", 2 * n) for n in (1, 2, 3)]
    send = call(pack_back_kernel, jax.ShapeDtypeStruct((HEADS, FPAD + 16, TOK), bf16), 8)(
        dq, mine[0:1], *came
    )
    back = lax.all_to_all(send, HEAD_AXES, 0, 0, tiled=True)
    strip = jax.ShapeDtypeStruct((4, 256), f32)
    canvas, to_core, to_chip = call(
        embed_kernel,
        [jax.ShapeDtypeStruct((72, 256), f32), strip, strip],
        24,
        [pltpu.VMEM((3 * D, TOK), f32), pltpu.VMEM((2, 72, 128), f32)],
    )(back, *weights)
    strip = jax.ShapeDtypeStruct((4, 64), f32)
    center, to_near, to_far = call(
        rows_kernel, [jax.ShapeDtypeStruct((64, 128), f32), strip, strip], 4
    )(canvas, swapped(to_core, "c", 1), neighbours(to_chip, BLK))
    return call(cols_kernel, jax.ShapeDtypeStruct((64, 128), f32), 4)(
        center, swapped(to_near, "yl", 1), neighbours(to_far, COL)
    )


def solution(mesh):
    fine = Mesh(mesh.devices.reshape(2, 4, 2, 8, 2), ("yh", "x", "c", "z", "yl"))
    split = P(BLK, COL, None)
    return jax.shard_map(
        on_device,
        mesh=fine,
        in_specs=(split, split, split, split, split, P(), P()),
        out_specs=P(BLK, COL),
        check_vma=False,
    )
```

```python
import functools
import math

import jax
import jax.numpy as jnp
from jax import lax
from jax.experimental import pallas as pl
from jax.experimental.pallas import tpu as pltpu
from jax.sharding import Mesh, PartitionSpec as P

D = 1152
HEADS = 16
DH = D // HEADS
POOL = 4
SCALE = DH**-0.5
SCALE2 = SCALE * math.log2(math.e)
ROWS, COLS = 8, 16
TOK = ROWS * COLS
CELLS = TOK // POOL**2
FPAD = 80
KEYS = 2048
HALF = KEYS // 2
TILE = 1024
PER = TILE // TOK
STEP = 256
HEAD_AXES = ("yh", "x", "yl")
BLK = ("yh", "x", "c")
COL = ("z", "yl")
NT = (((1,), (1,)), ((), ()))
WHOLE = pl.BlockSpec(memory_space=pltpu.VMEM)
ANYWHERE = pl.BlockSpec(memory_space=pl.ANY)
bf16, f32 = jnp.bfloat16, jnp.float32


def call(kernel, out, mib, scratch=(), specs=None, **more):
    if specs is not None:
        more["in_specs"] = specs
    return pl.pallas_call(
        kernel,
        out_shape=out,
        scratch_shapes=scratch,
        compiler_params=pltpu.CompilerParams(vmem_limit_bytes=mib * 2**20 if mib else None),
        **more,
    )


def pack_kernel(q_in, g_in, o_in, k_in, v_in, out_ref, q_ref, g_ref, o_ref, k_ref, v_ref, send_ref, sems, out_sems):
    copies = []
    quarter = TOK // 4
    for source, target in ((k_in, k_ref), (v_in, v_ref)):
        copies.append((source, target))
    for source, target in ((q_in, q_ref), (g_in, g_ref), (o_in, o_ref)):
        for at in range(0, TOK, quarter):
            copies.append((source.at[at : at + quarter], target.at[at : at + quarter]))
    copies = [pltpu.make_async_copy(*pair, sems.at[n]) for n, pair in enumerate(copies)]
    for copy in copies:
        copy.start()
    for copy in copies:
        copy.wait()
    outs = []
    q_t = q_ref[...].astype(f32).T
    g_t = g_ref[...].astype(f32).T
    prod = g_t * o_ref[...].astype(f32).T
    keys = jnp.concatenate([k_ref[0].astype(f32), k_ref[1].astype(f32)])
    vals = jnp.concatenate([v_ref[0].astype(f32), v_ref[1].astype(f32)])
    row = lax.broadcasted_iota(jnp.int32, (8, TOK), 0)
    lanes = jnp.zeros((CELLS, 128 - DH), f32)
    for h in range(HEADS):
        part = slice(h * DH, (h + 1) * DH)
        dot = -jnp.sum(prod[part], axis=0, keepdims=True)
        high = dot.astype(bf16).astype(f32)
        mid = (dot - high).astype(bf16).astype(f32)
        low = dot - high - mid
        dots = jnp.where(row == 0, high, jnp.where(row == 1, mid, jnp.where(row == 2, low, 0.0)))
        send_ref[h, 0:FPAD, :] = jnp.concatenate([q_t[part], jnp.zeros((8, TOK), f32)]).astype(bf16)
        send_ref[h, FPAD : 2 * FPAD, :] = jnp.concatenate([g_t[part], dots]).astype(bf16)
        k_h = jnp.concatenate([keys[:, part], lanes], axis=1)
        v_h = jnp.concatenate([vals[:, part], lanes], axis=1)
        send_ref[h, 2 * FPAD : 2 * FPAD + 16, :] = jnp.concatenate([k_h, v_h]).astype(bf16)
        if h % 4 == 3:
            heads = slice(h - 3, h + 1)
            copy = pltpu.make_async_copy(send_ref.at[heads], out_ref.at[heads], out_sems.at[h // 4])
            copy.start()
            outs.append(copy)
    for copy in outs:
        copy.wait()


def keys_kernel(got_ref, out_ref, kv_ref, sem):
    copy = pltpu.make_async_copy(got_ref.at[:, 2 * FPAD : 2 * FPAD + 16], kv_ref, sem)
    copy.start()
    copy.wait()
    kv = kv_ref[...].astype(f32).reshape(HEADS, 2, CELLS, 128)
    k_t = kv[:, 0].reshape(128, 128).T
    v_t = kv[:, 1].reshape(128, 128).T
    out_ref[...] = jnp.concatenate([k_t[0:DH], v_t[0:DH]]).astype(bf16)


def load_keys(kv_refs, k_s, kt_s=None, v_s=None):
    lane = lax.broadcasted_iota(jnp.int32, (128, 128), 1)
    pad = jnp.zeros((128 - DH, 128), f32)
    norms = jnp.zeros((1, 128), f32)
    for at, kv_ref in enumerate(kv_refs):
        for b in range(4):
            kv = kv_ref[b].astype(f32)
            keys = slice((4 * at + b) * 128, (4 * at + b + 1) * 128)
            k_t = jnp.concatenate([kv[0:DH], pad])
            norms = jnp.maximum(norms, jnp.sum(k_t * k_t, axis=0, keepdims=True))
            k_s[keys] = k_t.T.astype(bf16)
            if kt_s is not None:
                kt_s[:, keys] = k_t.astype(bf16)
                v = jnp.concatenate([kv[DH:], pad]).T
                v_s[keys] = jnp.where((lane >= DH) & (lane < DH + 3), 1.0, v).astype(bf16)
    return jnp.max(norms)


def tile_of(qg_ref, t, row):
    return jnp.concatenate([qg_ref[PER * t + n, row : row + FPAD] for n in range(PER)], axis=1)


def log_sums(q_t, k_s, norm):
    exact = q_t.astype(f32)
    bound = jnp.sqrt(jnp.sum(exact * exact, axis=0, keepdims=True) * norm) * (SCALE2 * 1.001)

    def scores(rows):
        return jnp.dot(k_s[rows, 0:FPAD], q_t, preferred_element_type=f32) * SCALE2

    total = jnp.zeros((1, TILE), f32)
    for at in range(0, HALF, STEP):
        exps = jnp.exp2(scores(slice(at, at + STEP)) - bound)
        total = total + jnp.sum(exps, axis=0, keepdims=True)

    def again():
        def rows(n):
            return pl.ds(pl.multiple_of(n * 128, 128), 128)

        def largest(n, top):
            return jnp.maximum(top, jnp.max(scores(rows(n)), axis=0, keepdims=True))

        top = lax.fori_loop(0, HALF // 128, largest, jnp.full((1, TILE), -jnp.inf, f32))

        def add(n, total):
            return total + jnp.sum(jnp.exp2(scores(rows(n)) - top), axis=0, keepdims=True)

        return top + jnp.log2(lax.fori_loop(0, HALF // 128, add, jnp.zeros((1, TILE), f32)))

    return lax.cond(jnp.min(total) < 2.0**-90, again, lambda: bound + jnp.log2(total))


def put_sums(out_ref, t, sums):
    for n in range(PER):
        out_ref[PER * t + n] = jnp.broadcast_to(sums[:, n * TOK : (n + 1) * TOK], (8, TOK))


def get_sums(sums_ref, t):
    return jnp.concatenate([sums_ref[PER * t + n, 0:1] for n in range(PER)], axis=1)


def sums_kernel(qg_ref, kv_own, kv_other, out_ref, k_s):
    norm = load_keys((kv_own, kv_other), k_s)

    def tile(t, _):
        put_sums(out_ref, t, log_sums(tile_of(qg_ref, t, 0), k_s, norm))
        return 0

    lax.fori_loop(0, KEYS // TILE, tile, 0)


def gradients(qg_ref, sums_ref, k_s, kt_s, v_s, dk_s, dv_s, put_dq):
    dk_s[...] = jnp.zeros_like(dk_s)
    dv_s[...] = jnp.zeros_like(dv_s)

    def tile(t, _):
        q_t = tile_of(qg_ref, t, 0)
        g_t = tile_of(qg_ref, t, FPAD)
        sums = get_sums(sums_ref, t)
        dq = jnp.zeros((FPAD, TILE), f32)
        for at in range(0, HALF, STEP):
            b = slice(at, at + STEP)
            scores = jnp.dot(k_s[b, 0:FPAD], q_t, preferred_element_type=f32)
            probs = jnp.exp2(scores * SCALE2 - sums)
            half_probs = probs.astype(bf16)
            shifted = jnp.dot(v_s[b, 0:FPAD], g_t, preferred_element_type=f32)
            ds = (probs * shifted).astype(bf16)
            dk_s[b, 0:FPAD] += lax.dot_general(ds, q_t, NT, preferred_element_type=f32)
            dv_s[b, 0:FPAD] += lax.dot_general(half_probs, g_t, NT, preferred_element_type=f32)
            dq = dq + jnp.dot(kt_s[0:FPAD, b], ds, preferred_element_type=f32)
        for n in range(PER):
            put_dq(PER * t + n, dq[:, n * TOK : (n + 1) * TOK])
        return 0

    lax.fori_loop(0, KEYS // TILE, tile, 0)


def put_keys(own_ref, other_ref, dk_s, dv_s):
    dk_t = dk_s[...].T
    dv_t = dv_s[...].T
    for at, out in enumerate((own_ref, other_ref)):
        for b in range(4):
            keys = slice((4 * at + b) * 128, (4 * at + b + 1) * 128)
            block = jnp.concatenate([dk_t[0:DH, keys] * SCALE, dv_t[0:DH, keys]])
            out[b] = block.astype(out.dtype)


def first_kernel(
    qg_ref, kv_own, kv_other, sums_in, sums_ref, dq_ref, own_ref, other_ref, k_s, kt_s, v_s, dk_s, dv_s
):
    norm = load_keys((kv_own, kv_other), k_s, kt_s, v_s)

    def tile(t, _):
        mine = log_sums(tile_of(qg_ref, t, 0), k_s, norm)
        other = get_sums(sums_in, t)
        top = jnp.maximum(mine, other)
        put_sums(sums_ref, t, top + jnp.log2(jnp.exp2(mine - top) + jnp.exp2(other - top)))
        return 0

    lax.fori_loop(0, KEYS // TILE, tile, 0)

    def put_dq(n, dq):
        dq_ref[n] = dq

    gradients(qg_ref, sums_ref, k_s, kt_s, v_s, dk_s, dv_s, put_dq)
    put_keys(own_ref, other_ref, dk_s, dv_s)


def second_kernel(
    qg_ref, kv_own, kv_other, sums_ref, dq_in, dq_ref, own_ref, other_ref, k_s, kt_s, v_s, dk_s, dv_s
):
    load_keys((kv_own, kv_other), k_s, kt_s, v_s)

    def put_dq(n, dq):
        dq_ref[n] = ((dq_in[n] + dq) * SCALE).astype(bf16)

    gradients(qg_ref, sums_ref, k_s, kt_s, v_s, dk_s, dv_s, put_dq)
    put_keys(own_ref, other_ref, dk_s, dv_s)


def pack_back_kernel(dq_ref, mine_ref, came_a, came_b, came_c, send_ref):
    total = mine_ref[0]
    for came in (came_a, came_b, came_c):
        total = total + came[...].astype(f32)
    lanes = jnp.zeros((128, 128 - DH), f32)
    dk = jnp.concatenate([total[0:DH].T, lanes], axis=1)
    dv = jnp.concatenate([total[DH : 2 * DH].T, lanes], axis=1)
    send_ref[:, 0:FPAD, :] = dq_ref[...]
    for a in range(HEADS):
        cells = slice(a * CELLS, (a + 1) * CELLS)
        send_ref[a, FPAD : FPAD + 16, :] = jnp.concatenate([dk[cells], dv[cells]]).astype(bf16)


def weights_kernel(part, patch_ref, qkv_ref, high_ref, low_ref, qkv_s, sems):
    step = 128
    copies = []
    for n in range(D // step):
        rows = slice(n * step, (n + 1) * step)
        source = qkv_ref.at[rows, part * D : (part + 1) * D]
        copies.append(pltpu.make_async_copy(source, qkv_s.at[rows], sems.at[n]))
        copies[-1].start()
    for copy in copies:
        copy.wait()
    both = jnp.dot(patch_ref[...], qkv_s[...], preferred_element_type=f32)
    both = both.reshape(16, 2, 8, D)
    both = jnp.concatenate([both[:, 0].reshape(128, D), both[:, 1].reshape(128, D)])
    high = both.astype(bf16)
    high_ref[...] = high
    low_ref[...] = (both - high.astype(f32)).astype(bf16)


def embed_kernel(back_ref, *refs):
    weights, (canvas_ref, core_out, chip_out, joined, sheet) = refs[:6], refs[6:]
    cols = (((0,), (0,)), ((), ()))
    cell = lax.broadcasted_iota(jnp.int32, (CELLS, TOK), 0)
    token = lax.broadcasted_iota(jnp.int32, (CELLS, TOK), 1)
    holds = (token // (POOL * COLS) == cell // 4) & (token % COLS // POOL == cell % 4)
    spread = jnp.where(holds, 1.0 / POOL**2, 0.0).astype(bf16)
    for h in range(HEADS):
        mine = back_ref[h].astype(f32)
        rows = slice(h * DH, (h + 1) * DH)
        joined[rows] = mine[0:DH]
        for part in (0, 1):
            at = FPAD + part * CELLS
            pooled = mine[at : at + CELLS].astype(bf16)
            wide = lax.dot_general(pooled, spread, cols, preferred_element_type=f32)
            joined[(part + 1) * D + h * DH : (part + 1) * D + (h + 1) * DH] = wide[0:DH]
    values = joined[...].astype(bf16)
    patch = jnp.zeros((256, TOK), f32)
    for n, weight in enumerate(weights):
        rows = slice(n // 2 * D, (n // 2 + 1) * D)
        patch = patch + jnp.dot(weight[...], values[rows], preferred_element_type=f32)
    patch = jnp.concatenate([patch[0:128].T, patch[128:256].T])
    high = patch.astype(bf16)
    rest = patch - high.astype(f32)
    mid = rest.astype(bf16)
    low = (rest - mid.astype(f32)).astype(bf16)
    lane = lax.broadcasted_iota(jnp.int32, (2 * TOK, 256), 1)
    row = lax.broadcasted_iota(jnp.int32, (2 * TOK, 256), 0)
    here = lane % 128 // 8 == row % COLS
    sheet[...] = jnp.zeros_like(sheet)
    parts = jnp.concatenate([high, mid, low], axis=1)
    to = lax.broadcasted_iota(jnp.int32, (128, 256), 1)
    at = lax.broadcasted_iota(jnp.int32, (128, 256), 0)
    for pair in range(8):
        tile = (to // 128 + 2 * pair == at // 8) & (to % 8 == at % 8)
        tile = jnp.where(tile, 1.0, 0.0).astype(bf16)
        tile = jnp.concatenate([tile] * 3)
        wide = jnp.dot(parts, tile, preferred_element_type=f32)
        wide = jnp.where(here, wide, 0.0)
        wide = jnp.sum(wide.reshape(2 * ROWS, COLS, 256), axis=1)
        for k in (0, 1):
            u = 2 * pair + k
            for side in (0, 1):
                piece = wide[side * ROWS : (side + 1) * ROWS, k * 128 : (k + 1) * 128]
                sheet[side, pl.ds(u, ROWS, stride=8), :] += piece
    left = sheet[0]
    right = sheet[1]
    lane = lax.broadcasted_iota(jnp.int32, left.shape, 1)
    center = jnp.where(lane < 124, pltpu.roll(left, 124, 1), 0.0)
    center = center + jnp.where(lane >= 4, pltpu.roll(right, 4, 1), 0.0)
    edges = jnp.where(lane < 4, left, pltpu.roll(right, 8, 1))
    canvas = jnp.concatenate([center, jnp.where(lane < 8, edges, 0.0)], axis=1)
    canvas_ref[...] = canvas
    first = lax.axis_index("c") == 0
    core_out[...] = jnp.where(first, canvas[68:72], canvas[0:4])
    chip_out[...] = jnp.where(first, canvas[0:4], canvas[68:72])


def rows_kernel(canvas_ref, chip_ref, core_ref, center_ref, near_out, far_out):
    first = lax.axis_index("c") == 0
    above = jnp.where(first, chip_ref[...], core_ref[...])
    below = jnp.where(first, core_ref[...], chip_ref[...])
    quiet = jnp.zeros((56, 256), f32)
    canvas = canvas_ref[4:68] + jnp.concatenate([above, quiet, below])
    center_ref[...] = canvas[:, 0:128]
    edges = canvas[:, 128:256].T[0:8]
    left, right = edges[0:4], edges[4:8]
    begins = lax.axis_index("yl") == 0
    near_out[...] = jnp.where(begins, right, left)
    far_out[...] = jnp.where(begins, left, right)


def cols_kernel(center_ref, far_ref, near_ref, out_ref):
    begins = lax.axis_index("yl") == 0
    left = jnp.where(begins, far_ref[...], near_ref[...])
    right = jnp.where(begins, near_ref[...], far_ref[...])
    quiet = jnp.zeros((120, 64), f32)
    out_ref[...] = center_ref[...] + jnp.concatenate([left, quiet, right]).T


def swapped(x, axis, by):
    peers = lax.axis_size(axis)
    return lax.ppermute(x, axis, [(i, i ^ by) for i in range(peers)])


def neighbours(x, axis):
    peers = lax.axis_size(axis)
    pairs = [(i, i + 1) for i in range(1, peers - 1, 2)]
    return lax.ppermute(x, axis, pairs + [(target, source) for source, target in pairs])


def cost(products):
    flops = products * 2 * KEYS * HALF * 256
    return pl.CostEstimate(flops=flops, bytes_accessed=2**20, transcendentals=KEYS * HALF)


def combined_weights(w_qkv, w_patch, part):
    shape = jax.ShapeDtypeStruct((256, D), bf16)
    return call(
        functools.partial(weights_kernel, part),
        [shape, shape],
        12,
        [pltpu.VMEM((D, D), bf16), pltpu.SemaphoreType.DMA((D // 128,))],
        [WHOLE, ANYWHERE],
        cost_estimate=pl.CostEstimate(flops=2**20, bytes_accessed=2**16, transcendentals=0),
    )(w_patch, w_qkv)


def on_device(queries, key_states, values, saved_out, grad_out, w_qkv, w_patch):
    tokens = pltpu.VMEM((TOK, D), bf16)
    cells = pltpu.VMEM((2, 4, D), bf16)
    packed = (HEADS, 2 * FPAD + 16, TOK)
    dma = pltpu.SemaphoreType.DMA
    send = call(
        pack_kernel,
        jax.ShapeDtypeStruct(packed, bf16),
        None,
        [tokens, tokens, tokens, cells, cells, pltpu.VMEM(packed, bf16), dma((14,)), dma((4,))],
        [ANYWHERE] * 5,
        out_specs=ANYWHERE,
    )(
        queries.reshape(TOK, D),
        grad_out.reshape(TOK, D),
        saved_out.reshape(TOK, D),
        key_states,
        values,
    )
    got = lax.all_to_all(send, HEAD_AXES, 0, 0, tiled=True)
    kv = call(
        keys_kernel,
        jax.ShapeDtypeStruct((2 * DH, 128), bf16),
        4,
        [pltpu.VMEM((HEADS, 16, 128), bf16), dma(())],
        [ANYWHERE],
    )(got)
    came = [swapped(kv, "z", by) for by in (2, 4, 6)]
    kv_a = jnp.stack([kv] + came)
    kv_b = swapped(kv_a, "z", 1)
    kv_c = swapped(kv_a, "c", 1)
    keys = pltpu.VMEM((HALF, 128), bf16)
    sums = jax.ShapeDtypeStruct((HEADS, 8, TOK), f32)
    even_sums = call(sums_kernel, sums, 24, [keys], cost_estimate=cost(1))(got, kv_a, kv_c)
    kv_b, even_sums = lax.optimization_barrier((kv_b, even_sums))
    kv_d = swapped(kv_b, "c", 1)
    scratch = [keys, pltpu.VMEM((128, HALF), bf16), keys]
    scratch += [pltpu.VMEM((HALF, 128), f32)] * 2
    block = (4, 2 * DH, 128)
    sums, dq, own, other = call(
        first_kernel,
        [sums, jax.ShapeDtypeStruct((HEADS, FPAD, TOK), f32)] + [jax.ShapeDtypeStruct(block, bf16)] * 2,
        28,
        scratch,
        cost_estimate=cost(6),
    )(got, kv_b, kv_d, even_sums)
    came = [swapped(own, "z", 1), swapped(other, ("c", "z"), 9)]
    dq, own, other = call(
        second_kernel,
        [jax.ShapeDtypeStruct((HEADS, FPAD, TOK), bf16)] + [jax.ShapeDtypeStruct(block, f32)] * 2,
        28,
        scratch,
        cost_estimate=cost(5),
    )(got, kv_a, kv_c, sums, dq)
    own, other, came = lax.optimization_barrier((own, other, came))
    mine = own + swapped(other, "c", 1) + came[0].astype(f32) + came[1].astype(f32)
    mine, w_qkv, w_patch = lax.optimization_barrier((mine, w_qkv, w_patch))
    came = [swapped(mine[n].astype(bf16), "z", 2 * n) for n in (1, 2, 3)]
    weights = [w for part in range(3) for w in combined_weights(w_qkv, w_patch, part)]
    came, weights = lax.optimization_barrier((came, weights))
    send = call(pack_back_kernel, jax.ShapeDtypeStruct((HEADS, FPAD + 16, TOK), bf16), 8)(
        dq, mine[0:1], *came
    )
    back = lax.all_to_all(send, HEAD_AXES, 0, 0, tiled=True)
    strip = jax.ShapeDtypeStruct((4, 256), f32)
    canvas, to_core, to_chip = call(
        embed_kernel,
        [jax.ShapeDtypeStruct((72, 256), f32), strip, strip],
        24,
        [pltpu.VMEM((3 * D, TOK), f32), pltpu.VMEM((2, 72, 128), f32)],
    )(back, *weights)
    strip = jax.ShapeDtypeStruct((4, 64), f32)
    center, to_near, to_far = call(
        rows_kernel, [jax.ShapeDtypeStruct((64, 128), f32), strip, strip], 4
    )(canvas, neighbours(to_chip, BLK), swapped(to_core, "c", 1))
    return call(cols_kernel, jax.ShapeDtypeStruct((64, 128), f32), 4)(
        center, neighbours(to_far, COL), swapped(to_near, "yl", 1)
    )


def solution(mesh):
    fine = Mesh(mesh.devices.reshape(2, 4, 2, 8, 2), ("yh", "x", "c", "z", "yl"))
    split = P(BLK, COL, None)
    return jax.shard_map(
        on_device,
        mesh=fine,
        in_specs=(split, split, split, split, split, P(), P()),
        out_specs=P(BLK, COL),
        check_vma=False,
    )
```

```python
import functools
import math

import jax
import jax.numpy as jnp
from jax import lax
from jax.experimental import pallas as pl
from jax.experimental.pallas import tpu as pltpu
from jax.sharding import Mesh, PartitionSpec as P

D = 1152
HEADS = 16
DH = D // HEADS
POOL = 4
SCALE = DH**-0.5
SCALE2 = SCALE * math.log2(math.e)
ROWS, COLS = 8, 16
TOK = ROWS * COLS
CELLS = TOK // POOL**2
FPAD = 80
QUERIES = 2048
HALF = 512
TILE = 1024
TILES = QUERIES // TILE
PER = TILE // TOK
STEP = 256
HEAD_AXES = ("yh", "x", "yl")
BLK = ("yh", "x", "c")
COL = ("z", "yl")
NT = (((1,), (1,)), ((), ()))
WHOLE = pl.BlockSpec(memory_space=pltpu.VMEM)
ANYWHERE = pl.BlockSpec(memory_space=pl.ANY)
bf16, f32 = jnp.bfloat16, jnp.float32


def call(kernel, out, mib, scratch=(), specs=None, **more):
    if specs is not None:
        more["in_specs"] = specs
    return pl.pallas_call(
        kernel,
        out_shape=out,
        scratch_shapes=scratch,
        compiler_params=pltpu.CompilerParams(vmem_limit_bytes=mib * 2**20 if mib else None),
        **more,
    )


def pack_kernel(
    q_in, g_in, o_in, k_in, v_in, out_ref, q_ref, g_ref, o_ref, k_ref, v_ref, send_ref, sems, out_sems
):
    pairs = [(k_in, k_ref), (v_in, v_ref)]
    quarter = TOK // 4
    for source, target in ((q_in, q_ref), (g_in, g_ref), (o_in, o_ref)):
        for at in range(0, TOK, quarter):
            pairs.append((source.at[at : at + quarter], target.at[at : at + quarter]))
    copies = [pltpu.make_async_copy(*pair, sems.at[n]) for n, pair in enumerate(pairs)]
    for copy in copies:
        copy.start()
    for copy in copies[:6]:
        copy.wait()
    q_t = q_ref[...].astype(f32).T
    keys = jnp.concatenate([k_ref[0].astype(f32), k_ref[1].astype(f32)])
    vals = jnp.concatenate([v_ref[0].astype(f32), v_ref[1].astype(f32)])
    lanes = jnp.zeros((CELLS, 128 - DH), f32)
    for h in range(HEADS):
        part = slice(h * DH, (h + 1) * DH)
        send_ref[h, 0:FPAD, :] = jnp.concatenate([q_t[part], jnp.zeros((8, TOK), f32)]).astype(bf16)
        k_h = jnp.concatenate([keys[:, part], lanes], axis=1)
        v_h = jnp.concatenate([vals[:, part], lanes], axis=1)
        send_ref[h, 2 * FPAD : 2 * FPAD + 16, :] = jnp.concatenate([k_h, v_h]).astype(bf16)
    for copy in copies[6:]:
        copy.wait()
    g_t = g_ref[...].astype(f32).T
    prod = g_t * o_ref[...].astype(f32).T
    row = lax.broadcasted_iota(jnp.int32, (8, TOK), 0)
    outs = []
    for h in range(HEADS):
        part = slice(h * DH, (h + 1) * DH)
        dot = -jnp.sum(prod[part], axis=0, keepdims=True)
        high = dot.astype(bf16).astype(f32)
        mid = (dot - high).astype(bf16).astype(f32)
        low = dot - high - mid
        dots = jnp.where(row == 0, high, jnp.where(row == 1, mid, jnp.where(row == 2, low, 0.0)))
        send_ref[h, FPAD : 2 * FPAD, :] = jnp.concatenate([g_t[part], dots]).astype(bf16)
        if h % 4 == 3:
            heads = slice(h - 3, h + 1)
            copy = pltpu.make_async_copy(send_ref.at[heads], out_ref.at[heads], out_sems.at[h // 4])
            copy.start()
            outs.append(copy)
    for copy in outs:
        copy.wait()


def keys_kernel(got_ref, out_ref, kv_ref, sem):
    copy = pltpu.make_async_copy(got_ref.at[:, 2 * FPAD : 2 * FPAD + 16], kv_ref, sem)
    copy.start()
    copy.wait()
    kv = kv_ref[...].astype(f32).reshape(HEADS, 2, CELLS, 128)
    k_t = kv[:, 0].reshape(128, 128).T
    v_t = kv[:, 1].reshape(128, 128).T
    out_ref[...] = jnp.concatenate([k_t[0:DH], v_t[0:DH]]).astype(bf16)


def load_keys(kv_ref, k_s, kt_s=None, v_s=None):
    lane = lax.broadcasted_iota(jnp.int32, (128, 128), 1)
    pad = jnp.zeros((128 - DH, 128), f32)
    norms = jnp.zeros((1, 128), f32)
    for b in range(4):
        kv = kv_ref[b].astype(f32)
        keys = slice(b * 128, (b + 1) * 128)
        k_t = jnp.concatenate([kv[0:DH], pad])
        norms = jnp.maximum(norms, jnp.sum(k_t * k_t, axis=0, keepdims=True))
        k_s[keys] = k_t.T.astype(bf16)
        if kt_s is not None:
            kt_s[:, keys] = k_t.astype(bf16)
            v = jnp.concatenate([kv[DH:], pad]).T
            v_s[keys] = jnp.where((lane >= DH) & (lane < DH + 3), 1.0, v).astype(bf16)
    return jnp.max(norms)


def tile_of(qg_ref, t, row):
    return jnp.concatenate([qg_ref[PER * t + n, row : row + FPAD] for n in range(PER)], axis=1)


def log_sums(q_t, k_s, norm):
    exact = q_t.astype(f32)
    bound = jnp.sqrt(jnp.sum(exact * exact, axis=0, keepdims=True) * norm) * (SCALE2 * 1.001)

    def scores(rows):
        return jnp.dot(k_s[rows, 0:FPAD], q_t, preferred_element_type=f32) * SCALE2

    total = jnp.zeros((1, TILE), f32)
    for at in range(0, HALF, STEP):
        exps = jnp.exp2(scores(slice(at, at + STEP)) - bound)
        total = total + jnp.sum(exps, axis=0, keepdims=True)

    def again():
        def rows(n):
            return pl.ds(pl.multiple_of(n * 128, 128), 128)

        def largest(n, top):
            return jnp.maximum(top, jnp.max(scores(rows(n)), axis=0, keepdims=True))

        top = lax.fori_loop(0, HALF // 128, largest, jnp.full((1, TILE), -jnp.inf, f32))

        def add(n, total):
            return total + jnp.sum(jnp.exp2(scores(rows(n)) - top), axis=0, keepdims=True)

        return top + jnp.log2(lax.fori_loop(0, HALF // 128, add, jnp.zeros((1, TILE), f32)))

    return lax.cond(jnp.min(total) < 2.0**-90, again, lambda: bound + jnp.log2(total))


def put_sums(out_ref, at, t, sums):
    for n in range(PER):
        out_ref[at, PER * t + n] = jnp.broadcast_to(sums[:, n * TOK : (n + 1) * TOK], (8, TOK))


def get_sums(sums_ref, at, t):
    return jnp.concatenate([sums_ref[at, PER * t + n, 0:1] for n in range(PER)], axis=1)


def added(one, two):
    top = jnp.maximum(one, two)
    return top + jnp.log2(jnp.exp2(one - top) + jnp.exp2(two - top))


def even_sums_kernel(qg_a, qg_b, kv_ref, out_ref, k_s):
    norm = load_keys(kv_ref, k_s)
    for at, qg_ref in enumerate((qg_a, qg_b)):

        def tile(t, _):
            put_sums(out_ref, at, t, log_sums(tile_of(qg_ref, t, 0), k_s, norm))
            return 0

        lax.fori_loop(0, TILES, tile, 0)


def odd_sums_kernel(qg_a, qg_b, kv_ref, even_ref, out_ref, k_s):
    norm = load_keys(kv_ref, k_s)
    for at, qg_ref in enumerate((qg_a, qg_b)):

        def tile(t, _):
            mine = log_sums(tile_of(qg_ref, t, 0), k_s, norm)
            put_sums(out_ref, at, t, added(mine, get_sums(even_ref, at, t)))
            return 0

        lax.fori_loop(0, TILES, tile, 0)


def gradients(sums_ref, work, k_s, kt_s, v_s, dk_s, dv_s):
    dk_s[...] = jnp.zeros_like(dk_s)
    dv_s[...] = jnp.zeros_like(dv_s)
    for at_core, (qg_ref, put_dq) in enumerate(work):

        def tile(t, _):
            q_t = tile_of(qg_ref, t, 0)
            g_t = tile_of(qg_ref, t, FPAD)
            sums = get_sums(sums_ref, at_core, t)
            dq = jnp.zeros((FPAD, TILE), f32)
            for at in range(0, HALF, STEP):
                b = slice(at, at + STEP)
                scores = jnp.dot(k_s[b, 0:FPAD], q_t, preferred_element_type=f32)
                probs = jnp.exp2(scores * SCALE2 - sums)
                half_probs = probs.astype(bf16)
                shifted = jnp.dot(v_s[b, 0:FPAD], g_t, preferred_element_type=f32)
                ds = (probs * shifted).astype(bf16)
                dk_s[b, 0:FPAD] += lax.dot_general(ds, q_t, NT, preferred_element_type=f32)
                dv_s[b, 0:FPAD] += lax.dot_general(half_probs, g_t, NT, preferred_element_type=f32)
                dq = dq + jnp.dot(kt_s[0:FPAD, b], ds, preferred_element_type=f32)
            for n in range(PER):
                put_dq(PER * t + n, dq[:, n * TOK : (n + 1) * TOK])
            return 0

        lax.fori_loop(0, TILES, tile, 0)


def put_keys(out_ref, dk_s, dv_s):
    dk_t = dk_s[...].T
    dv_t = dv_s[...].T
    for b in range(4):
        keys = slice(b * 128, (b + 1) * 128)
        block = jnp.concatenate([dk_t[0:DH, keys] * SCALE, dv_t[0:DH, keys]])
        out_ref[b] = block.astype(out_ref.dtype)


def first_kernel(
    qg_a, qg_b, kv_ref, mine_ref, came_ref, sums_ref, dq_a, dq_b, out_ref,
    k_s, kt_s, v_s, dk_s, dv_s,
):
    load_keys(kv_ref, k_s, kt_s, v_s)
    for at in (0, 1):
        sums_ref[at] = added(mine_ref[at], came_ref[1 - at])

    def put_a(n, dq):
        dq_a[n] = dq

    def put_b(n, dq):
        dq_b[n] = dq

    gradients(sums_ref, ((qg_a, put_a), (qg_b, put_b)), k_s, kt_s, v_s, dk_s, dv_s)
    put_keys(out_ref, dk_s, dv_s)


def second_kernel(
    qg_a, qg_b, kv_ref, sums_ref, in_a, in_b, dq_a, dq_b, out_ref,
    k_s, kt_s, v_s, dk_s, dv_s,
):
    load_keys(kv_ref, k_s, kt_s, v_s)

    def put_a(n, dq):
        dq_a[n] = in_a[n] + dq

    def put_b(n, dq):
        dq_b[n] = in_b[n] + dq

    gradients(sums_ref, ((qg_a, put_a), (qg_b, put_b)), k_s, kt_s, v_s, dk_s, dv_s)
    put_keys(out_ref, dk_s, dv_s)


def pack_back_kernel(dq_ref, other_ref, mine_ref, came_a, came_b, came_c, send_ref):
    total = mine_ref[0]
    for came in (came_a, came_b, came_c):
        total = total + came[...].astype(f32)
    lanes = jnp.zeros((128, 128 - DH), f32)
    dk = jnp.concatenate([total[0:DH].T, lanes], axis=1)
    dv = jnp.concatenate([total[DH : 2 * DH].T, lanes], axis=1)
    send_ref[:, 0:FPAD, :] = ((dq_ref[...] + other_ref[...]) * SCALE).astype(bf16)
    for a in range(HEADS):
        cells = slice(a * CELLS, (a + 1) * CELLS)
        send_ref[a, FPAD : FPAD + 16, :] = jnp.concatenate([dk[cells], dv[cells]]).astype(bf16)


def weights_kernel(part, patch_ref, qkv_ref, high_ref, low_ref, qkv_s, sems):
    step = 128
    copies = []
    for n in range(D // step):
        rows = slice(n * step, (n + 1) * step)
        source = qkv_ref.at[rows, part * D : (part + 1) * D]
        copies.append(pltpu.make_async_copy(source, qkv_s.at[rows], sems.at[n]))
        copies[-1].start()
    for copy in copies:
        copy.wait()
    both = jnp.dot(patch_ref[...], qkv_s[...], preferred_element_type=f32)
    both = both.reshape(16, 2, 8, D)
    both = jnp.concatenate([both[:, 0].reshape(128, D), both[:, 1].reshape(128, D)])
    high = both.astype(bf16)
    high_ref[...] = high
    low_ref[...] = (both - high.astype(f32)).astype(bf16)


def embed_kernel(back_ref, *refs):
    weights, (canvas_ref, core_out, chip_out, joined, sheet) = refs[:6], refs[6:]
    cols = (((0,), (0,)), ((), ()))
    cell = lax.broadcasted_iota(jnp.int32, (CELLS, TOK), 0)
    token = lax.broadcasted_iota(jnp.int32, (CELLS, TOK), 1)
    holds = (token // (POOL * COLS) == cell // 4) & (token % COLS // POOL == cell % 4)
    spread = jnp.where(holds, 1.0 / POOL**2, 0.0).astype(bf16)
    for h in range(HEADS):
        mine = back_ref[h].astype(f32)
        rows = slice(h * DH, (h + 1) * DH)
        joined[rows] = mine[0:DH]
        for part in (0, 1):
            at = FPAD + part * CELLS
            pooled = mine[at : at + CELLS].astype(bf16)
            wide = lax.dot_general(pooled, spread, cols, preferred_element_type=f32)
            joined[(part + 1) * D + h * DH : (part + 1) * D + (h + 1) * DH] = wide[0:DH]
    values = joined[...].astype(bf16)
    patch = jnp.zeros((256, TOK), f32)
    for n, weight in enumerate(weights):
        rows = slice(n // 2 * D, (n // 2 + 1) * D)
        patch = patch + jnp.dot(weight[...], values[rows], preferred_element_type=f32)
    patch = jnp.concatenate([patch[0:128].T, patch[128:256].T])
    high = patch.astype(bf16)
    rest = patch - high.astype(f32)
    mid = rest.astype(bf16)
    low = (rest - mid.astype(f32)).astype(bf16)
    lane = lax.broadcasted_iota(jnp.int32, (2 * TOK, 256), 1)
    row = lax.broadcasted_iota(jnp.int32, (2 * TOK, 256), 0)
    here = lane % 128 // 8 == row % COLS
    sheet[...] = jnp.zeros_like(sheet)
    parts = jnp.concatenate([high, mid, low], axis=1)
    to = lax.broadcasted_iota(jnp.int32, (128, 256), 1)
    at = lax.broadcasted_iota(jnp.int32, (128, 256), 0)
    for pair in range(8):
        tile = (to // 128 + 2 * pair == at // 8) & (to % 8 == at % 8)
        tile = jnp.where(tile, 1.0, 0.0).astype(bf16)
        tile = jnp.concatenate([tile] * 3)
        wide = jnp.dot(parts, tile, preferred_element_type=f32)
        wide = jnp.where(here, wide, 0.0)
        wide = jnp.sum(wide.reshape(2 * ROWS, COLS, 256), axis=1)
        for k in (0, 1):
            u = 2 * pair + k
            for side in (0, 1):
                piece = wide[side * ROWS : (side + 1) * ROWS, k * 128 : (k + 1) * 128]
                sheet[side, pl.ds(u, ROWS, stride=8), :] += piece
    left = sheet[0]
    right = sheet[1]
    lane = lax.broadcasted_iota(jnp.int32, left.shape, 1)
    center = jnp.where(lane < 124, pltpu.roll(left, 124, 1), 0.0)
    center = center + jnp.where(lane >= 4, pltpu.roll(right, 4, 1), 0.0)
    edges = jnp.where(lane < 4, left, pltpu.roll(right, 8, 1))
    canvas = jnp.concatenate([center, jnp.where(lane < 8, edges, 0.0)], axis=1)
    canvas_ref[...] = canvas
    first = lax.axis_index("c") == 0
    core_out[...] = jnp.where(first, canvas[68:72], canvas[0:4])
    chip_out[...] = jnp.where(first, canvas[0:4], canvas[68:72])


def rows_kernel(canvas_ref, chip_ref, core_ref, center_ref, near_out, far_out):
    first = lax.axis_index("c") == 0
    above = jnp.where(first, chip_ref[...], core_ref[...])
    below = jnp.where(first, core_ref[...], chip_ref[...])
    quiet = jnp.zeros((56, 256), f32)
    canvas = canvas_ref[4:68] + jnp.concatenate([above, quiet, below])
    center_ref[...] = canvas[:, 0:128]
    edges = canvas[:, 128:256].T[0:8]
    left, right = edges[0:4], edges[4:8]
    begins = lax.axis_index("yl") == 0
    near_out[...] = jnp.where(begins, right, left)
    far_out[...] = jnp.where(begins, left, right)


def cols_kernel(center_ref, far_ref, near_ref, out_ref):
    begins = lax.axis_index("yl") == 0
    left = jnp.where(begins, far_ref[...], near_ref[...])
    right = jnp.where(begins, near_ref[...], far_ref[...])
    quiet = jnp.zeros((120, 64), f32)
    out_ref[...] = center_ref[...] + jnp.concatenate([left, quiet, right]).T


def swapped(x, axis, by):
    peers = lax.axis_size(axis)
    return lax.ppermute(x, axis, [(i, i ^ by) for i in range(peers)])


def neighbours(x, axis):
    peers = lax.axis_size(axis)
    pairs = [(i, i + 1) for i in range(1, peers - 1, 2)]
    return lax.ppermute(x, axis, pairs + [(target, source) for source, target in pairs])


def cost(products):
    flops = products * 4 * QUERIES * HALF * 256
    return pl.CostEstimate(flops=flops, bytes_accessed=2**20, transcendentals=2 * QUERIES * HALF)


def combined_weights(w_qkv, w_patch, part):
    shape = jax.ShapeDtypeStruct((256, D), bf16)
    return call(
        functools.partial(weights_kernel, part),
        [shape, shape],
        12,
        [pltpu.VMEM((D, D), bf16), pltpu.SemaphoreType.DMA((D // 128,))],
        [WHOLE, ANYWHERE],
        cost_estimate=pl.CostEstimate(flops=2**20, bytes_accessed=2**16, transcendentals=0),
    )(w_patch, w_qkv)


def on_device(queries, key_states, values, saved_out, grad_out, w_qkv, w_patch):
    tokens = pltpu.VMEM((TOK, D), bf16)
    cells = pltpu.VMEM((2, 4, D), bf16)
    packed = (HEADS, 2 * FPAD + 16, TOK)
    dma = pltpu.SemaphoreType.DMA
    send = call(
        pack_kernel,
        jax.ShapeDtypeStruct(packed, bf16),
        None,
        [tokens, tokens, tokens, cells, cells, pltpu.VMEM(packed, bf16), dma((14,)), dma((4,))],
        [ANYWHERE] * 5,
        out_specs=ANYWHERE,
    )(
        queries.reshape(TOK, D),
        grad_out.reshape(TOK, D),
        saved_out.reshape(TOK, D),
        key_states,
        values,
    )
    got = lax.all_to_all(send, HEAD_AXES, 0, 0, tiled=True)
    kv = call(
        keys_kernel,
        jax.ShapeDtypeStruct((2 * DH, 128), bf16),
        4,
        [pltpu.VMEM((HEADS, 16, 128), bf16), dma(())],
        [ANYWHERE],
    )(got)
    came = [swapped(kv, "z", by) for by in (2, 4, 6)]
    even = jnp.stack([kv] + came)
    odd = swapped(even, "z", 1)
    there = swapped(got, "c", 1)
    keys = pltpu.VMEM((HALF, 128), bf16)
    sums = jax.ShapeDtypeStruct((2, HEADS, 8, TOK), f32)
    even_sums = call(even_sums_kernel, sums, 24, [keys], cost_estimate=cost(1))(got, there, even)
    odd, even_sums = lax.optimization_barrier((odd, even_sums))
    mine = call(odd_sums_kernel, sums, 24, [keys], cost_estimate=cost(1))(got, there, odd, even_sums)
    came = swapped(mine, "c", 1)
    scratch = [keys, pltpu.VMEM((128, HALF), bf16), keys]
    scratch += [pltpu.VMEM((HALF, 128), f32)] * 2
    dq = [jax.ShapeDtypeStruct((HEADS, FPAD, TOK), f32)] * 2
    block = (4, 2 * DH, 128)
    sums, dq_here, dq_there, grads = call(
        first_kernel, [sums] + dq + [jax.ShapeDtypeStruct(block, bf16)], 28, scratch, cost_estimate=cost(5)
    )(got, there, odd, mine, came)
    came = swapped(grads, "z", 1)
    dq_here, dq_there, grads = call(
        second_kernel, dq + [jax.ShapeDtypeStruct(block, f32)], 28, scratch, cost_estimate=cost(5)
    )(got, there, even, sums, dq_here, dq_there)
    dq_here, dq_there, grads, came = lax.optimization_barrier((dq_here, dq_there, grads, came))
    dq_there = swapped(dq_there, "c", 1)
    mine = grads + came.astype(f32)
    mine, w_qkv, w_patch = lax.optimization_barrier((mine, w_qkv, w_patch))
    came = [swapped(mine[n].astype(bf16), "z", 2 * n) for n in (1, 2, 3)]
    weights = [w for part in range(3) for w in combined_weights(w_qkv, w_patch, part)]
    came, weights = lax.optimization_barrier((came, weights))
    send = call(pack_back_kernel, jax.ShapeDtypeStruct((HEADS, FPAD + 16, TOK), bf16), 8)(
        dq_here, dq_there, mine[0:1], *came
    )
    back = lax.all_to_all(send, HEAD_AXES, 0, 0, tiled=True)
    strip = jax.ShapeDtypeStruct((4, 256), f32)
    canvas, to_core, to_chip = call(
        embed_kernel,
        [jax.ShapeDtypeStruct((72, 256), f32), strip, strip],
        24,
        [pltpu.VMEM((3 * D, TOK), f32), pltpu.VMEM((2, 72, 128), f32)],
    )(back, *weights)
    strip = jax.ShapeDtypeStruct((4, 64), f32)
    center, to_near, to_far = call(
        rows_kernel, [jax.ShapeDtypeStruct((64, 128), f32), strip, strip], 4
    )(canvas, neighbours(to_chip, BLK), swapped(to_core, "c", 1))
    return call(cols_kernel, jax.ShapeDtypeStruct((64, 128), f32), 4)(
        center, neighbours(to_far, COL), swapped(to_near, "yl", 1)
    )


def solution(mesh):
    fine = Mesh(mesh.devices.reshape(2, 4, 2, 8, 2), ("yh", "x", "c", "z", "yl"))
    split = P(BLK, COL, None)
    return jax.shard_map(
        on_device,
        mesh=fine,
        in_specs=(split, split, split, split, split, P(), P()),
        out_specs=P(BLK, COL),
        check_vma=False,
    )
```

```python
import functools
import math

import jax
import jax.numpy as jnp
from jax import lax
from jax.experimental import pallas as pl
from jax.experimental.pallas import tpu as pltpu
from jax.sharding import Mesh, PartitionSpec as P

D = 1152
HEADS = 16
DH = D // HEADS
POOL = 4
SCALE = DH**-0.5
SCALE2 = SCALE * math.log2(math.e)
ROWS, COLS = 8, 16
TOK = ROWS * COLS
CELLS = TOK // POOL**2
EXTENDED = TOK + 2 * COLS
FPAD = 80
QUERIES = 2048
HALF = 512
TILE = 1024
TILES = QUERIES // TILE
PER = TILE // TOK
STEP = 256
HEAD_AXES = ("yh", "x", "yl")
BLK = ("yh", "x", "c")
COL = ("z", "yl")
NT = (((1,), (1,)), ((), ()))
WHOLE = pl.BlockSpec(memory_space=pltpu.VMEM)
ANYWHERE = pl.BlockSpec(memory_space=pl.ANY)
bf16, f32 = jnp.bfloat16, jnp.float32


def call(kernel, out, mib, scratch=(), specs=None, **more):
    if specs is not None:
        more["in_specs"] = specs
    return pl.pallas_call(
        kernel,
        out_shape=out,
        scratch_shapes=scratch,
        compiler_params=pltpu.CompilerParams(vmem_limit_bytes=mib * 2**20 if mib else None),
        **more,
    )


def pack_kernel(
    q_in, g_in, o_in, k_in, v_in, out_ref, q_ref, g_ref, o_ref, k_ref, v_ref, send_ref, sems, out_sems
):
    pairs = [(k_in, k_ref), (v_in, v_ref)]
    quarter = TOK // 4
    for source, target in ((q_in, q_ref), (g_in, g_ref), (o_in, o_ref)):
        for at in range(0, TOK, quarter):
            pairs.append((source.at[at : at + quarter], target.at[at : at + quarter]))
    copies = [pltpu.make_async_copy(*pair, sems.at[n]) for n, pair in enumerate(pairs)]
    for copy in copies:
        copy.start()
    for copy in copies[:6]:
        copy.wait()
    q_t = q_ref[...].astype(f32).T
    keys = jnp.concatenate([k_ref[0].astype(f32), k_ref[1].astype(f32)])
    vals = jnp.concatenate([v_ref[0].astype(f32), v_ref[1].astype(f32)])
    lanes = jnp.zeros((CELLS, 128 - DH), f32)
    for h in range(HEADS):
        part = slice(h * DH, (h + 1) * DH)
        send_ref[h, 0:FPAD, :] = jnp.concatenate([q_t[part], jnp.zeros((8, TOK), f32)]).astype(bf16)
        k_h = jnp.concatenate([keys[:, part], lanes], axis=1)
        v_h = jnp.concatenate([vals[:, part], lanes], axis=1)
        send_ref[h, 2 * FPAD : 2 * FPAD + 16, :] = jnp.concatenate([k_h, v_h]).astype(bf16)
    for copy in copies[6:]:
        copy.wait()
    g_t = g_ref[...].astype(f32).T
    prod = g_t * o_ref[...].astype(f32).T
    row = lax.broadcasted_iota(jnp.int32, (8, TOK), 0)
    outs = []
    for h in range(HEADS):
        part = slice(h * DH, (h + 1) * DH)
        dot = -jnp.sum(prod[part], axis=0, keepdims=True)
        high = dot.astype(bf16).astype(f32)
        mid = (dot - high).astype(bf16).astype(f32)
        low = dot - high - mid
        dots = jnp.where(row == 0, high, jnp.where(row == 1, mid, jnp.where(row == 2, low, 0.0)))
        send_ref[h, FPAD : 2 * FPAD, :] = jnp.concatenate([g_t[part], dots]).astype(bf16)
        if h % 4 == 3:
            heads = slice(h - 3, h + 1)
            copy = pltpu.make_async_copy(send_ref.at[heads], out_ref.at[heads], out_sems.at[h // 4])
            copy.start()
            outs.append(copy)
    for copy in outs:
        copy.wait()


def keys_kernel(got_ref, out_ref, kv_ref, sem):
    copy = pltpu.make_async_copy(got_ref.at[:, 2 * FPAD : 2 * FPAD + 16], kv_ref, sem)
    copy.start()
    copy.wait()
    kv = kv_ref[...].astype(f32).reshape(HEADS, 2, CELLS, 128)
    k_t = kv[:, 0].reshape(128, 128).T
    v_t = kv[:, 1].reshape(128, 128).T
    out_ref[...] = jnp.concatenate([k_t[0:DH], v_t[0:DH]]).astype(bf16)


def load_keys(kv_ref, k_s, kt_s=None, v_s=None):
    lane = lax.broadcasted_iota(jnp.int32, (128, 128), 1)
    pad = jnp.zeros((128 - DH, 128), f32)
    norms = jnp.zeros((1, 128), f32)
    for b in range(4):
        kv = kv_ref[b].astype(f32)
        keys = slice(b * 128, (b + 1) * 128)
        k_t = jnp.concatenate([kv[0:DH], pad])
        norms = jnp.maximum(norms, jnp.sum(k_t * k_t, axis=0, keepdims=True))
        k_s[keys] = k_t.T.astype(bf16)
        if kt_s is not None:
            kt_s[:, keys] = k_t.astype(bf16)
            v = jnp.concatenate([kv[DH:], pad]).T
            v_s[keys] = jnp.where((lane >= DH) & (lane < DH + 3), 1.0, v).astype(bf16)
    return jnp.max(norms)


def tile_of(qg_ref, t, row):
    return jnp.concatenate([qg_ref[PER * t + n, row : row + FPAD] for n in range(PER)], axis=1)


def log_sums(q_t, k_s, norm):
    exact = q_t.astype(f32)
    bound = jnp.sqrt(jnp.sum(exact * exact, axis=0, keepdims=True) * norm) * (SCALE2 * 1.001)

    def scores(rows):
        return jnp.dot(k_s[rows, 0:FPAD], q_t, preferred_element_type=f32) * SCALE2

    total = jnp.zeros((1, TILE), f32)
    for at in range(0, HALF, STEP):
        exps = jnp.exp2(scores(slice(at, at + STEP)) - bound)
        total = total + jnp.sum(exps, axis=0, keepdims=True)

    def again():
        def rows(n):
            return pl.ds(pl.multiple_of(n * 128, 128), 128)

        def largest(n, top):
            return jnp.maximum(top, jnp.max(scores(rows(n)), axis=0, keepdims=True))

        top = lax.fori_loop(0, HALF // 128, largest, jnp.full((1, TILE), -jnp.inf, f32))

        def add(n, total):
            return total + jnp.sum(jnp.exp2(scores(rows(n)) - top), axis=0, keepdims=True)

        return top + jnp.log2(lax.fori_loop(0, HALF // 128, add, jnp.zeros((1, TILE), f32)))

    return lax.cond(jnp.min(total) < 2.0**-90, again, lambda: bound + jnp.log2(total))


def put_sums(out_ref, at, t, sums):
    for n in range(PER):
        out_ref[at, PER * t + n] = jnp.broadcast_to(sums[:, n * TOK : (n + 1) * TOK], (8, TOK))


def get_sums(sums_ref, at, t):
    return jnp.concatenate([sums_ref[at, PER * t + n, 0:1] for n in range(PER)], axis=1)


def added(one, two):
    top = jnp.maximum(one, two)
    return top + jnp.log2(jnp.exp2(one - top) + jnp.exp2(two - top))


def even_sums_kernel(qg_a, qg_b, kv_ref, out_ref, k_s):
    norm = load_keys(kv_ref, k_s)
    for at, qg_ref in enumerate((qg_a, qg_b)):

        def tile(t, _):
            put_sums(out_ref, at, t, log_sums(tile_of(qg_ref, t, 0), k_s, norm))
            return 0

        lax.fori_loop(0, TILES, tile, 0)


def odd_sums_kernel(qg_a, qg_b, kv_ref, even_ref, out_ref, k_s):
    norm = load_keys(kv_ref, k_s)
    for at, qg_ref in enumerate((qg_a, qg_b)):

        def tile(t, _):
            mine = log_sums(tile_of(qg_ref, t, 0), k_s, norm)
            put_sums(out_ref, at, t, added(mine, get_sums(even_ref, at, t)))
            return 0

        lax.fori_loop(0, TILES, tile, 0)


def gradients(sums_ref, work, k_s, kt_s, v_s, dk_s, dv_s):
    dk_s[...] = jnp.zeros_like(dk_s)
    dv_s[...] = jnp.zeros_like(dv_s)
    for at_core, (qg_ref, put_dq) in enumerate(work):

        def tile(t, _):
            q_t = tile_of(qg_ref, t, 0)
            g_t = tile_of(qg_ref, t, FPAD)
            sums = get_sums(sums_ref, at_core, t)
            dq = jnp.zeros((FPAD, TILE), f32)
            for at in range(0, HALF, STEP):
                b = slice(at, at + STEP)
                scores = jnp.dot(k_s[b, 0:FPAD], q_t, preferred_element_type=f32)
                probs = jnp.exp2(scores * SCALE2 - sums)
                half_probs = probs.astype(bf16)
                shifted = jnp.dot(v_s[b, 0:FPAD], g_t, preferred_element_type=f32)
                ds = (probs * shifted).astype(bf16)
                dk_s[b, 0:FPAD] += lax.dot_general(ds, q_t, NT, preferred_element_type=f32)
                dv_s[b, 0:FPAD] += lax.dot_general(half_probs, g_t, NT, preferred_element_type=f32)
                dq = dq + jnp.dot(kt_s[0:FPAD, b], ds, preferred_element_type=f32)
            for n in range(PER):
                put_dq(PER * t + n, dq[:, n * TOK : (n + 1) * TOK])
            return 0

        lax.fori_loop(0, TILES, tile, 0)


def put_keys(out_ref, dk_s, dv_s):
    dk_t = dk_s[...].T
    dv_t = dv_s[...].T
    for b in range(4):
        keys = slice(b * 128, (b + 1) * 128)
        block = jnp.concatenate([dk_t[0:DH, keys] * SCALE, dv_t[0:DH, keys]])
        out_ref[b] = block.astype(out_ref.dtype)


def first_kernel(
    qg_a, qg_b, kv_ref, mine_ref, came_ref, sums_ref, dq_a, dq_b, out_ref,
    k_s, kt_s, v_s, dk_s, dv_s,
):
    load_keys(kv_ref, k_s, kt_s, v_s)
    for at in (0, 1):
        sums_ref[at] = added(mine_ref[at], came_ref[1 - at])

    def put_a(n, dq):
        dq_a[n] = dq

    def put_b(n, dq):
        dq_b[n] = dq

    gradients(sums_ref, ((qg_a, put_a), (qg_b, put_b)), k_s, kt_s, v_s, dk_s, dv_s)
    put_keys(out_ref, dk_s, dv_s)


def edge_rows(dq):
    edges = jnp.concatenate([dq[0:DH, 0:COLS], dq[0:DH, TOK - COLS :]], axis=1)
    pad = jnp.zeros((24, 32), f32)
    return jnp.concatenate([edges[0:24], edges[24:48], edges[48:72], pad], axis=1)


def second_kernel(
    qg_a, qg_b, kv_ref, sums_ref, in_a, in_b, dq_a, dq_b, edge_a, edge_b, out_ref,
    k_s, kt_s, v_s, dk_s, dv_s,
):
    load_keys(kv_ref, k_s, kt_s, v_s)

    def put_a(n, dq):
        dq = in_a[n] + dq
        dq_a[n] = dq
        edge_a[n] = edge_rows(dq)

    def put_b(n, dq):
        dq = in_b[n] + dq
        dq_b[n] = dq
        edge_b[n] = edge_rows(dq)

    gradients(sums_ref, ((qg_a, put_a), (qg_b, put_b)), k_s, kt_s, v_s, dk_s, dv_s)
    put_keys(out_ref, dk_s, dv_s)


def keys_sum_kernel(mine_ref, came_a, came_b, came_c, out_ref):
    total = mine_ref[0]
    for came in (came_a, came_b, came_c):
        total = total + came[...].astype(f32)
    out_ref[...] = total.astype(bf16)


def beside(x, first):
    none = jnp.zeros_like(x[0:2])
    above = jnp.where(first, jnp.concatenate([none, x[:-2]]), x)
    below = jnp.where(first, x, jnp.concatenate([x[2:], none]))
    return above, below


def pack_back_kernel(dq_ref, came_ref, edge_ref, came_edge_ref, keys_ref, other_ref, send_ref):
    first = lax.axis_index("c") == 0
    dq = (dq_ref[...] + came_ref[...])[:, 0:DH] * SCALE
    above, below = beside((edge_ref[...] + came_edge_ref[...]) * SCALE, first)
    lane = lax.broadcasted_iota(jnp.int32, (HEADS, 24, 128), 2)
    above = pltpu.roll(above, 128 - COLS, 2)
    edges = jnp.where(lane % 32 < COLS, above, pltpu.roll(below, COLS, 2))
    lanes = jnp.zeros((128, 128 - DH), f32)
    row = lax.broadcasted_iota(jnp.int32, (HEADS, CELLS, 128), 1)

    def cells(ref, part):
        rows = ref[...].astype(f32)[part * DH : (part + 1) * DH].T
        return jnp.concatenate([rows, lanes], axis=1).reshape(HEADS, CELLS, 128)

    parts = [dq, edges, cells(keys_ref, 0), cells(keys_ref, 1)]
    for part in (0, 1):
        above, below = beside(cells(other_ref, part), first)
        half = CELLS // 2
        parts.append(jnp.where(row < half, pltpu.roll(above, half, 1), pltpu.roll(below, half, 1)))
    send_ref[...] = jnp.concatenate(parts, axis=1).astype(bf16)


def weights_kernel(part, patch_ref, qkv_ref, high_ref, low_ref, qkv_s, sems):
    step = 128
    copies = []
    for n in range(D // step):
        rows = slice(n * step, (n + 1) * step)
        source = qkv_ref.at[rows, part * D : (part + 1) * D]
        copies.append(pltpu.make_async_copy(source, qkv_s.at[rows], sems.at[n]))
        copies[-1].start()
    for copy in copies:
        copy.wait()
    both = jnp.dot(patch_ref[...], qkv_s[...], preferred_element_type=f32)
    both = both.reshape(16, 2, 8, D)
    both = jnp.concatenate([both[:, 0].reshape(128, D), both[:, 1].reshape(128, D)])
    high = both.astype(bf16)
    high_ref[...] = high
    low_ref[...] = (both - high.astype(f32)).astype(bf16)


def embed_kernel(back_ref, *refs):
    weights, (center_ref, near_out, far_out, joined, sheet) = refs[:6], refs[6:]
    cols = (((0,), (0,)), ((), ()))
    cell = lax.broadcasted_iota(jnp.int32, (2 * CELLS, 2 * TOK), 0)
    token = lax.broadcasted_iota(jnp.int32, (2 * CELLS, 2 * TOK), 1)
    mine = token // (POOL * COLS) * 4 + token % COLS // POOL
    beyond = CELLS + (token - TOK) // COLS * 4 + token % COLS // POOL
    holds = (cell == jnp.where(token < TOK, mine, beyond)) & (token < EXTENDED)
    spread = jnp.where(holds, 1.0 / POOL**2, 0.0).astype(bf16)
    for h in range(HEADS):
        head = back_ref[h].astype(f32)
        rows = slice(h * DH, (h + 1) * DH)
        joined[rows, 0:TOK] = head[0:DH]
        edges = head[DH : DH + 24]
        edges = [edges, pltpu.roll(edges, 96, 1), pltpu.roll(edges, 64, 1)]
        joined[rows, TOK:] = jnp.concatenate(edges)
        for part in (0, 1):
            at = DH + 24 + part * CELLS
            pooled = jnp.concatenate([head[at : at + CELLS], head[at + 16 : at + 16 + CELLS]]).astype(bf16)
            wide = lax.dot_general(pooled, spread, cols, preferred_element_type=f32)
            joined[(part + 1) * D + h * DH : (part + 1) * D + (h + 1) * DH] = wide[0:DH]
    values = joined[...].astype(bf16)
    patch = jnp.zeros((256, 2 * TOK), f32)
    for n, weight in enumerate(weights):
        rows = slice(n // 2 * D, (n // 2 + 1) * D)
        patch = patch + jnp.dot(weight[...], values[rows], preferred_element_type=f32)
    sides = []
    for side in (0, 1):
        rows = slice(side * 128, (side + 1) * 128)
        sides += [patch[rows, 0:TOK].T, patch[rows, TOK:].T[0 : EXTENDED - TOK]]
    patch = jnp.concatenate(sides)
    high = patch.astype(bf16)
    rest = patch - high.astype(f32)
    mid = rest.astype(bf16)
    low = (rest - mid.astype(f32)).astype(bf16)
    lane = lax.broadcasted_iota(jnp.int32, (2 * EXTENDED, 256), 1)
    row = lax.broadcasted_iota(jnp.int32, (2 * EXTENDED, 256), 0)
    here = lane % 128 // 8 == row % COLS
    sheet[...] = jnp.zeros_like(sheet)
    parts = jnp.concatenate([high, mid, low], axis=1)
    to = lax.broadcasted_iota(jnp.int32, (128, 256), 1)
    at = lax.broadcasted_iota(jnp.int32, (128, 256), 0)
    for pair in range(8):
        tile = (to // 128 + 2 * pair == at // 8) & (to % 8 == at % 8)
        tile = jnp.where(tile, 1.0, 0.0).astype(bf16)
        tile = jnp.concatenate([tile] * 3)
        wide = jnp.dot(parts, tile, preferred_element_type=f32)
        wide = jnp.where(here, wide, 0.0)
        wide = jnp.sum(wide.reshape(2 * (ROWS + 2), COLS, 256), axis=1)
        for k in (0, 1):
            u = 2 * pair + k
            for side in (0, 1):
                at_side = side * (ROWS + 2)
                piece = wide[at_side : at_side + ROWS + 2, k * 128 : (k + 1) * 128]
                sheet[side, pl.ds(u, ROWS, stride=8), :] += piece[0:ROWS]
                if u >= 12:
                    sheet[side, u - 8 : u - 7, :] += piece[ROWS : ROWS + 1]
                if u < 4:
                    sheet[side, 64 + u : 65 + u, :] += piece[ROWS + 1 :]
    left = sheet[0, 4:68]
    right = sheet[1, 4:68]
    lane = lax.broadcasted_iota(jnp.int32, left.shape, 1)
    center = jnp.where(lane < 124, pltpu.roll(left, 124, 1), 0.0)
    center_ref[...] = center + jnp.where(lane >= 4, pltpu.roll(right, 4, 1), 0.0)
    left = left.T[0:4]
    right = right.T[124:128]
    begins = lax.axis_index("yl") == 0
    near_out[...] = jnp.where(begins, right, left)
    far_out[...] = jnp.where(begins, left, right)


def cols_kernel(center_ref, far_ref, near_ref, out_ref):
    begins = lax.axis_index("yl") == 0
    left = jnp.where(begins, far_ref[...], near_ref[...])
    right = jnp.where(begins, near_ref[...], far_ref[...])
    quiet = jnp.zeros((120, 64), f32)
    out_ref[...] = center_ref[...] + jnp.concatenate([left, quiet, right]).T


def swapped(x, axis, by):
    peers = lax.axis_size(axis)
    return lax.ppermute(x, axis, [(i, i ^ by) for i in range(peers)])


def neighbours(x, axis):
    peers = lax.axis_size(axis)
    pairs = [(i, i + 1) for i in range(1, peers - 1, 2)]
    return lax.ppermute(x, axis, pairs + [(target, source) for source, target in pairs])


def cost(products):
    flops = products * 4 * QUERIES * HALF * 256
    return pl.CostEstimate(flops=flops, bytes_accessed=2**20, transcendentals=2 * QUERIES * HALF)


def combined_weights(w_qkv, w_patch, part):
    shape = jax.ShapeDtypeStruct((256, D), bf16)
    return call(
        functools.partial(weights_kernel, part),
        [shape, shape],
        12,
        [pltpu.VMEM((D, D), bf16), pltpu.SemaphoreType.DMA((D // 128,))],
        [WHOLE, ANYWHERE],
        cost_estimate=pl.CostEstimate(flops=2**20, bytes_accessed=2**16, transcendentals=0),
    )(w_patch, w_qkv)


def on_device(queries, key_states, values, saved_out, grad_out, w_qkv, w_patch):
    tokens = pltpu.VMEM((TOK, D), bf16)
    cells = pltpu.VMEM((2, 4, D), bf16)
    packed = (HEADS, 2 * FPAD + 16, TOK)
    dma = pltpu.SemaphoreType.DMA
    send = call(
        pack_kernel,
        jax.ShapeDtypeStruct(packed, bf16),
        None,
        [tokens, tokens, tokens, cells, cells, pltpu.VMEM(packed, bf16), dma((14,)), dma((4,))],
        [ANYWHERE] * 5,
        out_specs=ANYWHERE,
    )(
        queries.reshape(TOK, D),
        grad_out.reshape(TOK, D),
        saved_out.reshape(TOK, D),
        key_states,
        values,
    )
    got = lax.all_to_all(send, HEAD_AXES, 0, 0, tiled=True)
    kv = call(
        keys_kernel,
        jax.ShapeDtypeStruct((2 * DH, 128), bf16),
        4,
        [pltpu.VMEM((HEADS, 16, 128), bf16), dma(())],
        [ANYWHERE],
    )(got)
    came = [swapped(kv, "z", by) for by in (2, 4, 6)]
    even = jnp.stack([kv] + came)
    odd = swapped(even, "z", 1)
    there = swapped(got, "c", 1)
    keys = pltpu.VMEM((HALF, 128), bf16)
    sums = jax.ShapeDtypeStruct((2, HEADS, 8, TOK), f32)
    even_sums = call(even_sums_kernel, sums, 24, [keys], cost_estimate=cost(1))(got, there, even)
    odd, even_sums = lax.optimization_barrier((odd, even_sums))
    mine = call(odd_sums_kernel, sums, 24, [keys], cost_estimate=cost(1))(got, there, odd, even_sums)
    came = swapped(mine, "c", 1)
    scratch = [keys, pltpu.VMEM((128, HALF), bf16), keys]
    scratch += [pltpu.VMEM((HALF, 128), f32)] * 2
    dq = [jax.ShapeDtypeStruct((HEADS, FPAD, TOK), f32)] * 2
    block = (4, 2 * DH, 128)
    sums, dq_here, dq_there, grads = call(
        first_kernel, [sums] + dq + [jax.ShapeDtypeStruct(block, bf16)], 28, scratch, cost_estimate=cost(5)
    )(got, there, odd, mine, came)
    came = swapped(grads, "z", 1)
    edges = [jax.ShapeDtypeStruct((HEADS, 24, TOK), f32)] * 2
    *dq, grads = call(
        second_kernel,
        dq + edges + [jax.ShapeDtypeStruct(block, f32)],
        28,
        scratch,
        cost_estimate=cost(5),
    )(got, there, even, sums, dq_here, dq_there)
    dq, grads, came = lax.optimization_barrier((dq, grads, came))
    dq_here, dq_there, edge_here, edge_there = dq
    dq_there = swapped(dq_there, "c", 1)
    edge_here = swapped(edge_here, "c", 1)
    mine = grads + came.astype(f32)
    mine, w_qkv, w_patch = lax.optimization_barrier((mine, w_qkv, w_patch))
    came = [swapped(mine[n].astype(bf16), "z", 2 * n) for n in (1, 2, 3)]
    weights = [w for part in range(3) for w in combined_weights(w_qkv, w_patch, part)]
    came, weights = lax.optimization_barrier((came, weights))
    keys = call(keys_sum_kernel, jax.ShapeDtypeStruct((2 * DH, 128), bf16), 4)(mine[0:1], *came)
    other = swapped(keys, "c", 1)
    send = call(pack_back_kernel, jax.ShapeDtypeStruct((HEADS, 128, TOK), bf16), 16)(
        dq_here, dq_there, edge_there, edge_here, keys, other
    )
    back = lax.all_to_all(send, HEAD_AXES, 0, 0, tiled=True)
    strip = jax.ShapeDtypeStruct((4, 64), f32)
    center, to_near, to_far = call(
        embed_kernel,
        [jax.ShapeDtypeStruct((64, 128), f32), strip, strip],
        28,
        [pltpu.VMEM((3 * D, 2 * TOK), f32), pltpu.VMEM((2, 72, 128), f32)],
    )(back, *weights)
    return call(cols_kernel, jax.ShapeDtypeStruct((64, 128), f32), 4)(
        center, neighbours(to_far, COL), swapped(to_near, "yl", 1)
    )


def solution(mesh):
    fine = Mesh(mesh.devices.reshape(2, 4, 2, 8, 2), ("yh", "x", "c", "z", "yl"))
    split = P(BLK, COL, None)
    return jax.shard_map(
        on_device,
        mesh=fine,
        in_specs=(split, split, split, split, split, P(), P()),
        out_specs=P(BLK, COL),
        check_vma=False,
    )
```

```python
import functools
import math

import jax
import jax.numpy as jnp
from jax import lax
from jax.experimental import pallas as pl
from jax.experimental.pallas import tpu as pltpu
from jax.sharding import Mesh, PartitionSpec as P

D = 1152
HEADS = 16
DH = D // HEADS
POOL = 4
SCALE = DH**-0.5
SCALE2 = SCALE * math.log2(math.e)
ROWS, COLS = 8, 16
TOK = ROWS * COLS
CELLS = TOK // POOL**2
EXTENDED = TOK + 2 * COLS
FPAD = 80
QUERIES = 2048
HALF = 512
TILE = 1024
TILES = QUERIES // TILE
PER = TILE // TOK
STEP = 256
HEAD_AXES = ("yh", "x", "yl")
BLK = ("yh", "x", "c")
COL = ("z", "yl")
NT = (((1,), (1,)), ((), ()))
WHOLE = pl.BlockSpec(memory_space=pltpu.VMEM)
ANYWHERE = pl.BlockSpec(memory_space=pl.ANY)
bf16, f32 = jnp.bfloat16, jnp.float32


def call(kernel, out, mib, scratch=(), specs=None, **more):
    if specs is not None:
        more["in_specs"] = specs
    return pl.pallas_call(
        kernel,
        out_shape=out,
        scratch_shapes=scratch,
        compiler_params=pltpu.CompilerParams(vmem_limit_bytes=mib * 2**20 if mib else None),
        **more,
    )


def pack_kernel(
    q_in, g_in, o_in, k_in, v_in, out_ref, q_ref, g_ref, o_ref, k_ref, v_ref, send_ref, sems, out_sems
):
    pairs = [(k_in, k_ref), (v_in, v_ref)]
    quarter = TOK // 4
    for source, target in ((q_in, q_ref), (g_in, g_ref), (o_in, o_ref)):
        for at in range(0, TOK, quarter):
            pairs.append((source.at[at : at + quarter], target.at[at : at + quarter]))
    copies = [pltpu.make_async_copy(*pair, sems.at[n]) for n, pair in enumerate(pairs)]
    for copy in copies:
        copy.start()
    for copy in copies[:6]:
        copy.wait()
    q_t = q_ref[...].astype(f32).T
    keys = jnp.concatenate([k_ref[0].astype(f32), k_ref[1].astype(f32)])
    vals = jnp.concatenate([v_ref[0].astype(f32), v_ref[1].astype(f32)])
    lanes = jnp.zeros((CELLS, 128 - DH), f32)
    for h in range(HEADS):
        part = slice(h * DH, (h + 1) * DH)
        send_ref[h, 0:FPAD, :] = jnp.concatenate([q_t[part], jnp.zeros((8, TOK), f32)]).astype(bf16)
        k_h = jnp.concatenate([keys[:, part], lanes], axis=1)
        v_h = jnp.concatenate([vals[:, part], lanes], axis=1)
        send_ref[h, 2 * FPAD : 2 * FPAD + 16, :] = jnp.concatenate([k_h, v_h]).astype(bf16)
    for copy in copies[6:]:
        copy.wait()
    g_t = g_ref[...].astype(f32).T
    prod = g_t * o_ref[...].astype(f32).T
    row = lax.broadcasted_iota(jnp.int32, (8, TOK), 0)
    outs = []
    for h in range(HEADS):
        part = slice(h * DH, (h + 1) * DH)
        dot = -jnp.sum(prod[part], axis=0, keepdims=True)
        high = dot.astype(bf16).astype(f32)
        mid = (dot - high).astype(bf16).astype(f32)
        low = dot - high - mid
        dots = jnp.where(row == 0, high, jnp.where(row == 1, mid, jnp.where(row == 2, low, 0.0)))
        send_ref[h, FPAD : 2 * FPAD, :] = jnp.concatenate([g_t[part], dots]).astype(bf16)
        if h % 4 == 3:
            heads = slice(h - 3, h + 1)
            copy = pltpu.make_async_copy(send_ref.at[heads], out_ref.at[heads], out_sems.at[h // 4])
            copy.start()
            outs.append(copy)
    for copy in outs:
        copy.wait()


def keys_kernel(got_ref, out_ref, kv_ref, sem):
    copy = pltpu.make_async_copy(got_ref.at[:, 2 * FPAD : 2 * FPAD + 16], kv_ref, sem)
    copy.start()
    copy.wait()
    kv = kv_ref[...].astype(f32).reshape(HEADS, 2, CELLS, 128)
    k_t = kv[:, 0].reshape(128, 128).T
    v_t = kv[:, 1].reshape(128, 128).T
    out_ref[...] = jnp.concatenate([k_t[0:DH], v_t[0:DH]]).astype(bf16)


def load_keys(kv_ref, k_s, kt_s=None, v_s=None):
    lane = lax.broadcasted_iota(jnp.int32, (128, 128), 1)
    pad = jnp.zeros((128 - DH, 128), f32)
    norms = jnp.zeros((1, 128), f32)
    for b in range(4):
        kv = kv_ref[b].astype(f32)
        keys = slice(b * 128, (b + 1) * 128)
        k_t = jnp.concatenate([kv[0:DH], pad])
        norms = jnp.maximum(norms, jnp.sum(k_t * k_t, axis=0, keepdims=True))
        k_s[keys] = k_t.T.astype(bf16)
        if kt_s is not None:
            kt_s[:, keys] = k_t.astype(bf16)
            v = jnp.concatenate([kv[DH:], pad]).T
            v_s[keys] = jnp.where((lane >= DH) & (lane < DH + 3), 1.0, v).astype(bf16)
    return jnp.max(norms)


def tile_of(qg_ref, t, row):
    return jnp.concatenate([qg_ref[PER * t + n, row : row + FPAD] for n in range(PER)], axis=1)


def log_sums(q_t, k_s, norm):
    exact = q_t.astype(f32)
    bound = jnp.sqrt(jnp.sum(exact * exact, axis=0, keepdims=True) * norm) * (SCALE2 * 1.001)

    def scores(rows):
        return jnp.dot(k_s[rows, 0:FPAD], q_t, preferred_element_type=f32) * SCALE2

    total = jnp.zeros((1, TILE), f32)
    for at in range(0, HALF, STEP):
        exps = jnp.exp2(scores(slice(at, at + STEP)) - bound)
        total = total + jnp.sum(exps, axis=0, keepdims=True)

    def again():
        def rows(n):
            return pl.ds(pl.multiple_of(n * 128, 128), 128)

        def largest(n, top):
            return jnp.maximum(top, jnp.max(scores(rows(n)), axis=0, keepdims=True))

        top = lax.fori_loop(0, HALF // 128, largest, jnp.full((1, TILE), -jnp.inf, f32))

        def add(n, total):
            return total + jnp.sum(jnp.exp2(scores(rows(n)) - top), axis=0, keepdims=True)

        return top + jnp.log2(lax.fori_loop(0, HALF // 128, add, jnp.zeros((1, TILE), f32)))

    return lax.cond(jnp.min(total) < 2.0**-90, again, lambda: bound + jnp.log2(total))


def put_sums(out_ref, at, t, sums):
    for n in range(PER):
        out_ref[at, PER * t + n] = jnp.broadcast_to(sums[:, n * TOK : (n + 1) * TOK], (8, TOK))


def get_sums(sums_ref, at, t):
    return jnp.concatenate([sums_ref[at, PER * t + n, 0:1] for n in range(PER)], axis=1)


def added(one, two):
    top = jnp.maximum(one, two)
    return top + jnp.log2(jnp.exp2(one - top) + jnp.exp2(two - top))


def even_sums_kernel(qg_a, qg_b, kv_ref, out_ref, k_s):
    norm = load_keys(kv_ref, k_s)
    for at, qg_ref in enumerate((qg_a, qg_b)):

        def tile(t, _):
            put_sums(out_ref, at, t, log_sums(tile_of(qg_ref, t, 0), k_s, norm))
            return 0

        lax.fori_loop(0, TILES, tile, 0)


def odd_sums_kernel(qg_a, qg_b, kv_ref, even_ref, out_ref, k_s):
    norm = load_keys(kv_ref, k_s)
    for at, qg_ref in enumerate((qg_a, qg_b)):

        def tile(t, _):
            mine = log_sums(tile_of(qg_ref, t, 0), k_s, norm)
            put_sums(out_ref, at, t, added(mine, get_sums(even_ref, at, t)))
            return 0

        lax.fori_loop(0, TILES, tile, 0)


def gradients(sums_ref, work, k_s, kt_s, v_s, dk_s, dv_s):
    dk_s[...] = jnp.zeros_like(dk_s)
    dv_s[...] = jnp.zeros_like(dv_s)
    for at_core, (qg_ref, put_dq) in enumerate(work):

        def tile(t, _):
            q_t = tile_of(qg_ref, t, 0)
            g_t = tile_of(qg_ref, t, FPAD)
            sums = get_sums(sums_ref, at_core, t)
            dq = jnp.zeros((FPAD, TILE), f32)
            for at in range(0, HALF, STEP):
                b = slice(at, at + STEP)
                scores = jnp.dot(k_s[b, 0:FPAD], q_t, preferred_element_type=f32)
                probs = jnp.exp2(scores * SCALE2 - sums)
                half_probs = probs.astype(bf16)
                shifted = jnp.dot(v_s[b, 0:FPAD], g_t, preferred_element_type=f32)
                ds = (probs * shifted).astype(bf16)
                dk_s[b, 0:FPAD] += lax.dot_general(ds, q_t, NT, preferred_element_type=f32)
                dv_s[b, 0:FPAD] += lax.dot_general(half_probs, g_t, NT, preferred_element_type=f32)
                dq = dq + jnp.dot(kt_s[0:FPAD, b], ds, preferred_element_type=f32)
            for n in range(PER):
                put_dq(PER * t + n, dq[:, n * TOK : (n + 1) * TOK])
            return 0

        lax.fori_loop(0, TILES, tile, 0)


def put_keys(out_ref, dk_s, dv_s):
    dk_t = dk_s[...].T
    dv_t = dv_s[...].T
    for b in range(4):
        keys = slice(b * 128, (b + 1) * 128)
        block = jnp.concatenate([dk_t[0:DH, keys] * SCALE, dv_t[0:DH, keys]])
        out_ref[b] = block.astype(out_ref.dtype)


def first_kernel(
    qg_a, qg_b, kv_ref, mine_ref, came_ref, sums_ref, dq_a, dq_b, out_ref,
    k_s, kt_s, v_s, dk_s, dv_s,
):
    load_keys(kv_ref, k_s, kt_s, v_s)
    for at in (0, 1):
        sums_ref[at] = added(mine_ref[at], came_ref[1 - at])

    def put_a(n, dq):
        dq_a[n] = dq

    def put_b(n, dq):
        dq_b[n] = dq

    gradients(sums_ref, ((qg_a, put_a), (qg_b, put_b)), k_s, kt_s, v_s, dk_s, dv_s)
    put_keys(out_ref, dk_s, dv_s)


def edge_rows(dq):
    lane = lax.broadcasted_iota(jnp.int32, (24, TOK), 1)
    edges = pltpu.roll(dq[0:24], COLS, 1)
    for n in (1, 2):
        rolled = pltpu.roll(dq[24 * n : 24 * (n + 1)], COLS + 32 * n, 1)
        edges = jnp.where(lane < 32 * n, edges, rolled)
    return edges


def second_kernel(
    qg_a, qg_b, kv_ref, sums_ref, in_a, in_b, dq_a, dq_b, edge_a, edge_b, out_ref,
    k_s, kt_s, v_s, dk_s, dv_s,
):
    load_keys(kv_ref, k_s, kt_s, v_s)

    def put_a(n, dq):
        dq = in_a[n] + dq
        dq_a[n] = dq
        edge_a[n] = edge_rows(dq)

    def put_b(n, dq):
        dq = in_b[n] + dq
        dq_b[n] = dq
        edge_b[n] = edge_rows(dq)

    gradients(sums_ref, ((qg_a, put_a), (qg_b, put_b)), k_s, kt_s, v_s, dk_s, dv_s)
    put_keys(out_ref, dk_s, dv_s)


def keys_sum_kernel(mine_ref, came_a, came_b, came_c, out_ref):
    total = mine_ref[0]
    for came in (came_a, came_b, came_c):
        total = total + came[...].astype(f32)
    out_ref[...] = total.astype(bf16)


def beside(x, first):
    none = jnp.zeros_like(x[0:2])
    above = jnp.where(first, jnp.concatenate([none, x[:-2]]), x)
    below = jnp.where(first, x, jnp.concatenate([x[2:], none]))
    return above, below


def pack_back_kernel(dq_ref, came_ref, edge_ref, came_edge_ref, keys_ref, other_ref, send_ref):
    first = lax.axis_index("c") == 0
    dq = (dq_ref[...] + came_ref[...])[:, 0:DH] * SCALE
    above, below = beside((edge_ref[...] + came_edge_ref[...]) * SCALE, first)
    lane = lax.broadcasted_iota(jnp.int32, (HEADS, 24, 128), 2)
    edges = jnp.where(lane % 32 < COLS, above, below)
    lanes = jnp.zeros((128, 128 - DH), f32)
    row = lax.broadcasted_iota(jnp.int32, (HEADS, CELLS, 128), 1)

    def cells(ref, part):
        rows = ref[...].astype(f32)[part * DH : (part + 1) * DH].T
        return jnp.concatenate([rows, lanes], axis=1).reshape(HEADS, CELLS, 128)

    parts = [dq, edges, cells(keys_ref, 0), cells(keys_ref, 1)]
    for part in (0, 1):
        above, below = beside(cells(other_ref, part), first)
        half = CELLS // 2
        parts.append(jnp.where(row < half, pltpu.roll(above, half, 1), pltpu.roll(below, half, 1)))
    send_ref[...] = jnp.concatenate(parts, axis=1).astype(bf16)


def weights_kernel(part, patch_ref, qkv_ref, out_ref, qkv_s, sems):
    step = 128
    copies = []
    for n in range(D // step):
        rows = slice(n * step, (n + 1) * step)
        source = qkv_ref.at[rows, part * D : (part + 1) * D]
        copies.append(pltpu.make_async_copy(source, qkv_s.at[rows], sems.at[n]))
        copies[-1].start()
    for copy in copies:
        copy.wait()
    both = jnp.dot(patch_ref[...], qkv_s[...], preferred_element_type=f32)
    both = both.reshape(16, 2, 8, D)
    both = jnp.concatenate([both[:, 0].reshape(128, D), both[:, 1].reshape(128, D)])
    high = both.astype(bf16)
    out_ref[0:256] = high
    out_ref[256:512] = (both - high.astype(f32)).astype(bf16)


def split(x):
    high = x.astype(bf16)
    return high, (x - high.astype(f32)).astype(bf16)


def iota(shape, dim):
    return lax.broadcasted_iota(jnp.int32, shape, dim)


def one_hot(where, value=1.0):
    return jnp.where(where, value, 0.0).astype(bf16)


def embed_kernel(back_ref, *refs):
    weights, (center_ref, near_out, far_out, joined, pooled, sheet) = refs[:3], refs[3:]
    for h in range(0, HEADS, 2):
        pair = []
        wide = []
        for n in (h, h + 1):
            pair.append(back_ref[n, 0:TOK].astype(f32)[0:DH])
            edges = back_ref[n, 64 : 64 + 32].astype(f32)[DH - 64 :]
            wide += [edges, pltpu.roll(edges, 96, 1), pltpu.roll(edges, 64, 1)]
        rows = slice(h * DH, (h + 2) * DH)
        joined[rows, 0:TOK] = jnp.concatenate(pair).astype(bf16)
        joined[rows, TOK:] = jnp.concatenate(wide).astype(bf16)
    at = DH + 24
    group = iota((DH, 128), 1) // 16
    for h in range(0, HEADS, 4):
        cells = []
        for part in (0, 1):
            for n in range(h, h + 4):
                head = back_ref[n, at:].astype(f32)
                cells += [head[part * CELLS : (part + 1) * CELLS], head[16 + part * CELLS : 16 + (part + 1) * CELLS]]
        cells = jnp.concatenate(cells).T[0:DH]
        for part in (0, 1):
            for n in (0, 2):
                two = [jnp.where(group == 4 * part + k, cells, 0.0) for k in (n, n + 1)]
                rows = part * D + (h + n) * DH
                pooled[rows : rows + 2 * DH] = jnp.concatenate(two).astype(bf16)
    patch = jnp.dot(weights[0][...], joined[...], preferred_element_type=f32)
    patch = patch[0:256] + patch[256:512]
    cells = jnp.dot(weights[1][...], pooled[0:D], preferred_element_type=f32)
    cells = cells + jnp.dot(weights[2][...], pooled[D:], preferred_element_type=f32)
    cells = jnp.concatenate(split(cells[0:256] + cells[256:512]), axis=1)
    cell, token = iota((256, 256), 0) % 16, iota((256, 256), 1)
    mine = token // (POOL * COLS) * 4 + token % COLS // POOL
    beyond = CELLS + (token - TOK) // COLS * 4 + token % COLS // POOL
    holds = (cell == jnp.where(token < TOK, mine, beyond)) & (token < EXTENDED)
    patch = patch + jnp.dot(cells, one_hot(holds, 1.0 / POOL**2), preferred_element_type=f32)
    to, token = iota((EXTENDED, 256), 0), iota((EXTENDED, 256), 1)
    far = to - TOK
    column = jnp.where(to < TOK, to // 8, far // 8 * 4 + far % 8 // 2)
    source = jnp.where(to < TOK, to % 8 * COLS, TOK + far % 2 * COLS) + column
    turned = lax.dot_general(
        one_hot(token == source), jnp.concatenate(split(patch)), NT, preferred_element_type=f32
    ).astype(bf16)
    sheet[...] = jnp.zeros_like(sheet)
    here = iota((EXTENDED, 256), 1) % 128 // 8 == column
    to, at = iota((256, 256), 1), iota((256, 256), 0) % 128
    for pair in range(8):
        tile = one_hot((to // 128 + 2 * pair == at // 8) & (to % 8 == at % 8))
        for side in (0, 1):
            parts = [turned[:, n * 256 + side * 128 : n * 256 + (side + 1) * 128] for n in (0, 1)]
            wide = jnp.dot(jnp.concatenate(parts, axis=1), tile, preferred_element_type=f32)
            wide = jnp.where(here, wide, 0.0)
            own = jnp.sum(wide[0:TOK].reshape(COLS, ROWS, 256), axis=0)
            edge = jnp.sum(wide[TOK:].reshape(4, 8, 256), axis=0)
            edge = edge + pltpu.roll(edge, 4, 0)
            edge = edge + pltpu.roll(edge, 2, 0)
            for k in (0, 1):
                u = 2 * pair + k
                lanes = slice(k * 128, (k + 1) * 128)
                sheet[side, pl.ds(u, ROWS, stride=8), :] += own[:, lanes]
                if u >= 12:
                    sheet[side, u - 8 : u - 7, :] += edge[0:1, lanes]
                if u < 4:
                    sheet[side, 64 + u : 65 + u, :] += edge[1:2, lanes]
    left = sheet[0, 4:68]
    right = sheet[1, 4:68]
    lane = lax.broadcasted_iota(jnp.int32, left.shape, 1)
    center = jnp.where(lane < 124, pltpu.roll(left, 124, 1), 0.0)
    center_ref[...] = center + jnp.where(lane >= 4, pltpu.roll(right, 4, 1), 0.0)
    left = left.T[0:4]
    right = right.T[124:128]
    begins = lax.axis_index("yl") == 0
    near_out[...] = jnp.where(begins, right, left)
    far_out[...] = jnp.where(begins, left, right)


def cols_kernel(center_ref, far_ref, near_ref, out_ref):
    begins = lax.axis_index("yl") == 0
    left = jnp.where(begins, far_ref[...], near_ref[...])
    right = jnp.where(begins, near_ref[...], far_ref[...])
    quiet = jnp.zeros((120, 64), f32)
    out_ref[...] = center_ref[...] + jnp.concatenate([left, quiet, right]).T


def swapped(x, axis, by):
    peers = lax.axis_size(axis)
    return lax.ppermute(x, axis, [(i, i ^ by) for i in range(peers)])


def neighbours(x, axis):
    peers = lax.axis_size(axis)
    pairs = [(i, i + 1) for i in range(1, peers - 1, 2)]
    return lax.ppermute(x, axis, pairs + [(target, source) for source, target in pairs])


def cost(products):
    flops = products * 4 * QUERIES * HALF * 256
    return pl.CostEstimate(flops=flops, bytes_accessed=2**20, transcendentals=2 * QUERIES * HALF)


def combined_weights(w_qkv, w_patch, part):
    return call(
        functools.partial(weights_kernel, part),
        jax.ShapeDtypeStruct((512, D), bf16),
        12,
        [pltpu.VMEM((D, D), bf16), pltpu.SemaphoreType.DMA((D // 128,))],
        [WHOLE, ANYWHERE],
        cost_estimate=pl.CostEstimate(flops=2**20, bytes_accessed=2**16, transcendentals=0),
    )(w_patch, w_qkv)


def on_device(queries, key_states, values, saved_out, grad_out, w_qkv, w_patch):
    tokens = pltpu.VMEM((TOK, D), bf16)
    cells = pltpu.VMEM((2, 4, D), bf16)
    packed = (HEADS, 2 * FPAD + 16, TOK)
    dma = pltpu.SemaphoreType.DMA
    send = call(
        pack_kernel,
        jax.ShapeDtypeStruct(packed, bf16),
        None,
        [tokens, tokens, tokens, cells, cells, pltpu.VMEM(packed, bf16), dma((14,)), dma((4,))],
        [ANYWHERE] * 5,
        out_specs=ANYWHERE,
    )(
        queries.reshape(TOK, D),
        grad_out.reshape(TOK, D),
        saved_out.reshape(TOK, D),
        key_states,
        values,
    )
    got = lax.all_to_all(send, HEAD_AXES, 0, 0, tiled=True)
    kv = call(
        keys_kernel,
        jax.ShapeDtypeStruct((2 * DH, 128), bf16),
        4,
        [pltpu.VMEM((HEADS, 16, 128), bf16), dma(())],
        [ANYWHERE],
    )(got)
    came = [swapped(kv, "z", by) for by in (2, 4, 6)]
    even = jnp.stack([kv] + came)
    odd = swapped(even, "z", 1)
    there = swapped(got, "c", 1)
    keys = pltpu.VMEM((HALF, 128), bf16)
    sums = jax.ShapeDtypeStruct((2, HEADS, 8, TOK), f32)
    even_sums = call(even_sums_kernel, sums, 24, [keys], cost_estimate=cost(1))(got, there, even)
    odd, even_sums = lax.optimization_barrier((odd, even_sums))
    mine = call(odd_sums_kernel, sums, 24, [keys], cost_estimate=cost(1))(got, there, odd, even_sums)
    came = swapped(mine, "c", 1)
    scratch = [keys, pltpu.VMEM((128, HALF), bf16), keys]
    scratch += [pltpu.VMEM((HALF, 128), f32)] * 2
    dq = [jax.ShapeDtypeStruct((HEADS, FPAD, TOK), f32)] * 2
    block = (4, 2 * DH, 128)
    sums, dq_here, dq_there, grads = call(
        first_kernel, [sums] + dq + [jax.ShapeDtypeStruct(block, bf16)], 28, scratch, cost_estimate=cost(5)
    )(got, there, odd, mine, came)
    came = swapped(grads, "z", 1)
    edges = [jax.ShapeDtypeStruct((HEADS, 24, TOK), f32)] * 2
    *dq, grads = call(
        second_kernel,
        dq + edges + [jax.ShapeDtypeStruct(block, f32)],
        28,
        scratch,
        cost_estimate=cost(5),
    )(got, there, even, sums, dq_here, dq_there)
    dq, grads, came = lax.optimization_barrier((dq, grads, came))
    dq_here, dq_there, edge_here, edge_there = dq
    dq_there = swapped(dq_there, "c", 1)
    edge_here = swapped(edge_here, "c", 1)
    mine = grads + came.astype(f32)
    mine, w_qkv, w_patch = lax.optimization_barrier((mine, w_qkv, w_patch))
    came = [swapped(mine[n].astype(bf16), "z", 2 * n) for n in (1, 2, 3)]
    weights = [combined_weights(w_qkv, w_patch, part) for part in range(3)]
    came, weights = lax.optimization_barrier((came, weights))
    keys = call(keys_sum_kernel, jax.ShapeDtypeStruct((2 * DH, 128), bf16), 4)(mine[0:1], *came)
    other = swapped(keys, "c", 1)
    send = call(pack_back_kernel, jax.ShapeDtypeStruct((HEADS, 128, TOK), bf16), 16)(
        dq_here, dq_there, edge_there, edge_here, keys, other
    )
    back = lax.all_to_all(send, HEAD_AXES, 0, 0, tiled=True)
    strip = jax.ShapeDtypeStruct((4, 64), f32)
    center, to_near, to_far = call(
        embed_kernel,
        [jax.ShapeDtypeStruct((64, 128), f32), strip, strip],
        28,
        [pltpu.VMEM((D, 2 * TOK), bf16), pltpu.VMEM((2 * D, 128), bf16), pltpu.VMEM((2, 72, 128), f32)],
    )(back, *weights)
    return call(cols_kernel, jax.ShapeDtypeStruct((64, 128), f32), 4)(
        center, neighbours(to_far, COL), swapped(to_near, "yl", 1)
    )


def solution(mesh):
    fine = Mesh(mesh.devices.reshape(2, 4, 2, 8, 2), ("yh", "x", "c", "z", "yl"))
    split = P(BLK, COL, None)
    return jax.shard_map(
        on_device,
        mesh=fine,
        in_specs=(split, split, split, split, split, P(), P()),
        out_specs=P(BLK, COL),
        check_vma=False,
    )
```

```python
import functools
import math

import jax
import jax.numpy as jnp
from jax import lax
from jax.experimental import pallas as pl
from jax.experimental.pallas import tpu as pltpu
from jax.sharding import Mesh, PartitionSpec as P

D = 1152
HEADS = 16
DH = D // HEADS
POOL = 4
SCALE = DH**-0.5
SCALE2 = SCALE * math.log2(math.e)
ROWS, COLS = 8, 16
TOK = ROWS * COLS
CELLS = TOK // POOL**2
EXTENDED = TOK + 2 * COLS
FPAD = 80
QUERIES = 2048
HALF = 512
TILE = 2048
TILES = QUERIES // TILE
PER = TILE // TOK
STEP = 256
HEAD_AXES = ("yh", "x", "yl")
BLK = ("yh", "x", "c")
EVEN = (2, 6, 4)
COL = ("z", "yl")
NT = (((1,), (1,)), ((), ()))
WHOLE = pl.BlockSpec(memory_space=pltpu.VMEM)
ANYWHERE = pl.BlockSpec(memory_space=pl.ANY)
bf16, f32 = jnp.bfloat16, jnp.float32


def call(kernel, out, mib, scratch=(), specs=None, **more):
    if specs is not None:
        more["in_specs"] = specs
    return pl.pallas_call(
        kernel,
        out_shape=out,
        scratch_shapes=scratch,
        compiler_params=pltpu.CompilerParams(vmem_limit_bytes=mib * 2**20 if mib else None),
        **more,
    )


def pack_kernel(
    q_in, g_in, o_in, k_in, v_in, out_ref, q_ref, g_ref, o_ref, k_ref, v_ref, send_ref, sems, out_sems
):
    pairs = [(k_in, k_ref), (v_in, v_ref)]
    quarter = TOK // 4
    for source, target in ((q_in, q_ref), (g_in, g_ref), (o_in, o_ref)):
        for at in range(0, TOK, quarter):
            pairs.append((source.at[at : at + quarter], target.at[at : at + quarter]))
    copies = [pltpu.make_async_copy(*pair, sems.at[n]) for n, pair in enumerate(pairs)]
    for copy in copies:
        copy.start()
    for copy in copies[:6]:
        copy.wait()
    q_t = q_ref[...].astype(f32).T
    keys = jnp.concatenate([k_ref[0].astype(f32), k_ref[1].astype(f32)])
    vals = jnp.concatenate([v_ref[0].astype(f32), v_ref[1].astype(f32)])
    lanes = jnp.zeros((CELLS, 128 - DH), f32)
    for h in range(HEADS):
        part = slice(h * DH, (h + 1) * DH)
        send_ref[h, 0:FPAD, :] = jnp.concatenate([q_t[part], jnp.zeros((8, TOK), f32)]).astype(bf16)
        k_h = jnp.concatenate([keys[:, part], lanes], axis=1)
        v_h = jnp.concatenate([vals[:, part], lanes], axis=1)
        send_ref[h, 2 * FPAD : 2 * FPAD + 16, :] = jnp.concatenate([k_h, v_h]).astype(bf16)
    for copy in copies[6:]:
        copy.wait()
    g_t = g_ref[...].astype(f32).T
    prod = g_t * o_ref[...].astype(f32).T
    row = lax.broadcasted_iota(jnp.int32, (8, TOK), 0)
    outs = []
    for h in range(HEADS):
        part = slice(h * DH, (h + 1) * DH)
        dot = -jnp.sum(prod[part], axis=0, keepdims=True)
        high = dot.astype(bf16).astype(f32)
        mid = (dot - high).astype(bf16).astype(f32)
        low = dot - high - mid
        dots = jnp.where(row == 0, high, jnp.where(row == 1, mid, jnp.where(row == 2, low, 0.0)))
        send_ref[h, FPAD : 2 * FPAD, :] = jnp.concatenate([g_t[part], dots]).astype(bf16)
        if h % 4 == 3:
            heads = slice(h - 3, h + 1)
            copy = pltpu.make_async_copy(send_ref.at[heads], out_ref.at[heads], out_sems.at[h // 4])
            copy.start()
            outs.append(copy)
    for copy in outs:
        copy.wait()


def keys_kernel(got_ref, out_ref, kv_ref, sem):
    copy = pltpu.make_async_copy(got_ref.at[:, 2 * FPAD : 2 * FPAD + 16], kv_ref, sem)
    copy.start()
    copy.wait()
    kv = kv_ref[...].astype(f32).reshape(HEADS, 2, CELLS, 128)
    k_t = kv[:, 0].reshape(128, 128).T
    v_t = kv[:, 1].reshape(128, 128).T
    out_ref[...] = jnp.concatenate([k_t[0:DH], v_t[0:DH]]).astype(bf16)


def load_keys(kv_ref, k_s, kt_s=None, v_s=None):
    lane = lax.broadcasted_iota(jnp.int32, (128, 128), 1)
    pad = jnp.zeros((128 - DH, 128), f32)
    norms = jnp.zeros((1, 128), f32)
    for b in range(4):
        kv = kv_ref[b].astype(f32)
        keys = slice(b * 128, (b + 1) * 128)
        k_t = jnp.concatenate([kv[0:DH], pad])
        norms = jnp.maximum(norms, jnp.sum(k_t * k_t, axis=0, keepdims=True))
        k_s[keys] = k_t.T.astype(bf16)
        if kt_s is not None:
            kt_s[:, keys] = k_t.astype(bf16)
            v = jnp.concatenate([kv[DH:], pad]).T
            v_s[keys] = jnp.where((lane >= DH) & (lane < DH + 3), 1.0, v).astype(bf16)
    return jnp.max(norms)


def tile_of(qg_ref, t, row):
    return jnp.concatenate([qg_ref[PER * t + n, row : row + FPAD] for n in range(PER)], axis=1)


def log_sums(q_t, k_s, norm):
    exact = q_t.astype(f32)
    bound = jnp.sqrt(jnp.sum(exact * exact, axis=0, keepdims=True) * norm) * (SCALE2 * 1.001)

    def scores(rows):
        return jnp.dot(k_s[rows, 0:FPAD], q_t, preferred_element_type=f32) * SCALE2

    total = jnp.zeros((1, TILE), f32)
    for at in range(0, HALF, STEP):
        exps = jnp.exp2(scores(slice(at, at + STEP)) - bound)
        total = total + jnp.sum(exps, axis=0, keepdims=True)

    def again():
        def rows(n):
            return pl.ds(pl.multiple_of(n * 128, 128), 128)

        def largest(n, top):
            return jnp.maximum(top, jnp.max(scores(rows(n)), axis=0, keepdims=True))

        top = lax.fori_loop(0, HALF // 128, largest, jnp.full((1, TILE), -jnp.inf, f32))

        def add(n, total):
            return total + jnp.sum(jnp.exp2(scores(rows(n)) - top), axis=0, keepdims=True)

        return top + jnp.log2(lax.fori_loop(0, HALF // 128, add, jnp.zeros((1, TILE), f32)))

    return lax.cond(jnp.min(total) < 2.0**-90, again, lambda: bound + jnp.log2(total))


def put_sums(out_ref, at, t, sums):
    rows = [sums[:, n * TOK : (n + 1) * TOK] for n in range(PER)]
    out_ref[at, pl.ds(PER * t, PER)] = jnp.concatenate(rows)


def get_sums(sums_ref, at, t):
    rows = sums_ref[at, pl.ds(PER * t, PER)]
    return jnp.concatenate([rows[n : n + 1] for n in range(PER)], axis=1)


def added(one, two):
    top = jnp.maximum(one, two)
    return top + jnp.log2(jnp.exp2(one - top) + jnp.exp2(two - top))


def even_sums_kernel(qg_a, qg_b, kv_ref, out_ref, k_s):
    norm = load_keys(kv_ref, k_s)
    for at, qg_ref in enumerate((qg_a, qg_b)):

        def tile(t, _):
            put_sums(out_ref, at, t, log_sums(tile_of(qg_ref, t, 0), k_s, norm))
            return 0

        lax.fori_loop(0, TILES, tile, 0)


def odd_sums_kernel(qg_a, qg_b, kv_ref, even_ref, out_ref, k_s):
    norm = load_keys(kv_ref, k_s)
    for at, qg_ref in enumerate((qg_a, qg_b)):

        def tile(t, _):
            mine = log_sums(tile_of(qg_ref, t, 0), k_s, norm)
            put_sums(out_ref, at, t, added(mine, get_sums(even_ref, at, t)))
            return 0

        lax.fori_loop(0, TILES, tile, 0)


def gradients(sums_ref, work, k_s, kt_s, v_s, dk_s, dv_s):
    dk_s[...] = jnp.zeros_like(dk_s)
    dv_s[...] = jnp.zeros_like(dv_s)
    for at_core, (qg_ref, put_dq) in enumerate(work):

        def tile(t, _):
            q_t = tile_of(qg_ref, t, 0)
            g_t = tile_of(qg_ref, t, FPAD)
            sums = get_sums(sums_ref, at_core, t)
            dq = jnp.zeros((FPAD, TILE), f32)
            for at in range(0, HALF, STEP):
                b = slice(at, at + STEP)
                scores = jnp.dot(k_s[b, 0:FPAD], q_t, preferred_element_type=f32)
                probs = jnp.exp2(scores * SCALE2 - sums)
                half_probs = probs.astype(bf16)
                shifted = jnp.dot(v_s[b, 0:FPAD], g_t, preferred_element_type=f32)
                ds = (probs * shifted).astype(bf16)
                dk_s[b, 0:FPAD] += lax.dot_general(ds, q_t, NT, preferred_element_type=f32)
                dv_s[b, 0:FPAD] += lax.dot_general(half_probs, g_t, NT, preferred_element_type=f32)
                dq = dq + jnp.dot(kt_s[0:FPAD, b], ds, preferred_element_type=f32)
            for n in range(PER):
                put_dq(PER * t + n, dq[:, n * TOK : (n + 1) * TOK])
            return 0

        lax.fori_loop(0, TILES, tile, 0)


def put_keys(out_ref, dk_s, dv_s):
    dk_t = dk_s[...].T
    dv_t = dv_s[...].T
    for b in range(4):
        keys = slice(b * 128, (b + 1) * 128)
        block = jnp.concatenate([dk_t[0:DH, keys] * SCALE, dv_t[0:DH, keys]])
        out_ref[b] = block.astype(out_ref.dtype)


def first_kernel(
    qg_a, qg_b, kv_ref, mine_ref, came_ref, sums_ref, dq_a, dq_b, out_ref,
    k_s, kt_s, v_s, dk_s, dv_s,
):
    load_keys(kv_ref, k_s, kt_s, v_s)
    for at in (0, 1):
        sums_ref[at] = added(mine_ref[at], came_ref[1 - at])

    def put_a(n, dq):
        dq_a[n] = dq

    def put_b(n, dq):
        dq_b[n] = dq

    gradients(sums_ref, ((qg_a, put_a), (qg_b, put_b)), k_s, kt_s, v_s, dk_s, dv_s)
    put_keys(out_ref, dk_s, dv_s)


def edge_rows(dq):
    lane = lax.broadcasted_iota(jnp.int32, (24, TOK), 1)
    edges = pltpu.roll(dq[0:24], COLS, 1)
    for n in (1, 2):
        rolled = pltpu.roll(dq[24 * n : 24 * (n + 1)], COLS + 32 * n, 1)
        edges = jnp.where(lane < 32 * n, edges, rolled)
    return edges


def second_kernel(
    qg_a, qg_b, kv_ref, sums_ref, in_a, in_b, dq_a, dq_b, edge_a, edge_b, out_ref,
    k_s, kt_s, v_s, dk_s, dv_s,
):
    load_keys(kv_ref, k_s, kt_s, v_s)

    def put_a(n, dq):
        dq = in_a[n] + dq
        dq_a[n] = dq
        edge_a[n] = edge_rows(dq)

    def put_b(n, dq):
        dq = in_b[n] + dq
        dq_b[n] = dq
        edge_b[n] = edge_rows(dq)

    gradients(sums_ref, ((qg_a, put_a), (qg_b, put_b)), k_s, kt_s, v_s, dk_s, dv_s)
    put_keys(out_ref, dk_s, dv_s)


def keys_sum_kernel(mine_ref, came_a, came_b, came_c, out_ref):
    total = mine_ref[0]
    for came in (came_a, came_b, came_c):
        total = total + came[...].astype(f32)
    out_ref[...] = total.astype(bf16)


def beside(x, first):
    none = jnp.zeros_like(x[0:2])
    above = jnp.where(first, jnp.concatenate([none, x[:-2]]), x)
    below = jnp.where(first, x, jnp.concatenate([x[2:], none]))
    return above, below


def pack_back_kernel(dq_ref, came_ref, edge_ref, came_edge_ref, keys_ref, other_ref, send_ref):
    first = lax.axis_index("c") == 0
    dq = (dq_ref[...] + came_ref[...])[:, 0:DH] * SCALE
    above, below = beside((edge_ref[...] + came_edge_ref[...]) * SCALE, first)
    lane = lax.broadcasted_iota(jnp.int32, (HEADS, 24, 128), 2)
    edges = jnp.where(lane % 32 < COLS, above, below)
    lanes = jnp.zeros((128, 128 - DH), f32)
    row = lax.broadcasted_iota(jnp.int32, (HEADS, CELLS, 128), 1)

    def cells(ref, part):
        rows = ref[...].astype(f32)[part * DH : (part + 1) * DH].T
        return jnp.concatenate([rows, lanes], axis=1).reshape(HEADS, CELLS, 128)

    parts = [dq, edges, cells(keys_ref, 0), cells(keys_ref, 1)]
    for part in (0, 1):
        above, below = beside(cells(other_ref, part), first)
        half = CELLS // 2
        parts.append(jnp.where(row < half, pltpu.roll(above, half, 1), pltpu.roll(below, half, 1)))
    send_ref[...] = jnp.concatenate(parts, axis=1).astype(bf16)


def weights_kernel(part, patch_ref, qkv_ref, out_ref, qkv_s, sems):
    step = 128
    copies = []
    for n in range(D // step):
        rows = slice(n * step, (n + 1) * step)
        source = qkv_ref.at[rows, part * D : (part + 1) * D]
        copies.append(pltpu.make_async_copy(source, qkv_s.at[rows], sems.at[n]))
        copies[-1].start()
    for copy in copies:
        copy.wait()
    both = jnp.dot(patch_ref[...], qkv_s[...], preferred_element_type=f32)
    both = both.reshape(16, 2, 8, D)
    both = jnp.concatenate([both[:, 0].reshape(128, D), both[:, 1].reshape(128, D)])
    high = both.astype(bf16)
    out_ref[0:256] = high
    out_ref[256:512] = (both - high.astype(f32)).astype(bf16)


def split(x):
    high = x.astype(bf16)
    return high, (x - high.astype(f32)).astype(bf16)


def iota(shape, dim):
    return lax.broadcasted_iota(jnp.int32, shape, dim)


def one_hot(where, value=1.0):
    return jnp.where(where, value, 0.0).astype(bf16)


def embed_kernel(back_ref, *refs):
    weights, (center_ref, near_out, far_out, joined, pooled, sheet) = refs[:3], refs[3:]
    for h in range(0, HEADS, 2):
        pair = []
        wide = []
        for n in (h, h + 1):
            pair.append(back_ref[n, 0:TOK].astype(f32)[0:DH])
            edges = back_ref[n, 64 : 64 + 32].astype(f32)[DH - 64 :]
            wide += [edges, pltpu.roll(edges, 96, 1), pltpu.roll(edges, 64, 1)]
        rows = slice(h * DH, (h + 2) * DH)
        joined[rows, 0:TOK] = jnp.concatenate(pair).astype(bf16)
        joined[rows, TOK:] = jnp.concatenate(wide).astype(bf16)
    at = DH + 24
    group = iota((DH, 128), 1) // 16
    for h in range(0, HEADS, 4):
        cells = []
        for part in (0, 1):
            for n in range(h, h + 4):
                head = back_ref[n, at:].astype(f32)
                cells += [head[part * CELLS : (part + 1) * CELLS], head[16 + part * CELLS : 16 + (part + 1) * CELLS]]
        cells = jnp.concatenate(cells).T[0:DH]
        for part in (0, 1):
            for n in (0, 2):
                two = [jnp.where(group == 4 * part + k, cells, 0.0) for k in (n, n + 1)]
                rows = part * D + (h + n) * DH
                pooled[rows : rows + 2 * DH] = jnp.concatenate(two).astype(bf16)
    patch = jnp.dot(weights[0][...], joined[...], preferred_element_type=f32)
    patch = patch[0:256] + patch[256:512]
    cells = jnp.dot(weights[1][...], pooled[0:D], preferred_element_type=f32)
    cells = cells + jnp.dot(weights[2][...], pooled[D:], preferred_element_type=f32)
    cells = jnp.concatenate(split(cells[0:256] + cells[256:512]), axis=1)
    cell, token = iota((256, 256), 0) % 16, iota((256, 256), 1)
    mine = token // (POOL * COLS) * 4 + token % COLS // POOL
    beyond = CELLS + (token - TOK) // COLS * 4 + token % COLS // POOL
    holds = (cell == jnp.where(token < TOK, mine, beyond)) & (token < EXTENDED)
    patch = patch + jnp.dot(cells, one_hot(holds, 1.0 / POOL**2), preferred_element_type=f32)
    to, token = iota((EXTENDED, 256), 0), iota((EXTENDED, 256), 1)
    far = to - TOK
    column = jnp.where(to < TOK, to // 8, far // 8 * 4 + far % 8 // 2)
    source = jnp.where(to < TOK, to % 8 * COLS, TOK + far % 2 * COLS) + column
    turned = lax.dot_general(
        one_hot(token == source), jnp.concatenate(split(patch)), NT, preferred_element_type=f32
    ).astype(bf16)
    sheet[...] = jnp.zeros_like(sheet)
    here = iota((EXTENDED, 256), 1) % 128 // 8 == column
    to, at = iota((256, 256), 1), iota((256, 256), 0) % 128
    for pair in range(8):
        tile = one_hot((to // 128 + 2 * pair == at // 8) & (to % 8 == at % 8))
        for side in (0, 1):
            parts = [turned[:, n * 256 + side * 128 : n * 256 + (side + 1) * 128] for n in (0, 1)]
            wide = jnp.dot(jnp.concatenate(parts, axis=1), tile, preferred_element_type=f32)
            wide = jnp.where(here, wide, 0.0)
            own = jnp.sum(wide[0:TOK].reshape(COLS, ROWS, 256), axis=0)
            edge = jnp.sum(wide[TOK:].reshape(4, 8, 256), axis=0)
            edge = edge + pltpu.roll(edge, 4, 0)
            edge = edge + pltpu.roll(edge, 2, 0)
            for k in (0, 1):
                u = 2 * pair + k
                lanes = slice(k * 128, (k + 1) * 128)
                sheet[side, pl.ds(u, ROWS, stride=8), :] += own[:, lanes]
                if u >= 12:
                    sheet[side, u - 8 : u - 7, :] += edge[0:1, lanes]
                if u < 4:
                    sheet[side, 64 + u : 65 + u, :] += edge[1:2, lanes]
    left = sheet[0, 4:68]
    right = sheet[1, 4:68]
    lane = lax.broadcasted_iota(jnp.int32, left.shape, 1)
    center = jnp.where(lane < 124, pltpu.roll(left, 124, 1), 0.0)
    center_ref[...] = center + jnp.where(lane >= 4, pltpu.roll(right, 4, 1), 0.0)
    left = left.T[0:4]
    right = right.T[124:128]
    begins = lax.axis_index("yl") == 0
    near_out[...] = jnp.where(begins, right, left)
    far_out[...] = jnp.where(begins, left, right)


def cols_kernel(center_ref, far_ref, near_ref, out_ref):
    begins = lax.axis_index("yl") == 0
    left = jnp.where(begins, far_ref[...], near_ref[...])
    right = jnp.where(begins, near_ref[...], far_ref[...])
    quiet = jnp.zeros((120, 64), f32)
    out_ref[...] = center_ref[...] + jnp.concatenate([left, quiet, right]).T


def swapped(x, axis, by):
    peers = lax.axis_size(axis)
    return lax.ppermute(x, axis, [(i, i ^ by) for i in range(peers)])


def neighbours(x, axis):
    peers = lax.axis_size(axis)
    pairs = [(i, i + 1) for i in range(1, peers - 1, 2)]
    return lax.ppermute(x, axis, pairs + [(target, source) for source, target in pairs])


def cost(products):
    flops = products * 4 * QUERIES * HALF * 256
    return pl.CostEstimate(flops=flops, bytes_accessed=2**20, transcendentals=2 * QUERIES * HALF)


def combined_weights(w_qkv, w_patch, part):
    return call(
        functools.partial(weights_kernel, part),
        jax.ShapeDtypeStruct((512, D), bf16),
        12,
        [pltpu.VMEM((D, D), bf16), pltpu.SemaphoreType.DMA((D // 128,))],
        [WHOLE, ANYWHERE],
        cost_estimate=pl.CostEstimate(flops=2**20, bytes_accessed=2**16, transcendentals=0),
    )(w_patch, w_qkv)


def on_device(queries, key_states, values, saved_out, grad_out, w_qkv, w_patch):
    tokens = pltpu.VMEM((TOK, D), bf16)
    cells = pltpu.VMEM((2, 4, D), bf16)
    packed = (HEADS, 2 * FPAD + 16, TOK)
    dma = pltpu.SemaphoreType.DMA
    send = call(
        pack_kernel,
        jax.ShapeDtypeStruct(packed, bf16),
        None,
        [tokens, tokens, tokens, cells, cells, pltpu.VMEM(packed, bf16), dma((14,)), dma((4,))],
        [ANYWHERE] * 5,
        out_specs=ANYWHERE,
    )(
        queries.reshape(TOK, D),
        grad_out.reshape(TOK, D),
        saved_out.reshape(TOK, D),
        key_states,
        values,
    )
    got = lax.all_to_all(send, HEAD_AXES, 0, 0, tiled=True)
    kv = call(
        keys_kernel,
        jax.ShapeDtypeStruct((2 * DH, 128), bf16),
        4,
        [pltpu.VMEM((HEADS, 16, 128), bf16), dma(())],
        [ANYWHERE],
    )(got)
    came = [swapped(kv, "z", by) for by in EVEN]
    even = jnp.stack([kv] + came)
    odd = swapped(even, "z", 1)
    there = swapped(got, "c", 1)
    keys = pltpu.VMEM((HALF, 128), bf16)
    sums = jax.ShapeDtypeStruct((2, HEADS, TOK), f32)
    even_sums = call(even_sums_kernel, sums, 24, [keys], cost_estimate=cost(1))(got, there, even)
    odd, even_sums = lax.optimization_barrier((odd, even_sums))
    mine = call(odd_sums_kernel, sums, 24, [keys], cost_estimate=cost(1))(got, there, odd, even_sums)
    came = swapped(mine, "c", 1)
    scratch = [keys, pltpu.VMEM((128, HALF), bf16), keys]
    scratch += [pltpu.VMEM((HALF, 128), f32)] * 2
    dq = [jax.ShapeDtypeStruct((HEADS, FPAD, TOK), f32)] * 2
    block = (4, 2 * DH, 128)
    sums, dq_here, dq_there, grads = call(
        first_kernel, [sums] + dq + [jax.ShapeDtypeStruct(block, bf16)], 28, scratch, cost_estimate=cost(5)
    )(got, there, odd, mine, came)
    came = swapped(grads, "z", 1)
    edges = [jax.ShapeDtypeStruct((HEADS, 24, TOK), f32)] * 2
    *dq, grads = call(
        second_kernel,
        dq + edges + [jax.ShapeDtypeStruct(block, f32)],
        28,
        scratch,
        cost_estimate=cost(5),
    )(got, there, even, sums, dq_here, dq_there)
    dq, grads, came = lax.optimization_barrier((dq, grads, came))
    dq_here, dq_there, edge_here, edge_there = dq
    dq_there = swapped(dq_there, "c", 1)
    edge_here = swapped(edge_here, "c", 1)
    mine = grads + came.astype(f32)
    mine, w_qkv, w_patch = lax.optimization_barrier((mine, w_qkv, w_patch))
    came = [swapped(mine[n + 1].astype(bf16), "z", by) for n, by in enumerate(EVEN)]
    weights = [combined_weights(w_qkv, w_patch, part) for part in range(3)]
    came, weights = lax.optimization_barrier((came, weights))
    keys = call(keys_sum_kernel, jax.ShapeDtypeStruct((2 * DH, 128), bf16), 4)(mine[0:1], *came)
    other = swapped(keys, "c", 1)
    send = call(pack_back_kernel, jax.ShapeDtypeStruct((HEADS, 128, TOK), bf16), 16)(
        dq_here, dq_there, edge_there, edge_here, keys, other
    )
    back = lax.all_to_all(send, HEAD_AXES, 0, 0, tiled=True)
    strip = jax.ShapeDtypeStruct((4, 64), f32)
    center, to_near, to_far = call(
        embed_kernel,
        [jax.ShapeDtypeStruct((64, 128), f32), strip, strip],
        28,
        [pltpu.VMEM((D, 2 * TOK), bf16), pltpu.VMEM((2 * D, 128), bf16), pltpu.VMEM((2, 72, 128), f32)],
    )(back, *weights)
    return call(cols_kernel, jax.ShapeDtypeStruct((64, 128), f32), 4)(
        center, neighbours(to_far, COL), swapped(to_near, "yl", 1)
    )


def solution(mesh):
    fine = Mesh(mesh.devices.reshape(2, 4, 2, 8, 2), ("yh", "x", "c", "z", "yl"))
    split = P(BLK, COL, None)
    return jax.shard_map(
        on_device,
        mesh=fine,
        in_specs=(split, split, split, split, split, P(), P()),
        out_specs=P(BLK, COL),
        check_vma=False,
    )
```

```python
import functools
import math

import jax
import jax.numpy as jnp
from jax import lax
from jax.experimental import pallas as pl
from jax.experimental.pallas import tpu as pltpu
from jax.sharding import Mesh, PartitionSpec as P

D = 1152
HEADS = 16
DH = D // HEADS
POOL = 4
SCALE = DH**-0.5
SCALE2 = SCALE * math.log2(math.e)
ROWS, COLS = 8, 16
TOK = ROWS * COLS
CELLS = TOK // POOL**2
EXTENDED = TOK + 2 * COLS
FPAD = 80
QUERIES = 2048
HALF = 512
TILE = 2 * QUERIES
STEP = 256
HEAD_AXES = ("yh", "x", "yl")
BLK = ("yh", "x", "c")
EVEN = (2, 6, 4)
COL = ("z", "yl")
NT = (((1,), (1,)), ((), ()))
SMALL = pl.CostEstimate(flops=2**20, bytes_accessed=2**16, transcendentals=0)
WHOLE = pl.BlockSpec(memory_space=pltpu.VMEM)
ANYWHERE = pl.BlockSpec(memory_space=pl.ANY)
bf16, f32 = jnp.bfloat16, jnp.float32


def call(kernel, out, mib, scratch=(), specs=None, **more):
    if specs is not None:
        more["in_specs"] = specs
    return pl.pallas_call(
        kernel,
        out_shape=out,
        scratch_shapes=scratch,
        compiler_params=pltpu.CompilerParams(vmem_limit_bytes=mib * 2**20 if mib else None),
        **more,
    )


def pack_kernel(
    q_in, g_in, o_in, k_in, v_in, out_ref, q_ref, g_ref, o_ref, k_ref, v_ref, send_ref, sems, out_sems
):
    pairs = [(k_in, k_ref), (v_in, v_ref)]
    quarter = TOK // 4
    for source, target in ((q_in, q_ref), (g_in, g_ref), (o_in, o_ref)):
        for at in range(0, TOK, quarter):
            pairs.append((source.at[at : at + quarter], target.at[at : at + quarter]))
    copies = [pltpu.make_async_copy(*pair, sems.at[n]) for n, pair in enumerate(pairs)]
    for copy in copies:
        copy.start()
    for copy in copies[:6]:
        copy.wait()
    q_t = q_ref[...].astype(f32).T
    keys = jnp.concatenate([k_ref[0].astype(f32), k_ref[1].astype(f32)])
    vals = jnp.concatenate([v_ref[0].astype(f32), v_ref[1].astype(f32)])
    lanes = jnp.zeros((CELLS, 128 - DH), f32)
    for h in range(HEADS):
        part = slice(h * DH, (h + 1) * DH)
        send_ref[h, 0:FPAD, :] = jnp.concatenate([q_t[part], jnp.zeros((8, TOK), f32)]).astype(bf16)
        k_h = jnp.concatenate([keys[:, part], lanes], axis=1)
        v_h = jnp.concatenate([vals[:, part], lanes], axis=1)
        send_ref[h, 2 * FPAD : 2 * FPAD + 16, :] = jnp.concatenate([k_h, v_h]).astype(bf16)
    for copy in copies[6:]:
        copy.wait()
    g_t = g_ref[...].astype(f32).T
    prod = g_t * o_ref[...].astype(f32).T
    row = lax.broadcasted_iota(jnp.int32, (8, TOK), 0)
    outs = []
    for h in range(HEADS):
        part = slice(h * DH, (h + 1) * DH)
        dot = -jnp.sum(prod[part], axis=0, keepdims=True)
        high = dot.astype(bf16).astype(f32)
        mid = (dot - high).astype(bf16).astype(f32)
        low = dot - high - mid
        dots = jnp.where(row == 0, high, jnp.where(row == 1, mid, jnp.where(row == 2, low, 0.0)))
        send_ref[h, FPAD : 2 * FPAD, :] = jnp.concatenate([g_t[part], dots]).astype(bf16)
        if h % 4 == 3:
            heads = slice(h - 3, h + 1)
            copy = pltpu.make_async_copy(send_ref.at[heads], out_ref.at[heads], out_sems.at[h // 4])
            copy.start()
            outs.append(copy)
    for copy in outs:
        copy.wait()


def keys_kernel(got_ref, out_ref, kv_ref, sem):
    copy = pltpu.make_async_copy(got_ref.at[:, 2 * FPAD : 2 * FPAD + 16], kv_ref, sem)
    copy.start()
    copy.wait()
    kv = kv_ref[...].astype(f32).reshape(HEADS, 2, CELLS, 128)
    k_t = kv[:, 0].reshape(128, 128).T
    v_t = kv[:, 1].reshape(128, 128).T
    out_ref[...] = jnp.concatenate([k_t[0:DH], v_t[0:DH]]).astype(bf16)


def load_keys(kv_ref, k_s, kt_s=None, v_s=None):
    lane = lax.broadcasted_iota(jnp.int32, (128, 128), 1)
    pad = jnp.zeros((128 - DH, 128), f32)
    norms = jnp.zeros((1, 128), f32)
    for b in range(4):
        kv = kv_ref[b].astype(f32)
        keys = slice(b * 128, (b + 1) * 128)
        k_t = jnp.concatenate([kv[0:DH], pad])
        norms = jnp.maximum(norms, jnp.sum(k_t * k_t, axis=0, keepdims=True))
        k_s[keys] = k_t.T.astype(bf16)
        if kt_s is not None:
            kt_s[:, keys] = k_t.astype(bf16)
            v = jnp.concatenate([kv[DH:], pad]).T
            v_s[keys] = jnp.where((lane >= DH) & (lane < DH + 3), 1.0, v).astype(bf16)
    return jnp.max(norms)


def tile_of(qg_refs, row):
    blocks = [qg_ref[n, row : row + FPAD] for qg_ref in qg_refs for n in range(HEADS)]
    return jnp.concatenate(blocks, axis=1)


def log_sums(q_t, k_s, norm):
    exact = q_t.astype(f32)
    bound = jnp.sqrt(jnp.sum(exact * exact, axis=0, keepdims=True) * norm) * (SCALE2 * 1.001)

    def scores(rows):
        return jnp.dot(k_s[rows, 0:FPAD], q_t, preferred_element_type=f32) * SCALE2

    total = jnp.zeros((1, TILE), f32)
    for at in range(0, HALF, STEP):
        exps = jnp.exp2(scores(slice(at, at + STEP)) - bound)
        total = total + jnp.sum(exps, axis=0, keepdims=True)

    def again():
        def rows(n):
            return pl.ds(pl.multiple_of(n * 128, 128), 128)

        def largest(n, top):
            return jnp.maximum(top, jnp.max(scores(rows(n)), axis=0, keepdims=True))

        top = lax.fori_loop(0, HALF // 128, largest, jnp.full((1, TILE), -jnp.inf, f32))

        def add(n, total):
            return total + jnp.sum(jnp.exp2(scores(rows(n)) - top), axis=0, keepdims=True)

        return top + jnp.log2(lax.fori_loop(0, HALF // 128, add, jnp.zeros((1, TILE), f32)))

    return lax.cond(jnp.min(total) < 2.0**-90, again, lambda: bound + jnp.log2(total))


def put_sums(out_ref, sums):
    rows = [sums[:, n * TOK : (n + 1) * TOK] for n in range(2 * HEADS)]
    out_ref[...] = jnp.concatenate(rows).reshape(2, HEADS, TOK)


def get_sums(sums_ref):
    rows = sums_ref[...].reshape(2 * HEADS, TOK)
    return jnp.concatenate([rows[n : n + 1] for n in range(2 * HEADS)], axis=1)


def added(one, two):
    top = jnp.maximum(one, two)
    return top + jnp.log2(jnp.exp2(one - top) + jnp.exp2(two - top))


def even_sums_kernel(qg_a, qg_b, kv_ref, out_ref, k_s):
    norm = load_keys(kv_ref, k_s)
    put_sums(out_ref, log_sums(tile_of((qg_a, qg_b), 0), k_s, norm))


def odd_sums_kernel(qg_a, qg_b, kv_ref, even_ref, out_ref, k_s):
    norm = load_keys(kv_ref, k_s)
    mine = log_sums(tile_of((qg_a, qg_b), 0), k_s, norm)
    put_sums(out_ref, added(mine, get_sums(even_ref)))


def gradients(sums_ref, qg_refs, put_dq, k_s, kt_s, v_s, dk_s, dv_s):
    q_t = tile_of(qg_refs, 0)
    g_t = tile_of(qg_refs, FPAD)
    sums = get_sums(sums_ref)
    dq = jnp.zeros((FPAD, TILE), f32)
    for at in range(0, HALF, STEP):
        b = slice(at, at + STEP)
        scores = jnp.dot(k_s[b, 0:FPAD], q_t, preferred_element_type=f32)
        probs = jnp.exp2(scores * SCALE2 - sums)
        half_probs = probs.astype(bf16)
        shifted = jnp.dot(v_s[b, 0:FPAD], g_t, preferred_element_type=f32)
        ds = (probs * shifted).astype(bf16)
        dk_s[b, 0:FPAD] = lax.dot_general(ds, q_t, NT, preferred_element_type=f32)
        dv_s[b, 0:FPAD] = lax.dot_general(half_probs, g_t, NT, preferred_element_type=f32)
        dq = dq + jnp.dot(kt_s[0:FPAD, b], ds, preferred_element_type=f32)
    for n in range(2 * HEADS):
        put_dq(n // HEADS, n % HEADS, dq[:, n * TOK : (n + 1) * TOK])


def put_keys(out_ref, dk_s, dv_s):
    dk_t = dk_s[...].T
    dv_t = dv_s[...].T
    for b in range(4):
        keys = slice(b * 128, (b + 1) * 128)
        block = jnp.concatenate([dk_t[0:DH, keys] * SCALE, dv_t[0:DH, keys]])
        out_ref[b] = block.astype(out_ref.dtype)


def first_kernel(
    qg_a, qg_b, kv_ref, mine_ref, came_ref, sums_ref, dq_a, dq_b, out_ref,
    k_s, kt_s, v_s, dk_s, dv_s,
):
    load_keys(kv_ref, k_s, kt_s, v_s)
    for at in (0, 1):
        sums_ref[at] = added(mine_ref[at], came_ref[1 - at])

    def put_dq(at, n, dq):
        (dq_a, dq_b)[at][n] = dq

    gradients(sums_ref, (qg_a, qg_b), put_dq, k_s, kt_s, v_s, dk_s, dv_s)
    put_keys(out_ref, dk_s, dv_s)


def edge_rows(dq):
    lane = lax.broadcasted_iota(jnp.int32, (24, TOK), 1)
    edges = pltpu.roll(dq[0:24], COLS, 1)
    for n in (1, 2):
        rolled = pltpu.roll(dq[24 * n : 24 * (n + 1)], COLS + 32 * n, 1)
        edges = jnp.where(lane < 32 * n, edges, rolled)
    return edges


def second_kernel(
    qg_a, qg_b, kv_ref, sums_ref, in_a, in_b, dq_a, dq_b, edge_a, edge_b, out_ref,
    k_s, kt_s, v_s, dk_s, dv_s,
):
    load_keys(kv_ref, k_s, kt_s, v_s)

    def put_dq(at, n, dq):
        dq = (in_a, in_b)[at][n] + dq
        (dq_a, dq_b)[at][n] = dq
        (edge_a, edge_b)[at][n] = edge_rows(dq)

    gradients(sums_ref, (qg_a, qg_b), put_dq, k_s, kt_s, v_s, dk_s, dv_s)
    put_keys(out_ref, dk_s, dv_s)


def keys_sum_kernel(mine_ref, came_a, came_b, came_c, out_ref):
    total = mine_ref[0]
    for came in (came_a, came_b, came_c):
        total = total + came[...].astype(f32)
    out_ref[...] = total.astype(bf16)


def beside(x, first):
    none = jnp.zeros_like(x[0:2])
    above = jnp.where(first, jnp.concatenate([none, x[:-2]]), x)
    below = jnp.where(first, x, jnp.concatenate([x[2:], none]))
    return above, below


def pack_back_kernel(dq_ref, came_ref, edge_ref, came_edge_ref, keys_ref, other_ref, send_ref):
    first = lax.axis_index("c") == 0
    dq = (dq_ref[...] + came_ref[...])[:, 0:DH] * SCALE
    above, below = beside((edge_ref[...] + came_edge_ref[...]) * SCALE, first)
    lane = lax.broadcasted_iota(jnp.int32, (HEADS, 24, 128), 2)
    edges = jnp.where(lane % 32 < COLS, above, below)
    lanes = jnp.zeros((128, 128 - DH), f32)
    row = lax.broadcasted_iota(jnp.int32, (HEADS, CELLS, 128), 1)

    def cells(ref, part):
        rows = ref[...].astype(f32)[part * DH : (part + 1) * DH].T
        return jnp.concatenate([rows, lanes], axis=1).reshape(HEADS, CELLS, 128)

    parts = [dq, edges, cells(keys_ref, 0), cells(keys_ref, 1)]
    for part in (0, 1):
        above, below = beside(cells(other_ref, part), first)
        half = CELLS // 2
        parts.append(jnp.where(row < half, pltpu.roll(above, half, 1), pltpu.roll(below, half, 1)))
    send_ref[...] = jnp.concatenate(parts, axis=1).astype(bf16)


def weights_kernel(part, patch_ref, qkv_ref, out_ref, qkv_s, sems):
    step = 128
    copies = []
    for n in range(D // step):
        rows = slice(n * step, (n + 1) * step)
        source = qkv_ref.at[rows, part * D : (part + 1) * D]
        copies.append(pltpu.make_async_copy(source, qkv_s.at[rows], sems.at[n]))
        copies[-1].start()
    for copy in copies:
        copy.wait()
    both = jnp.dot(patch_ref[...], qkv_s[...], preferred_element_type=f32)
    both = both.reshape(16, 2, 8, D)
    both = jnp.concatenate([both[:, 0].reshape(128, D), both[:, 1].reshape(128, D)])
    high = both.astype(bf16)
    out_ref[0:256] = high
    out_ref[256:512] = (both - high.astype(f32)).astype(bf16)


def split(x):
    high = x.astype(bf16)
    return high, (x - high.astype(f32)).astype(bf16)


def iota(shape, dim):
    return lax.broadcasted_iota(jnp.int32, shape, dim)


def one_hot(where, value=1.0):
    return jnp.where(where, value, 0.0).astype(bf16)


def embed_kernel(back_ref, *refs):
    weights, (turned_ref, near_out, far_out, joined, pooled, sheet) = refs[:3], refs[3:]
    for h in range(0, HEADS, 2):
        pair = []
        wide = []
        for n in (h, h + 1):
            pair.append(back_ref[n, 0:TOK].astype(f32)[0:DH])
            edges = back_ref[n, 64 : 64 + 32].astype(f32)[DH - 64 :]
            wide += [edges, pltpu.roll(edges, 96, 1), pltpu.roll(edges, 64, 1)]
        rows = slice(h * DH, (h + 2) * DH)
        joined[rows, 0:TOK] = jnp.concatenate(pair).astype(bf16)
        joined[rows, TOK:] = jnp.concatenate(wide).astype(bf16)
    at = DH + 24
    group = iota((DH, 128), 1) // 16
    for h in range(0, HEADS, 4):
        cells = []
        for part in (0, 1):
            for n in range(h, h + 4):
                head = back_ref[n, at:].astype(f32)
                cells += [head[part * CELLS : (part + 1) * CELLS], head[16 + part * CELLS : 16 + (part + 1) * CELLS]]
        cells = jnp.concatenate(cells).T[0:DH]
        for part in (0, 1):
            for n in (0, 2):
                two = [jnp.where(group == 4 * part + k, cells, 0.0) for k in (n, n + 1)]
                rows = part * D + (h + n) * DH
                pooled[rows : rows + 2 * DH] = jnp.concatenate(two).astype(bf16)
    patch = jnp.dot(weights[0][...], joined[...], preferred_element_type=f32)
    patch = patch[0:256] + patch[256:512]
    cells = jnp.dot(weights[1][...], pooled[0:D], preferred_element_type=f32)
    cells = cells + jnp.dot(weights[2][...], pooled[D:], preferred_element_type=f32)
    cells = jnp.concatenate(split(cells[0:256] + cells[256:512]), axis=1)
    cell, token = iota((256, 256), 0) % 16, iota((256, 256), 1)
    mine = token // (POOL * COLS) * 4 + token % COLS // POOL
    beyond = CELLS + (token - TOK) // COLS * 4 + token % COLS // POOL
    holds = (cell == jnp.where(token < TOK, mine, beyond)) & (token < EXTENDED)
    patch = patch + jnp.dot(cells, one_hot(holds, 1.0 / POOL**2), preferred_element_type=f32)
    to, token = iota((EXTENDED, 256), 0), iota((EXTENDED, 256), 1)
    source = jnp.where(to < TOK, to % 8 * COLS, TOK + to % 2 * COLS) + column_of(to)
    turned = lax.dot_general(
        one_hot(token == source), jnp.concatenate(split(patch)), NT, preferred_element_type=f32
    )
    turned_ref[...] = turned.astype(bf16)
    whole = turned[:, 0:256] + turned[:, 256:512]
    left, right = whole[:, 0:128], whole[:, 128:256]
    lane = iota((8, 128), 1)
    own = jnp.where(lane % 8 < 4, left[0:ROWS], right[TOK - ROWS : TOK])
    beyond = jnp.where(lane % 8 < 4, left[TOK : TOK + 8], pltpu.roll(right[EXTENDED - 8 :], 2, 0))
    sheet[...] = jnp.zeros_like(sheet)
    for u in range(16):
        sheet[pl.ds(u, ROWS, stride=8), :] += pltpu.roll(own, (128 - 8 * u) % 128, 1)
        if u >= 12:
            sheet[u - 8 : u - 7, :] += pltpu.roll(beyond, 128 - 8 * u, 1)[0:1]
        if u < 4:
            sheet[64 + u : 65 + u, :] += pltpu.roll(beyond, (128 - 8 * u) % 128, 1)[1:2]
    edges = sheet[4:68].T
    begins = lax.axis_index("yl") == 0
    near_out[...] = jnp.where(begins, edges[4:8], edges[0:4])
    far_out[...] = jnp.where(begins, edges[0:4], edges[4:8])


def column_of(row):
    far = row - TOK
    return jnp.where(row < TOK, row // 8, far // 8 * 4 + far % 8 // 2)


def fold_kernel(turned_ref, center_ref, sheet):
    turned = turned_ref[...]
    sheet[...] = jnp.zeros_like(sheet)
    here = iota((EXTENDED, 256), 1) % 128 // 8 == column_of(iota((EXTENDED, 256), 0))
    to, at = iota((256, 256), 1), iota((256, 256), 0) % 128
    for pair in range(8):
        tile = one_hot((to // 128 + 2 * pair == at // 8) & (to % 8 == at % 8))
        for side in (0, 1):
            parts = [turned[:, n * 256 + side * 128 : n * 256 + (side + 1) * 128] for n in (0, 1)]
            wide = jnp.dot(jnp.concatenate(parts, axis=1), tile, preferred_element_type=f32)
            wide = jnp.where(here, wide, 0.0)
            own = jnp.sum(wide[0:TOK].reshape(COLS, ROWS, 256), axis=0)
            edge = jnp.sum(wide[TOK:].reshape(4, 8, 256), axis=0)
            edge = edge + pltpu.roll(edge, 4, 0)
            edge = edge + pltpu.roll(edge, 2, 0)
            for k in (0, 1):
                u = 2 * pair + k
                lanes = slice(k * 128, (k + 1) * 128)
                sheet[side, pl.ds(u, ROWS, stride=8), :] += own[:, lanes]
                if u >= 12:
                    sheet[side, u - 8 : u - 7, :] += edge[0:1, lanes]
                if u < 4:
                    sheet[side, 64 + u : 65 + u, :] += edge[1:2, lanes]
    left = sheet[0, 4:68]
    right = sheet[1, 4:68]
    lane = lax.broadcasted_iota(jnp.int32, left.shape, 1)
    center = jnp.where(lane < 124, pltpu.roll(left, 124, 1), 0.0)
    center_ref[...] = center + jnp.where(lane >= 4, pltpu.roll(right, 4, 1), 0.0)


def cols_kernel(center_ref, far_ref, near_ref, out_ref):
    begins = lax.axis_index("yl") == 0
    left = jnp.where(begins, far_ref[...], near_ref[...])
    right = jnp.where(begins, near_ref[...], far_ref[...])
    quiet = jnp.zeros((120, 64), f32)
    out_ref[...] = center_ref[...] + jnp.concatenate([left, quiet, right]).T


def swapped(x, axis, by):
    peers = lax.axis_size(axis)
    return lax.ppermute(x, axis, [(i, i ^ by) for i in range(peers)])


def neighbours(x, axis):
    peers = lax.axis_size(axis)
    pairs = [(i, i + 1) for i in range(1, peers - 1, 2)]
    return lax.ppermute(x, axis, pairs + [(target, source) for source, target in pairs])


def cost(products):
    flops = products * 4 * QUERIES * HALF * 256
    return pl.CostEstimate(flops=flops, bytes_accessed=2**20, transcendentals=2 * QUERIES * HALF)


def combined_weights(w_qkv, w_patch, part):
    return call(
        functools.partial(weights_kernel, part),
        jax.ShapeDtypeStruct((512, D), bf16),
        12,
        [pltpu.VMEM((D, D), bf16), pltpu.SemaphoreType.DMA((D // 128,))],
        [WHOLE, ANYWHERE],
        cost_estimate=SMALL,
    )(w_patch, w_qkv)


def on_device(queries, key_states, values, saved_out, grad_out, w_qkv, w_patch):
    tokens = pltpu.VMEM((TOK, D), bf16)
    cells = pltpu.VMEM((2, 4, D), bf16)
    packed = (HEADS, 2 * FPAD + 16, TOK)
    dma = pltpu.SemaphoreType.DMA
    send = call(
        pack_kernel,
        jax.ShapeDtypeStruct(packed, bf16),
        None,
        [tokens, tokens, tokens, cells, cells, pltpu.VMEM(packed, bf16), dma((14,)), dma((4,))],
        [ANYWHERE] * 5,
        out_specs=ANYWHERE,
    )(
        queries.reshape(TOK, D),
        grad_out.reshape(TOK, D),
        saved_out.reshape(TOK, D),
        key_states,
        values,
    )
    got = lax.all_to_all(send, HEAD_AXES, 0, 0, tiled=True)
    kv = call(
        keys_kernel,
        jax.ShapeDtypeStruct((2 * DH, 128), bf16),
        4,
        [pltpu.VMEM((HEADS, 16, 128), bf16), dma(())],
        [ANYWHERE],
    )(got)
    came = [swapped(kv, "z", by) for by in EVEN]
    even = jnp.stack([kv] + came)
    odd = swapped(even, "z", 1)
    there = swapped(got, "c", 1)
    keys = pltpu.VMEM((HALF, 128), bf16)
    sums = jax.ShapeDtypeStruct((2, HEADS, TOK), f32)
    even_sums = call(even_sums_kernel, sums, 24, [keys], cost_estimate=cost(1))(got, there, even)
    odd, even_sums = lax.optimization_barrier((odd, even_sums))
    mine = call(odd_sums_kernel, sums, 24, [keys], cost_estimate=cost(1))(got, there, odd, even_sums)
    came = swapped(mine, "c", 1)
    scratch = [keys, pltpu.VMEM((128, HALF), bf16), keys]
    scratch += [pltpu.VMEM((HALF, 128), f32)] * 2
    dq = [jax.ShapeDtypeStruct((HEADS, FPAD, TOK), f32)] * 2
    block = (4, 2 * DH, 128)
    sums, dq_here, dq_there, grads = call(
        first_kernel, [sums] + dq + [jax.ShapeDtypeStruct(block, bf16)], 32, scratch, cost_estimate=cost(5)
    )(got, there, odd, mine, came)
    came = swapped(grads, "z", 1)
    edges = [jax.ShapeDtypeStruct((HEADS, 24, TOK), f32)] * 2
    *dq, grads = call(
        second_kernel,
        dq + edges + [jax.ShapeDtypeStruct(block, f32)],
        32,
        scratch,
        cost_estimate=cost(5),
    )(got, there, even, sums, dq_here, dq_there)
    dq, grads, came = lax.optimization_barrier((dq, grads, came))
    dq_here, dq_there, edge_here, edge_there = dq
    dq_there = swapped(dq_there, "c", 1)
    edge_here = swapped(edge_here, "c", 1)
    mine = grads + came.astype(f32)
    mine, w_qkv, w_patch = lax.optimization_barrier((mine, w_qkv, w_patch))
    came = [swapped(mine[n + 1].astype(bf16), "z", by) for n, by in enumerate(EVEN)]
    weights = [combined_weights(w_qkv, w_patch, part) for part in range(3)]
    came, weights = lax.optimization_barrier((came, weights))
    keys = call(keys_sum_kernel, jax.ShapeDtypeStruct((2 * DH, 128), bf16), 4)(mine[0:1], *came)
    other = swapped(keys, "c", 1)
    send = call(pack_back_kernel, jax.ShapeDtypeStruct((HEADS, 128, TOK), bf16), 16)(
        dq_here, dq_there, edge_there, edge_here, keys, other
    )
    back = lax.all_to_all(send, HEAD_AXES, 0, 0, tiled=True)
    strip = jax.ShapeDtypeStruct((4, 64), f32)
    turned, to_near, to_far = call(
        embed_kernel,
        [jax.ShapeDtypeStruct((EXTENDED, 512), bf16), strip, strip],
        28,
        [pltpu.VMEM((D, 2 * TOK), bf16), pltpu.VMEM((2 * D, 128), bf16), pltpu.VMEM((72, 128), f32)],
    )(back, *weights)
    far, near = neighbours(to_far, COL), swapped(to_near, "yl", 1)
    center = call(
        fold_kernel,
        jax.ShapeDtypeStruct((64, 128), f32),
        8,
        [pltpu.VMEM((2, 72, 128), f32)],
        cost_estimate=SMALL,
    )(turned)
    far, near, center = lax.optimization_barrier((far, near, center))
    return call(cols_kernel, jax.ShapeDtypeStruct((64, 128), f32), 4)(center, far, near)


def solution(mesh):
    fine = Mesh(mesh.devices.reshape(2, 4, 2, 8, 2), ("yh", "x", "c", "z", "yl"))
    split = P(BLK, COL, None)
    return jax.shard_map(
        on_device,
        mesh=fine,
        in_specs=(split, split, split, split, split, P(), P()),
        out_specs=P(BLK, COL),
        check_vma=False,
    )
```

```python
import math

import jax
import jax.numpy as jnp
from jax import lax
from jax.experimental import pallas as pl
from jax.experimental.pallas import tpu as pltpu
from jax.sharding import Mesh, PartitionSpec as P

D = 1152
HEADS = 16
DH = D // HEADS
POOL = 4
SCALE = DH**-0.5
SCALE2 = SCALE * math.log2(math.e)
ROWS, COLS = 8, 16
TOK = ROWS * COLS
CELLS = TOK // POOL**2
EXTENDED = TOK + 2 * COLS
FPAD = 80
QUERIES = 2048
HALF = 512
TILE = 2 * QUERIES
STEP = 256
HEAD_AXES = ("yh", "x", "yl")
BLK = ("yh", "x", "c")
EVEN = (2, 6, 4)
COL = ("z", "yl")
NT = (((1,), (1,)), ((), ()))
SMALL = pl.CostEstimate(flops=2**20, bytes_accessed=2**16, transcendentals=0)
WHOLE = pl.BlockSpec(memory_space=pltpu.VMEM)
ANYWHERE = pl.BlockSpec(memory_space=pl.ANY)
bf16, f32 = jnp.bfloat16, jnp.float32


def call(kernel, out, mib, scratch=(), specs=None, **more):
    if specs is not None:
        more["in_specs"] = specs
    return pl.pallas_call(
        kernel,
        out_shape=out,
        scratch_shapes=scratch,
        compiler_params=pltpu.CompilerParams(vmem_limit_bytes=mib * 2**20 if mib else None),
        **more,
    )


def pack_kernel(
    q_in, g_in, o_in, k_in, v_in, out_ref, q_ref, g_ref, o_ref, k_ref, v_ref, send_ref, sems, out_sems
):
    pairs = [(k_in, k_ref), (v_in, v_ref)]
    quarter = TOK // 4
    for source, target in ((q_in, q_ref), (g_in, g_ref), (o_in, o_ref)):
        for at in range(0, TOK, quarter):
            pairs.append((source.at[at : at + quarter], target.at[at : at + quarter]))
    copies = [pltpu.make_async_copy(*pair, sems.at[n]) for n, pair in enumerate(pairs)]
    for copy in copies:
        copy.start()
    for copy in copies[:6]:
        copy.wait()
    q_t = q_ref[...].astype(f32).T
    keys = jnp.concatenate([k_ref[0].astype(f32), k_ref[1].astype(f32)])
    vals = jnp.concatenate([v_ref[0].astype(f32), v_ref[1].astype(f32)])
    lanes = jnp.zeros((CELLS, 128 - DH), f32)
    for h in range(HEADS):
        part = slice(h * DH, (h + 1) * DH)
        send_ref[h, 0:FPAD, :] = jnp.concatenate([q_t[part], jnp.zeros((8, TOK), f32)]).astype(bf16)
        k_h = jnp.concatenate([keys[:, part], lanes], axis=1)
        v_h = jnp.concatenate([vals[:, part], lanes], axis=1)
        send_ref[h, 2 * FPAD : 2 * FPAD + 16, :] = jnp.concatenate([k_h, v_h]).astype(bf16)
    for copy in copies[6:]:
        copy.wait()
    g_t = g_ref[...].astype(f32).T
    prod = g_t * o_ref[...].astype(f32).T
    row = lax.broadcasted_iota(jnp.int32, (8, TOK), 0)
    outs = []
    for h in range(HEADS):
        part = slice(h * DH, (h + 1) * DH)
        dot = -jnp.sum(prod[part], axis=0, keepdims=True)
        high = dot.astype(bf16).astype(f32)
        mid = (dot - high).astype(bf16).astype(f32)
        low = dot - high - mid
        dots = jnp.where(row == 0, high, jnp.where(row == 1, mid, jnp.where(row == 2, low, 0.0)))
        send_ref[h, FPAD : 2 * FPAD, :] = jnp.concatenate([g_t[part], dots]).astype(bf16)
        if h % 4 == 3:
            heads = slice(h - 3, h + 1)
            copy = pltpu.make_async_copy(send_ref.at[heads], out_ref.at[heads], out_sems.at[h // 4])
            copy.start()
            outs.append(copy)
    for copy in outs:
        copy.wait()


def keys_kernel(got_ref, out_ref, kv_ref, sem):
    copy = pltpu.make_async_copy(got_ref.at[:, 2 * FPAD : 2 * FPAD + 16], kv_ref, sem)
    copy.start()
    copy.wait()
    kv = kv_ref[...].astype(f32).reshape(HEADS, 2, CELLS, 128)
    k_t = kv[:, 0].reshape(128, 128).T
    v_t = kv[:, 1].reshape(128, 128).T
    out_ref[...] = jnp.concatenate([k_t[0:DH], v_t[0:DH]]).astype(bf16)


def load_keys(blocks, k_s, kt_s=None, v_s=None):
    lane = lax.broadcasted_iota(jnp.int32, (128, 128), 1)
    pad = jnp.zeros((128 - DH, 128), f32)
    norms = jnp.zeros((1, 128), f32)
    for b, block in enumerate(blocks):
        kv = block.astype(f32)
        keys = slice(b * 128, (b + 1) * 128)
        k_t = jnp.concatenate([kv[0:DH], pad])
        norms = jnp.maximum(norms, jnp.sum(k_t * k_t, axis=0, keepdims=True))
        k_s[keys] = k_t.T.astype(bf16)
        if kt_s is not None:
            kt_s[:, keys] = k_t.astype(bf16)
            v = jnp.concatenate([kv[DH:], pad]).T
            v_s[keys] = jnp.where((lane >= DH) & (lane < DH + 3), 1.0, v).astype(bf16)
    return jnp.max(norms)


def tile_of(qg_refs, row):
    blocks = [qg_ref[n, row : row + FPAD] for qg_ref in qg_refs for n in range(HEADS)]
    return jnp.concatenate(blocks, axis=1)


def log_sums(q_t, k_s, norm):
    exact = q_t.astype(f32)
    bound = jnp.sqrt(jnp.sum(exact * exact, axis=0, keepdims=True) * norm) * (SCALE2 * 1.001)

    def scores(rows):
        return jnp.dot(k_s[rows, 0:FPAD], q_t, preferred_element_type=f32) * SCALE2

    total = jnp.zeros((1, TILE), f32)
    for at in range(0, HALF, STEP):
        exps = jnp.exp2(scores(slice(at, at + STEP)) - bound)
        total = total + jnp.sum(exps, axis=0, keepdims=True)

    def again():
        def rows(n):
            return pl.ds(pl.multiple_of(n * 128, 128), 128)

        def largest(n, top):
            return jnp.maximum(top, jnp.max(scores(rows(n)), axis=0, keepdims=True))

        top = lax.fori_loop(0, HALF // 128, largest, jnp.full((1, TILE), -jnp.inf, f32))

        def add(n, total):
            return total + jnp.sum(jnp.exp2(scores(rows(n)) - top), axis=0, keepdims=True)

        return top + jnp.log2(lax.fori_loop(0, HALF // 128, add, jnp.zeros((1, TILE), f32)))

    return lax.cond(jnp.min(total) < 2.0**-90, again, lambda: bound + jnp.log2(total))


def put_sums(out_ref, sums):
    rows = [sums[:, n * TOK : (n + 1) * TOK] for n in range(2 * HEADS)]
    out_ref[...] = jnp.concatenate(rows).reshape(2, HEADS, TOK)


def get_sums(sums_ref):
    rows = sums_ref[...].reshape(2 * HEADS, TOK)
    return jnp.concatenate([rows[n : n + 1] for n in range(2 * HEADS)], axis=1)


def added(one, two):
    top = jnp.maximum(one, two)
    return top + jnp.log2(jnp.exp2(one - top) + jnp.exp2(two - top))


def first_sums_kernel(qg_a, qg_b, kv_0, kv_1, kv_2, kv_6, out_ref, k_s):
    norm = load_keys((kv_0[...], kv_1[...], kv_2[...], kv_6[...]), k_s)
    put_sums(out_ref, log_sums(tile_of((qg_a, qg_b), 0), k_s, norm))


def second_sums_kernel(qg_a, qg_b, kv_37, kv_45, first_ref, out_ref, k_s):
    norm = load_keys((kv_37[0], kv_37[1], kv_45[0], kv_45[1]), k_s)
    mine = log_sums(tile_of((qg_a, qg_b), 0), k_s, norm)
    put_sums(out_ref, added(mine, get_sums(first_ref)))


def gradients(sums_ref, qg_refs, put_dq, k_s, kt_s, v_s, dk_s, dv_s):
    q_t = tile_of(qg_refs, 0)
    g_t = tile_of(qg_refs, FPAD)
    sums = get_sums(sums_ref)
    dq = jnp.zeros((FPAD, TILE), f32)
    for at in range(0, HALF, STEP):
        b = slice(at, at + STEP)
        scores = jnp.dot(k_s[b, 0:FPAD], q_t, preferred_element_type=f32)
        probs = jnp.exp2(scores * SCALE2 - sums)
        half_probs = probs.astype(bf16)
        shifted = jnp.dot(v_s[b, 0:FPAD], g_t, preferred_element_type=f32)
        ds = (probs * shifted).astype(bf16)
        dk_s[b, 0:FPAD] = lax.dot_general(ds, q_t, NT, preferred_element_type=f32)
        dv_s[b, 0:FPAD] = lax.dot_general(half_probs, g_t, NT, preferred_element_type=f32)
        dq = dq + jnp.dot(kt_s[0:FPAD, b], ds, preferred_element_type=f32)
    for n in range(2 * HEADS):
        put_dq(n // HEADS, n % HEADS, dq[:, n * TOK : (n + 1) * TOK])


def put_keys(out_ref, dk_s, dv_s):
    dk_t = dk_s[...].T
    dv_t = dv_s[...].T
    for b in range(4):
        keys = slice(b * 128, (b + 1) * 128)
        block = jnp.concatenate([dk_t[0:DH, keys] * SCALE, dv_t[0:DH, keys]])
        out_ref[b] = block.astype(out_ref.dtype)


def first_kernel(
    qg_a, qg_b, kv_1, kv_37, kv_45, mine_ref, came_ref, sums_ref, dq_a, dq_b, out_ref,
    k_s, kt_s, v_s, dk_s, dv_s,
):
    load_keys((kv_1[...], kv_37[0], kv_37[1], kv_45[1]), k_s, kt_s, v_s)
    for at in (0, 1):
        sums_ref[at] = added(mine_ref[at], came_ref[1 - at])

    def put_dq(at, n, dq):
        (dq_a, dq_b)[at][n] = dq

    gradients(sums_ref, (qg_a, qg_b), put_dq, k_s, kt_s, v_s, dk_s, dv_s)
    put_keys(out_ref, dk_s, dv_s)


def edge_rows(dq):
    lane = lax.broadcasted_iota(jnp.int32, (24, TOK), 1)
    edges = pltpu.roll(dq[0:24], COLS, 1)
    for n in (1, 2):
        rolled = pltpu.roll(dq[24 * n : 24 * (n + 1)], COLS + 32 * n, 1)
        edges = jnp.where(lane < 32 * n, edges, rolled)
    return edges


def second_kernel(
    qg_a, qg_b, kv_0, kv_2, kv_6, kv_45, sums_ref, in_a, in_b, dq_a, dq_b, edge_a, edge_b, out_ref,
    k_s, kt_s, v_s, dk_s, dv_s,
):
    load_keys((kv_0[...], kv_2[...], kv_6[...], kv_45[0]), k_s, kt_s, v_s)

    def put_dq(at, n, dq):
        dq = (in_a, in_b)[at][n] + dq
        (dq_a, dq_b)[at][n] = dq
        (edge_a, edge_b)[at][n] = edge_rows(dq)

    gradients(sums_ref, (qg_a, qg_b), put_dq, k_s, kt_s, v_s, dk_s, dv_s)
    put_keys(out_ref, dk_s, dv_s)


def keys_sum_kernel(mine_ref, came_a, came_b, came_c, out_ref):
    total = mine_ref[0]
    for came in (came_a, came_b, came_c):
        total = total + came[...].astype(f32)
    out_ref[...] = total.astype(bf16)


def beside(x, first):
    none = jnp.zeros_like(x[0:2])
    above = jnp.where(first, jnp.concatenate([none, x[:-2]]), x)
    below = jnp.where(first, x, jnp.concatenate([x[2:], none]))
    return above, below


def pack_back_kernel(dq_ref, came_ref, edge_ref, came_edge_ref, keys_ref, other_ref, send_ref):
    first = lax.axis_index("c") == 0
    dq = (dq_ref[...] + came_ref[...])[:, 0:DH] * SCALE
    above, below = beside((edge_ref[...] + came_edge_ref[...]) * SCALE, first)
    lane = lax.broadcasted_iota(jnp.int32, (HEADS, 24, 128), 2)
    edges = jnp.where(lane % 32 < COLS, above, below)
    lanes = jnp.zeros((128, 128 - DH), f32)
    row = lax.broadcasted_iota(jnp.int32, (HEADS, CELLS, 128), 1)

    def cells(ref, part):
        rows = ref[...].astype(f32)[part * DH : (part + 1) * DH].T
        return jnp.concatenate([rows, lanes], axis=1).reshape(HEADS, CELLS, 128)

    parts = [dq, edges, cells(keys_ref, 0), cells(keys_ref, 1)]
    for part in (0, 1):
        above, below = beside(cells(other_ref, part), first)
        half = CELLS // 2
        parts.append(jnp.where(row < half, pltpu.roll(above, half, 1), pltpu.roll(below, half, 1)))
    send_ref[...] = jnp.concatenate(parts, axis=1).astype(bf16)


def weights_kernel(patch_ref, qkv_ref, out_ref):
    for part in range(3):
        cols = slice(part * D, (part + 1) * D)
        both = jnp.dot(patch_ref[...], qkv_ref[:, cols], preferred_element_type=f32)
        both = both.reshape(16, 2, 8, D)
        both = jnp.concatenate([both[:, 0].reshape(128, D), both[:, 1].reshape(128, D)])
        high, low = split(both)
        out_ref[0:256, cols] = high
        out_ref[256:512, cols] = low


def split(x):
    high = x.astype(bf16)
    return high, (x - high.astype(f32)).astype(bf16)


def iota(shape, dim):
    return lax.broadcasted_iota(jnp.int32, shape, dim)


def one_hot(where, value=1.0):
    return jnp.where(where, value, 0.0).astype(bf16)


def embed_kernel(back_ref, weights, turned_ref, near_out, far_out, joined, pooled, sheet):
    for h in range(0, HEADS, 2):
        pair = []
        wide = []
        for n in (h, h + 1):
            pair.append(back_ref[n, 0:TOK].astype(f32)[0:DH])
            edges = back_ref[n, 64 : 64 + 32].astype(f32)[DH - 64 :]
            wide += [edges, pltpu.roll(edges, 96, 1), pltpu.roll(edges, 64, 1)]
        rows = slice(h * DH, (h + 2) * DH)
        joined[rows, 0:TOK] = jnp.concatenate(pair).astype(bf16)
        joined[rows, TOK:] = jnp.concatenate(wide).astype(bf16)
    at = DH + 24
    group = iota((DH, 128), 1) // 16
    for h in range(0, HEADS, 4):
        cells = []
        for part in (0, 1):
            for n in range(h, h + 4):
                head = back_ref[n, at:].astype(f32)
                cells += [head[part * CELLS : (part + 1) * CELLS], head[16 + part * CELLS : 16 + (part + 1) * CELLS]]
        cells = jnp.concatenate(cells).T[0:DH]
        for part in (0, 1):
            for n in (0, 2):
                two = [jnp.where(group == 4 * part + k, cells, 0.0) for k in (n, n + 1)]
                rows = part * D + (h + n) * DH
                pooled[rows : rows + 2 * DH] = jnp.concatenate(two).astype(bf16)
    patch = jnp.dot(weights[:, 0:D], joined[...], preferred_element_type=f32)
    patch = patch[0:256] + patch[256:512]
    cells = jnp.dot(weights[:, D:], pooled[...], preferred_element_type=f32)
    cells = jnp.concatenate(split(cells[0:256] + cells[256:512]), axis=1)
    cell, token = iota((256, 256), 0) % 16, iota((256, 256), 1)
    mine = token // (POOL * COLS) * 4 + token % COLS // POOL
    beyond = CELLS + (token - TOK) // COLS * 4 + token % COLS // POOL
    holds = (cell == jnp.where(token < TOK, mine, beyond)) & (token < EXTENDED)
    patch = patch + jnp.dot(cells, one_hot(holds, 1.0 / POOL**2), preferred_element_type=f32)
    to, token = iota((EXTENDED, 256), 0), iota((EXTENDED, 256), 1)
    source = jnp.where(to < TOK, to % 8 * COLS, TOK + to % 2 * COLS) + column_of(to)
    turned = lax.dot_general(
        one_hot(token == source), jnp.concatenate(split(patch)), NT, preferred_element_type=f32
    )
    turned_ref[...] = turned.astype(bf16)
    whole = turned[:, 0:256] + turned[:, 256:512]
    left, right = whole[:, 0:128], whole[:, 128:256]
    lane = iota((8, 128), 1)
    own = jnp.where(lane % 8 < 4, left[0:ROWS], right[TOK - ROWS : TOK])
    beyond = jnp.where(lane % 8 < 4, left[TOK : TOK + 8], pltpu.roll(right[EXTENDED - 8 :], 2, 0))
    sheet[...] = jnp.zeros_like(sheet)
    for u in range(16):
        sheet[pl.ds(u, ROWS, stride=8), :] += pltpu.roll(own, (128 - 8 * u) % 128, 1)
        if u >= 12:
            sheet[u - 8 : u - 7, :] += pltpu.roll(beyond, 128 - 8 * u, 1)[0:1]
        if u < 4:
            sheet[64 + u : 65 + u, :] += pltpu.roll(beyond, (128 - 8 * u) % 128, 1)[1:2]
    edges = sheet[4:68].T
    begins = lax.axis_index("yl") == 0
    near_out[...] = jnp.where(begins, edges[4:8], edges[0:4])
    far_out[...] = jnp.where(begins, edges[0:4], edges[4:8])


def column_of(row):
    far = row - TOK
    return jnp.where(row < TOK, row // 8, far // 8 * 4 + far % 8 // 2)


def fold_kernel(turned_ref, center_ref, sheet):
    turned = turned_ref[...]
    sheet[...] = jnp.zeros_like(sheet)
    here = iota((EXTENDED, 256), 1) % 128 // 8 == column_of(iota((EXTENDED, 256), 0))
    to, at = iota((256, 256), 1), iota((256, 256), 0) % 128
    for pair in range(8):
        tile = one_hot((to // 128 + 2 * pair == at // 8) & (to % 8 == at % 8))
        for side in (0, 1):
            parts = [turned[:, n * 256 + side * 128 : n * 256 + (side + 1) * 128] for n in (0, 1)]
            wide = jnp.dot(jnp.concatenate(parts, axis=1), tile, preferred_element_type=f32)
            wide = jnp.where(here, wide, 0.0)
            own = jnp.sum(wide[0:TOK].reshape(COLS, ROWS, 256), axis=0)
            edge = jnp.sum(wide[TOK:].reshape(4, 8, 256), axis=0)
            edge = edge + pltpu.roll(edge, 4, 0)
            edge = edge + pltpu.roll(edge, 2, 0)
            for k in (0, 1):
                u = 2 * pair + k
                lanes = slice(k * 128, (k + 1) * 128)
                sheet[side, pl.ds(u, ROWS, stride=8), :] += own[:, lanes]
                if u >= 12:
                    sheet[side, u - 8 : u - 7, :] += edge[0:1, lanes]
                if u < 4:
                    sheet[side, 64 + u : 65 + u, :] += edge[1:2, lanes]
    left = sheet[0, 4:68]
    right = sheet[1, 4:68]
    lane = lax.broadcasted_iota(jnp.int32, left.shape, 1)
    center = jnp.where(lane < 124, pltpu.roll(left, 124, 1), 0.0)
    center_ref[...] = center + jnp.where(lane >= 4, pltpu.roll(right, 4, 1), 0.0)


def cols_kernel(center_ref, far_ref, near_ref, out_ref):
    begins = lax.axis_index("yl") == 0
    left = jnp.where(begins, far_ref[...], near_ref[...])
    right = jnp.where(begins, near_ref[...], far_ref[...])
    quiet = jnp.zeros((120, 64), f32)
    out_ref[...] = center_ref[...] + jnp.concatenate([left, quiet, right]).T


def swapped(x, axis, by):
    peers = lax.axis_size(axis)
    return lax.ppermute(x, axis, [(i, i ^ by) for i in range(peers)])


def neighbours(x, axis):
    peers = lax.axis_size(axis)
    pairs = [(i, i + 1) for i in range(1, peers - 1, 2)]
    return lax.ppermute(x, axis, pairs + [(target, source) for source, target in pairs])


def cost(products):
    flops = products * 4 * QUERIES * HALF * 256
    return pl.CostEstimate(flops=flops, bytes_accessed=2**20, transcendentals=2 * QUERIES * HALF)


def on_device(queries, key_states, values, saved_out, grad_out, w_qkv, w_patch):
    tokens = pltpu.VMEM((TOK, D), bf16)
    cells = pltpu.VMEM((2, 4, D), bf16)
    packed = (HEADS, 2 * FPAD + 16, TOK)
    dma = pltpu.SemaphoreType.DMA
    send = call(
        pack_kernel,
        jax.ShapeDtypeStruct(packed, bf16),
        None,
        [tokens, tokens, tokens, cells, cells, pltpu.VMEM(packed, bf16), dma((14,)), dma((4,))],
        [ANYWHERE] * 5,
        out_specs=ANYWHERE,
    )(
        queries.reshape(TOK, D),
        grad_out.reshape(TOK, D),
        saved_out.reshape(TOK, D),
        key_states,
        values,
    )
    got = lax.all_to_all(send, HEAD_AXES, 0, 0, tiled=True)
    kv = call(
        keys_kernel,
        jax.ShapeDtypeStruct((2 * DH, 128), bf16),
        4,
        [pltpu.VMEM((HEADS, 16, 128), bf16), dma(())],
        [ANYWHERE],
    )(got)
    kv_1, kv_2, kv_6 = [swapped(kv, "z", by) for by in (1, 2, 6)]
    kv_37 = swapped(jnp.stack([kv_2, kv_6]), "z", 1)
    kv_45 = swapped(jnp.stack([kv, kv_1]), "z", 4)
    there = swapped(got, "c", 1)
    keys = pltpu.VMEM((HALF, 128), bf16)
    sums = jax.ShapeDtypeStruct((2, HEADS, TOK), f32)
    mine = call(first_sums_kernel, sums, 24, [keys], cost_estimate=cost(1))(got, there, kv, kv_1, kv_2, kv_6)
    kv_37, kv_45, mine = lax.optimization_barrier((kv_37, kv_45, mine))
    mine = call(second_sums_kernel, sums, 24, [keys], cost_estimate=cost(1))(got, there, kv_37, kv_45, mine)
    came = swapped(mine, "c", 1)
    scratch = [keys, pltpu.VMEM((128, HALF), bf16), keys]
    scratch += [pltpu.VMEM((HALF, 128), f32)] * 2
    dq = [jax.ShapeDtypeStruct((HEADS, FPAD, TOK), f32)] * 2
    block = (4, 2 * DH, 128)
    sums, dq_here, dq_there, grads = call(
        first_kernel, [sums] + dq + [jax.ShapeDtypeStruct(block, bf16)], 32, scratch, cost_estimate=cost(5)
    )(got, there, kv_1, kv_37, kv_45, mine, came)
    came = swapped(grads, "z", 1)
    edges = [jax.ShapeDtypeStruct((HEADS, 24, TOK), f32)] * 2
    *dq, grads = call(
        second_kernel,
        dq + edges + [jax.ShapeDtypeStruct(block, f32)],
        32,
        scratch,
        cost_estimate=cost(5),
    )(got, there, kv, kv_2, kv_6, kv_45, sums, dq_here, dq_there)
    dq, grads, came = lax.optimization_barrier((dq, grads, came))
    dq_here, dq_there, edge_here, edge_there = dq
    dq_there = swapped(dq_there, "c", 1)
    edge_here = swapped(edge_here, "c", 1)
    mine = grads + came.astype(f32)
    mine, w_qkv, w_patch = lax.optimization_barrier((mine, w_qkv, w_patch))
    came = [swapped(mine[n + 1].astype(bf16), "z", by) for n, by in enumerate(EVEN)]
    weights = call(
        weights_kernel, jax.ShapeDtypeStruct((512, 3 * D), bf16), 24, cost_estimate=SMALL
    )(w_patch, w_qkv)
    came, weights = lax.optimization_barrier((came, weights))
    keys = call(keys_sum_kernel, jax.ShapeDtypeStruct((2 * DH, 128), bf16), 4)(mine[0:1], *came)
    other = swapped(keys, "c", 1)
    send = call(pack_back_kernel, jax.ShapeDtypeStruct((HEADS, 128, TOK), bf16), 16)(
        dq_here, dq_there, edge_there, edge_here, keys, other
    )
    back = lax.all_to_all(send, HEAD_AXES, 0, 0, tiled=True)
    strip = jax.ShapeDtypeStruct((4, 64), f32)
    turned, to_near, to_far = call(
        embed_kernel,
        [jax.ShapeDtypeStruct((EXTENDED, 512), bf16), strip, strip],
        28,
        [pltpu.VMEM((D, 2 * TOK), bf16), pltpu.VMEM((2 * D, 128), bf16), pltpu.VMEM((72, 128), f32)],
    )(back, weights)
    far, near = neighbours(to_far, COL), swapped(to_near, "yl", 1)
    center = call(
        fold_kernel,
        jax.ShapeDtypeStruct((64, 128), f32),
        8,
        [pltpu.VMEM((2, 72, 128), f32)],
        cost_estimate=SMALL,
    )(turned)
    far, near, center = lax.optimization_barrier((far, near, center))
    return call(cols_kernel, jax.ShapeDtypeStruct((64, 128), f32), 4)(center, far, near)


def solution(mesh):
    fine = Mesh(mesh.devices.reshape(2, 4, 2, 8, 2), ("yh", "x", "c", "z", "yl"))
    split = P(BLK, COL, None)
    return jax.shard_map(
        on_device,
        mesh=fine,
        in_specs=(split, split, split, split, split, P(), P()),
        out_specs=P(BLK, COL),
        check_vma=False,
    )
```

```python
import math

import jax
import jax.numpy as jnp
from jax import lax
from jax.experimental import pallas as pl
from jax.experimental.pallas import tpu as pltpu
from jax.sharding import Mesh, PartitionSpec as P

D = 1152
HEADS = 16
DH = D // HEADS
POOL = 4
SCALE = DH**-0.5
SCALE2 = SCALE * math.log2(math.e)
ROWS, COLS = 8, 16
TOK = ROWS * COLS
CELLS = TOK // POOL**2
EXTENDED = TOK + 2 * COLS
FPAD = 80
QUERIES = 2048
HALF = 512
TILE = 2 * QUERIES
STEP = 256
HEAD_AXES = ("yh", "x", "yl")
BLK = ("yh", "x", "c")
EVEN = (2, 6, 4)
COL = ("z", "yl")
REST = 96
NT = (((1,), (1,)), ((), ()))
SMALL = pl.CostEstimate(flops=2**20, bytes_accessed=2**16, transcendentals=0)
WHOLE = pl.BlockSpec(memory_space=pltpu.VMEM)
ANYWHERE = pl.BlockSpec(memory_space=pl.ANY)
bf16, f32 = jnp.bfloat16, jnp.float32


def call(kernel, out, mib, scratch=(), specs=None, **more):
    if specs is not None:
        more["in_specs"] = specs
    return pl.pallas_call(
        kernel,
        out_shape=out,
        scratch_shapes=scratch,
        compiler_params=pltpu.CompilerParams(vmem_limit_bytes=mib * 2**20 if mib else None),
        **more,
    )


def pack_kernel(
    q_in, g_in, o_in, k_in, v_in, out_ref, q_ref, g_ref, o_ref, k_ref, v_ref, send_ref, sems, out_sems
):
    pairs = [(k_in, k_ref), (v_in, v_ref)]
    quarter = TOK // 4
    for source, target in ((q_in, q_ref), (g_in, g_ref), (o_in, o_ref)):
        for at in range(0, TOK, quarter):
            pairs.append((source.at[at : at + quarter], target.at[at : at + quarter]))
    copies = [pltpu.make_async_copy(*pair, sems.at[n]) for n, pair in enumerate(pairs)]
    for copy in copies:
        copy.start()
    for copy in copies[:6]:
        copy.wait()
    q_t = q_ref[...].astype(f32).T
    keys = jnp.concatenate([k_ref[0].astype(f32), k_ref[1].astype(f32)])
    vals = jnp.concatenate([v_ref[0].astype(f32), v_ref[1].astype(f32)])
    lanes = jnp.zeros((CELLS, 128 - DH), f32)
    for h in range(HEADS):
        part = slice(h * DH, (h + 1) * DH)
        send_ref[h, 0:FPAD, :] = jnp.concatenate([q_t[part], jnp.zeros((8, TOK), f32)]).astype(bf16)
        k_h = jnp.concatenate([keys[:, part], lanes], axis=1)
        v_h = jnp.concatenate([vals[:, part], lanes], axis=1)
        send_ref[h, 2 * FPAD : 2 * FPAD + 16, :] = jnp.concatenate([k_h, v_h]).astype(bf16)
    for copy in copies[6:]:
        copy.wait()
    g_t = g_ref[...].astype(f32).T
    prod = g_t * o_ref[...].astype(f32).T
    row = lax.broadcasted_iota(jnp.int32, (8, TOK), 0)
    outs = []
    for h in range(HEADS):
        part = slice(h * DH, (h + 1) * DH)
        dot = -jnp.sum(prod[part], axis=0, keepdims=True)
        high = dot.astype(bf16).astype(f32)
        mid = (dot - high).astype(bf16).astype(f32)
        low = dot - high - mid
        dots = jnp.where(row == 0, high, jnp.where(row == 1, mid, jnp.where(row == 2, low, 0.0)))
        send_ref[h, FPAD : 2 * FPAD, :] = jnp.concatenate([g_t[part], dots]).astype(bf16)
        if h % 4 == 3:
            heads = slice(h - 3, h + 1)
            copy = pltpu.make_async_copy(send_ref.at[heads], out_ref.at[heads], out_sems.at[h // 4])
            copy.start()
            outs.append(copy)
    for copy in outs:
        copy.wait()


def keys_kernel(got_ref, out_ref, kv_ref, sem):
    copy = pltpu.make_async_copy(got_ref.at[:, 2 * FPAD : 2 * FPAD + 16], kv_ref, sem)
    copy.start()
    copy.wait()
    kv = kv_ref[...].astype(f32).reshape(HEADS, 2, CELLS, 128)
    k_t = kv[:, 0].reshape(128, 128).T
    v_t = kv[:, 1].reshape(128, 128).T
    out_ref[...] = jnp.concatenate([k_t[0:DH], v_t[0:DH]]).astype(bf16)


def load_keys(blocks, k_s, kt_s=None, v_s=None):
    lane = lax.broadcasted_iota(jnp.int32, (128, 128), 1)
    pad = jnp.zeros((128 - DH, 128), f32)
    norms = jnp.zeros((1, 128), f32)
    for b, block in enumerate(blocks):
        kv = block.astype(f32)
        keys = slice(b * 128, (b + 1) * 128)
        k_t = jnp.concatenate([kv[0:DH], pad])
        norms = jnp.maximum(norms, jnp.sum(k_t * k_t, axis=0, keepdims=True))
        k_s[keys] = k_t.T.astype(bf16)
        if kt_s is not None:
            kt_s[:, keys] = k_t.astype(bf16)
            v = jnp.concatenate([kv[DH:], pad]).T
            v_s[keys] = jnp.where((lane >= DH) & (lane < DH + 3), 1.0, v).astype(bf16)
    return jnp.max(norms)


def tile_of(qg_refs, row):
    blocks = [qg_ref[n, row : row + FPAD] for qg_ref in qg_refs for n in range(HEADS)]
    return jnp.concatenate(blocks, axis=1)


def log_sums(q_t, k_s, norm):
    exact = q_t.astype(f32)
    bound = jnp.sqrt(jnp.sum(exact * exact, axis=0, keepdims=True) * norm) * (SCALE2 * 1.001)

    def scores(rows):
        return jnp.dot(k_s[rows, 0:FPAD], q_t, preferred_element_type=f32) * SCALE2

    total = jnp.zeros((1, TILE), f32)
    for at in range(0, HALF, STEP):
        exps = jnp.exp2(scores(slice(at, at + STEP)) - bound)
        total = total + jnp.sum(exps, axis=0, keepdims=True)

    def again():
        def rows(n):
            return pl.ds(pl.multiple_of(n * 128, 128), 128)

        def largest(n, top):
            return jnp.maximum(top, jnp.max(scores(rows(n)), axis=0, keepdims=True))

        top = lax.fori_loop(0, HALF // 128, largest, jnp.full((1, TILE), -jnp.inf, f32))

        def add(n, total):
            return total + jnp.sum(jnp.exp2(scores(rows(n)) - top), axis=0, keepdims=True)

        return top + jnp.log2(lax.fori_loop(0, HALF // 128, add, jnp.zeros((1, TILE), f32)))

    return lax.cond(jnp.min(total) < 2.0**-90, again, lambda: bound + jnp.log2(total))


def put_sums(out_ref, sums):
    rows = [sums[:, n * TOK : (n + 1) * TOK] for n in range(2 * HEADS)]
    out_ref[...] = jnp.concatenate(rows).reshape(2, HEADS, TOK)


def get_sums(sums_ref):
    rows = sums_ref[...].reshape(2 * HEADS, TOK)
    return jnp.concatenate([rows[n : n + 1] for n in range(2 * HEADS)], axis=1)


def added(one, two):
    top = jnp.maximum(one, two)
    return top + jnp.log2(jnp.exp2(one - top) + jnp.exp2(two - top))


def first_sums_kernel(qg_a, qg_b, kv_0, kv_1, kv_2, kv_6, out_ref, k_s):
    norm = load_keys((kv_0[...], kv_1[...], kv_2[...], kv_6[...]), k_s)
    put_sums(out_ref, log_sums(tile_of((qg_a, qg_b), 0), k_s, norm))


def second_sums_kernel(qg_a, qg_b, kv_37, kv_45, first_ref, out_ref, k_s):
    norm = load_keys((kv_37[0], kv_37[1], kv_45[0], kv_45[1]), k_s)
    mine = log_sums(tile_of((qg_a, qg_b), 0), k_s, norm)
    put_sums(out_ref, added(mine, get_sums(first_ref)))


def gradients(sums_ref, qg_refs, put_dq, k_s, kt_s, v_s, dk_s, dv_s):
    q_t = tile_of(qg_refs, 0)
    g_t = tile_of(qg_refs, FPAD)
    sums = get_sums(sums_ref)
    dq = jnp.zeros((FPAD, TILE), f32)
    for at in range(0, HALF, STEP):
        b = slice(at, at + STEP)
        scores = jnp.dot(k_s[b, 0:FPAD], q_t, preferred_element_type=f32)
        probs = jnp.exp2(scores * SCALE2 - sums)
        half_probs = probs.astype(bf16)
        shifted = jnp.dot(v_s[b, 0:FPAD], g_t, preferred_element_type=f32)
        ds = (probs * shifted).astype(bf16)
        dk_s[b, 0:FPAD] = lax.dot_general(ds, q_t, NT, preferred_element_type=f32)
        dv_s[b, 0:FPAD] = lax.dot_general(half_probs, g_t, NT, preferred_element_type=f32)
        dq = dq + jnp.dot(kt_s[0:FPAD, b], ds, preferred_element_type=f32)
    for n in range(2 * HEADS):
        put_dq(n // HEADS, n % HEADS, dq[:, n * TOK : (n + 1) * TOK])


def put_keys(out_ref, dk_s, dv_s):
    dk_t = dk_s[...].T
    dv_t = dv_s[...].T
    for b in range(4):
        keys = slice(b * 128, (b + 1) * 128)
        block = jnp.concatenate([dk_t[0:DH, keys] * SCALE, dv_t[0:DH, keys]])
        out_ref[b] = block.astype(out_ref.dtype)


def first_kernel(
    qg_a, qg_b, kv_1, kv_37, kv_45, mine_ref, came_ref, sums_ref, dq_a, dq_b, out_ref,
    k_s, kt_s, v_s, dk_s, dv_s,
):
    load_keys((kv_1[...], kv_37[0], kv_37[1], kv_45[1]), k_s, kt_s, v_s)
    for at in (0, 1):
        sums_ref[at] = added(mine_ref[at], came_ref[1 - at])

    def put_dq(at, n, dq):
        (dq_a, dq_b)[at][n] = dq

    gradients(sums_ref, (qg_a, qg_b), put_dq, k_s, kt_s, v_s, dk_s, dv_s)
    put_keys(out_ref, dk_s, dv_s)


def edge_rows(dq):
    lane = lax.broadcasted_iota(jnp.int32, (24, TOK), 1)
    edges = pltpu.roll(dq[0:24], COLS, 1)
    for n in (1, 2):
        rolled = pltpu.roll(dq[24 * n : 24 * (n + 1)], COLS + 32 * n, 1)
        edges = jnp.where(lane < 32 * n, edges, rolled)
    return edges


def second_kernel(
    qg_a, qg_b, kv_0, kv_2, kv_6, kv_45, sums_ref, in_a, in_b, dq_a, dq_b, edge_a, edge_b, out_ref,
    k_s, kt_s, v_s, dk_s, dv_s,
):
    load_keys((kv_0[...], kv_2[...], kv_6[...], kv_45[0]), k_s, kt_s, v_s)

    def put_dq(at, n, dq):
        dq = (in_a, in_b)[at][n] + dq
        (dq_a, dq_b)[at][n] = dq
        (edge_a, edge_b)[at][n] = edge_rows(dq)

    gradients(sums_ref, (qg_a, qg_b), put_dq, k_s, kt_s, v_s, dk_s, dv_s)
    put_keys(out_ref, dk_s, dv_s)


def keys_sum_kernel(mine_ref, came_a, came_b, came_c, out_ref):
    total = mine_ref[0]
    for came in (came_a, came_b, came_c):
        total = total + came[...].astype(f32)
    out_ref[...] = total.astype(bf16)


def beside(x, first):
    none = jnp.zeros_like(x[0:2])
    above = jnp.where(first, jnp.concatenate([none, x[:-2]]), x)
    below = jnp.where(first, x, jnp.concatenate([x[2:], none]))
    return above, below


def pack_back_kernel(dq_ref, came_ref, edge_ref, came_edge_ref, keys_ref, other_ref, send_ref):
    first = lax.axis_index("c") == 0
    dq = (dq_ref[...] + came_ref[...])[:, 0:DH] * SCALE
    above, below = beside((edge_ref[...] + came_edge_ref[...]) * SCALE, first)
    lane = lax.broadcasted_iota(jnp.int32, (HEADS, 24, 128), 2)
    edges = jnp.where(lane % 32 < COLS, above, below)
    lanes = jnp.zeros((128, 128 - DH), f32)
    row = lax.broadcasted_iota(jnp.int32, (HEADS, CELLS, 128), 1)

    def cells(ref, part):
        rows = ref[...].astype(f32)[part * DH : (part + 1) * DH].T
        return jnp.concatenate([rows, lanes], axis=1).reshape(HEADS, CELLS, 128)

    both = []
    for part in (0, 1):
        above, below = beside(cells(other_ref, part), first)
        half = CELLS // 2
        near = jnp.where(row < half, pltpu.roll(above, half, 1), pltpu.roll(below, half, 1))
        both.append(jnp.concatenate([cells(keys_ref, part), near], axis=1))
    dk, dv = both
    lane = lax.broadcasted_iota(jnp.int32, dk.shape, 2)
    mixed = jnp.where(lane < DH, dk, pltpu.roll(dv, DH, 2))
    rest = pltpu.roll(dv, REST - (128 - DH), 2)
    rest = jnp.concatenate([rest, jnp.zeros((HEADS, 8, 128), f32)], axis=1)
    lane = lax.broadcasted_iota(jnp.int32, edges.shape, 2)
    edges = jnp.where(lane < REST, edges, rest)
    send_ref[...] = jnp.concatenate([dq, edges, mixed], axis=1).astype(bf16)


def weights_kernel(patch_ref, qkv_ref, out_ref):
    for part in range(3):
        cols = slice(part * D, (part + 1) * D)
        both = jnp.dot(patch_ref[...], qkv_ref[:, cols], preferred_element_type=f32)
        both = both.reshape(16, 2, 8, D)
        both = jnp.concatenate([both[:, 0].reshape(128, D), both[:, 1].reshape(128, D)])
        high, low = split(both)
        out_ref[0:256, cols] = high
        out_ref[256:512, cols] = low


def split(x):
    high = x.astype(bf16)
    return high, (x - high.astype(f32)).astype(bf16)


def iota(shape, dim):
    return lax.broadcasted_iota(jnp.int32, shape, dim)


def one_hot(where, value=1.0):
    return jnp.where(where, value, 0.0).astype(bf16)


def embed_kernel(back_ref, weights, turned_ref, near_out, far_out, joined, pooled, sheet):
    for h in range(0, HEADS, 2):
        pair = []
        wide = []
        for n in (h, h + 1):
            pair.append(back_ref[n, 0:TOK].astype(f32)[0:DH])
            edges = back_ref[n, 64 : 64 + 32].astype(f32)[DH - 64 :]
            wide += [edges, pltpu.roll(edges, 96, 1), pltpu.roll(edges, 64, 1)]
        rows = slice(h * DH, (h + 2) * DH)
        joined[rows, 0:TOK] = jnp.concatenate(pair).astype(bf16)
        joined[rows, TOK:] = jnp.concatenate(wide).astype(bf16)
    group = iota((DH, 128), 1) // 16
    fits = 128 - DH
    lane = iota((16, 128), 1)
    for h in range(0, HEADS, 4):
        keys, vals = [], []
        for n in range(h, h + 4):
            rest = back_ref[n, 64 : 64 + 32].astype(f32)[8 : 8 + 16]
            mixed = back_ref[n, 96:112].astype(f32)
            keys.append(mixed)
            vals.append(jnp.where(lane < fits, pltpu.roll(mixed, fits, 1), pltpu.roll(rest, 128 - (REST - fits), 1)))
        cells = keys + vals
        cells = jnp.concatenate(cells).T[0:DH]
        for part in (0, 1):
            for n in (0, 2):
                two = [jnp.where(group == 4 * part + k, cells, 0.0) for k in (n, n + 1)]
                rows = part * D + (h + n) * DH
                pooled[rows : rows + 2 * DH] = jnp.concatenate(two).astype(bf16)
    patch = jnp.dot(weights[:, 0:D], joined[...], preferred_element_type=f32)
    patch = patch[0:256] + patch[256:512]
    cells = jnp.dot(weights[:, D:], pooled[...], preferred_element_type=f32)
    cells = jnp.concatenate(split(cells[0:256] + cells[256:512]), axis=1)
    cell, token = iota((256, 256), 0) % 16, iota((256, 256), 1)
    mine = token // (POOL * COLS) * 4 + token % COLS // POOL
    beyond = CELLS + (token - TOK) // COLS * 4 + token % COLS // POOL
    holds = (cell == jnp.where(token < TOK, mine, beyond)) & (token < EXTENDED)
    patch = patch + jnp.dot(cells, one_hot(holds, 1.0 / POOL**2), preferred_element_type=f32)
    to, token = iota((EXTENDED, 256), 0), iota((EXTENDED, 256), 1)
    source = jnp.where(to < TOK, to % 8 * COLS, TOK + to % 2 * COLS) + column_of(to)
    turned = lax.dot_general(
        one_hot(token == source), jnp.concatenate(split(patch)), NT, preferred_element_type=f32
    )
    turned_ref[...] = turned.astype(bf16)
    whole = turned[:, 0:256] + turned[:, 256:512]
    left, right = whole[:, 0:128], whole[:, 128:256]
    lane = iota((8, 128), 1)
    own = jnp.where(lane % 8 < 4, left[0:ROWS], right[TOK - ROWS : TOK])
    beyond = jnp.where(lane % 8 < 4, left[TOK : TOK + 8], pltpu.roll(right[EXTENDED - 8 :], 2, 0))
    sheet[...] = jnp.zeros_like(sheet)
    for u in range(16):
        sheet[pl.ds(u, ROWS, stride=8), :] += pltpu.roll(own, (128 - 8 * u) % 128, 1)
        if u >= 12:
            sheet[u - 8 : u - 7, :] += pltpu.roll(beyond, 128 - 8 * u, 1)[0:1]
        if u < 4:
            sheet[64 + u : 65 + u, :] += pltpu.roll(beyond, (128 - 8 * u) % 128, 1)[1:2]
    edges = sheet[4:68].T
    begins = lax.axis_index("yl") == 0
    near_out[...] = jnp.where(begins, edges[4:8], edges[0:4])
    far_out[...] = jnp.where(begins, edges[0:4], edges[4:8])


def column_of(row):
    far = row - TOK
    return jnp.where(row < TOK, row // 8, far // 8 * 4 + far % 8 // 2)


def fold_kernel(turned_ref, center_ref, sheet):
    turned = turned_ref[...]
    sheet[...] = jnp.zeros_like(sheet)
    here = iota((EXTENDED, 256), 1) % 128 // 8 == column_of(iota((EXTENDED, 256), 0))
    to, at = iota((256, 256), 1), iota((256, 256), 0) % 128
    for pair in range(8):
        tile = one_hot((to // 128 + 2 * pair == at // 8) & (to % 8 == at % 8))
        for side in (0, 1):
            parts = [turned[:, n * 256 + side * 128 : n * 256 + (side + 1) * 128] for n in (0, 1)]
            wide = jnp.dot(jnp.concatenate(parts, axis=1), tile, preferred_element_type=f32)
            wide = jnp.where(here, wide, 0.0)
            own = jnp.sum(wide[0:TOK].reshape(COLS, ROWS, 256), axis=0)
            edge = jnp.sum(wide[TOK:].reshape(4, 8, 256), axis=0)
            edge = edge + pltpu.roll(edge, 4, 0)
            edge = edge + pltpu.roll(edge, 2, 0)
            for k in (0, 1):
                u = 2 * pair + k
                lanes = slice(k * 128, (k + 1) * 128)
                sheet[side, pl.ds(u, ROWS, stride=8), :] += own[:, lanes]
                if u >= 12:
                    sheet[side, u - 8 : u - 7, :] += edge[0:1, lanes]
                if u < 4:
                    sheet[side, 64 + u : 65 + u, :] += edge[1:2, lanes]
    left = sheet[0, 4:68]
    right = sheet[1, 4:68]
    lane = lax.broadcasted_iota(jnp.int32, left.shape, 1)
    center = jnp.where(lane < 124, pltpu.roll(left, 124, 1), 0.0)
    center_ref[...] = center + jnp.where(lane >= 4, pltpu.roll(right, 4, 1), 0.0)


def cols_kernel(center_ref, far_ref, near_ref, out_ref):
    begins = lax.axis_index("yl") == 0
    left = jnp.where(begins, far_ref[...], near_ref[...])
    right = jnp.where(begins, near_ref[...], far_ref[...])
    quiet = jnp.zeros((120, 64), f32)
    out_ref[...] = center_ref[...] + jnp.concatenate([left, quiet, right]).T


def swapped(x, axis, by):
    peers = lax.axis_size(axis)
    return lax.ppermute(x, axis, [(i, i ^ by) for i in range(peers)])


def neighbours(x, axis):
    peers = lax.axis_size(axis)
    pairs = [(i, i + 1) for i in range(1, peers - 1, 2)]
    return lax.ppermute(x, axis, pairs + [(target, source) for source, target in pairs])


def cost(products):
    flops = products * 4 * QUERIES * HALF * 256
    return pl.CostEstimate(flops=flops, bytes_accessed=2**20, transcendentals=2 * QUERIES * HALF)


def on_device(queries, key_states, values, saved_out, grad_out, w_qkv, w_patch):
    tokens = pltpu.VMEM((TOK, D), bf16)
    cells = pltpu.VMEM((2, 4, D), bf16)
    packed = (HEADS, 2 * FPAD + 16, TOK)
    dma = pltpu.SemaphoreType.DMA
    send = call(
        pack_kernel,
        jax.ShapeDtypeStruct(packed, bf16),
        None,
        [tokens, tokens, tokens, cells, cells, pltpu.VMEM(packed, bf16), dma((14,)), dma((4,))],
        [ANYWHERE] * 5,
        out_specs=ANYWHERE,
    )(
        queries.reshape(TOK, D),
        grad_out.reshape(TOK, D),
        saved_out.reshape(TOK, D),
        key_states,
        values,
    )
    got = lax.all_to_all(send, HEAD_AXES, 0, 0, tiled=True)
    kv = call(
        keys_kernel,
        jax.ShapeDtypeStruct((2 * DH, 128), bf16),
        4,
        [pltpu.VMEM((HEADS, 16, 128), bf16), dma(())],
        [ANYWHERE],
    )(got)
    kv_1, kv_2, kv_6 = [swapped(kv, "z", by) for by in (1, 2, 6)]
    kv_37 = swapped(jnp.stack([kv_2, kv_6]), "z", 1)
    kv_45 = swapped(jnp.stack([kv, kv_1]), "z", 4)
    there = swapped(got, "c", 1)
    keys = pltpu.VMEM((HALF, 128), bf16)
    sums = jax.ShapeDtypeStruct((2, HEADS, TOK), f32)
    mine = call(first_sums_kernel, sums, 24, [keys], cost_estimate=cost(1))(got, there, kv, kv_1, kv_2, kv_6)
    kv_37, kv_45, mine = lax.optimization_barrier((kv_37, kv_45, mine))
    mine = call(second_sums_kernel, sums, 24, [keys], cost_estimate=cost(1))(got, there, kv_37, kv_45, mine)
    came = swapped(mine, "c", 1)
    scratch = [keys, pltpu.VMEM((128, HALF), bf16), keys]
    scratch += [pltpu.VMEM((HALF, 128), f32)] * 2
    dq = [jax.ShapeDtypeStruct((HEADS, FPAD, TOK), f32)] * 2
    block = (4, 2 * DH, 128)
    sums, dq_here, dq_there, grads = call(
        first_kernel, [sums] + dq + [jax.ShapeDtypeStruct(block, bf16)], 32, scratch, cost_estimate=cost(5)
    )(got, there, kv_1, kv_37, kv_45, mine, came)
    came = swapped(grads, "z", 1)
    edges = [jax.ShapeDtypeStruct((HEADS, 24, TOK), f32)] * 2
    *dq, grads = call(
        second_kernel,
        dq + edges + [jax.ShapeDtypeStruct(block, f32)],
        32,
        scratch,
        cost_estimate=cost(5),
    )(got, there, kv, kv_2, kv_6, kv_45, sums, dq_here, dq_there)
    dq, grads, came = lax.optimization_barrier((dq, grads, came))
    dq_here, dq_there, edge_here, edge_there = dq
    dq_there = swapped(dq_there, "c", 1)
    edge_here = swapped(edge_here, "c", 1)
    mine = grads + came.astype(f32)
    mine, w_qkv, w_patch = lax.optimization_barrier((mine, w_qkv, w_patch))
    came = [swapped(mine[n + 1].astype(bf16), "z", by) for n, by in enumerate(EVEN)]
    weights = call(
        weights_kernel, jax.ShapeDtypeStruct((512, 3 * D), bf16), 24, cost_estimate=SMALL
    )(w_patch, w_qkv)
    came, weights = lax.optimization_barrier((came, weights))
    keys = call(keys_sum_kernel, jax.ShapeDtypeStruct((2 * DH, 128), bf16), 4)(mine[0:1], *came)
    other = swapped(keys, "c", 1)
    send = call(pack_back_kernel, jax.ShapeDtypeStruct((HEADS, 112, TOK), bf16), 16)(
        dq_here, dq_there, edge_there, edge_here, keys, other
    )
    back = lax.all_to_all(send, HEAD_AXES, 0, 0, tiled=True)
    strip = jax.ShapeDtypeStruct((4, 64), f32)
    turned, to_near, to_far = call(
        embed_kernel,
        [jax.ShapeDtypeStruct((EXTENDED, 512), bf16), strip, strip],
        28,
        [pltpu.VMEM((D, 2 * TOK), bf16), pltpu.VMEM((2 * D, 128), bf16), pltpu.VMEM((72, 128), f32)],
    )(back, weights)
    far, near = neighbours(to_far, COL), swapped(to_near, "yl", 1)
    center = call(
        fold_kernel,
        jax.ShapeDtypeStruct((64, 128), f32),
        8,
        [pltpu.VMEM((2, 72, 128), f32)],
        cost_estimate=SMALL,
    )(turned)
    far, near, center = lax.optimization_barrier((far, near, center))
    return call(cols_kernel, jax.ShapeDtypeStruct((64, 128), f32), 4)(center, far, near)


def solution(mesh):
    fine = Mesh(mesh.devices.reshape(2, 4, 2, 8, 2), ("yh", "x", "c", "z", "yl"))
    split = P(BLK, COL, None)
    return jax.shard_map(
        on_device,
        mesh=fine,
        in_specs=(split, split, split, split, split, P(), P()),
        out_specs=P(BLK, COL),
        check_vma=False,
    )
```

```python
import math

import jax
import jax.numpy as jnp
from jax import lax
from jax.experimental import pallas as pl
from jax.experimental.pallas import tpu as pltpu
from jax.sharding import Mesh, PartitionSpec as P

D = 1152
HEADS = 16
DH = D // HEADS
POOL = 4
SCALE = DH**-0.5
SCALE2 = SCALE * math.log2(math.e)
ROWS, COLS = 8, 16
TOK = ROWS * COLS
CELLS = TOK // POOL**2
EXTENDED = TOK + 2 * COLS
FPAD = 80
QUERIES = 2048
HALF = 512
TILE = 2 * QUERIES
STEP = 256
HEAD_AXES = ("yh", "x", "yl")
BLK = ("yh", "x", "c")
EVEN = (2, 6, 4)
COL = ("z", "yl")
REST = 96
NT = (((1,), (1,)), ((), ()))
SMALL = pl.CostEstimate(flops=2**20, bytes_accessed=2**16, transcendentals=0)
WHOLE = pl.BlockSpec(memory_space=pltpu.VMEM)
ANYWHERE = pl.BlockSpec(memory_space=pl.ANY)
bf16, f32 = jnp.bfloat16, jnp.float32


def call(kernel, out, mib, scratch=(), specs=None, **more):
    if specs is not None:
        more["in_specs"] = specs
    return pl.pallas_call(
        kernel,
        out_shape=out,
        scratch_shapes=scratch,
        compiler_params=pltpu.CompilerParams(vmem_limit_bytes=mib * 2**20 if mib else None),
        **more,
    )


def pack_kernel(
    q_in, g_in, o_in, k_in, v_in, out_ref, q_ref, g_ref, o_ref, k_ref, v_ref, send_ref, sems, out_sems
):
    pairs = [(k_in, k_ref), (v_in, v_ref)]
    quarter = TOK // 4
    for source, target in ((q_in, q_ref), (g_in, g_ref), (o_in, o_ref)):
        for at in range(0, TOK, quarter):
            pairs.append((source.at[at : at + quarter], target.at[at : at + quarter]))
    copies = [pltpu.make_async_copy(*pair, sems.at[n]) for n, pair in enumerate(pairs)]
    for copy in copies:
        copy.start()
    for copy in copies[:6]:
        copy.wait()
    q_t = q_ref[...].astype(f32).T
    keys = jnp.concatenate([k_ref[0].astype(f32), k_ref[1].astype(f32)])
    vals = jnp.concatenate([v_ref[0].astype(f32), v_ref[1].astype(f32)])
    lanes = jnp.zeros((CELLS, 128 - DH), f32)
    for h in range(HEADS):
        part = slice(h * DH, (h + 1) * DH)
        send_ref[h, 0:FPAD, :] = jnp.concatenate([q_t[part], jnp.zeros((8, TOK), f32)]).astype(bf16)
        k_h = jnp.concatenate([keys[:, part], lanes], axis=1)
        v_h = jnp.concatenate([vals[:, part], lanes], axis=1)
        send_ref[h, 2 * FPAD : 2 * FPAD + 16, :] = jnp.concatenate([k_h, v_h]).astype(bf16)
    for copy in copies[6:]:
        copy.wait()
    g_t = g_ref[...].astype(f32).T
    prod = g_t * o_ref[...].astype(f32).T
    row = lax.broadcasted_iota(jnp.int32, (8, TOK), 0)
    outs = []
    for h in range(HEADS):
        part = slice(h * DH, (h + 1) * DH)
        dot = -jnp.sum(prod[part], axis=0, keepdims=True)
        high = dot.astype(bf16).astype(f32)
        mid = (dot - high).astype(bf16).astype(f32)
        low = dot - high - mid
        dots = jnp.where(row == 0, high, jnp.where(row == 1, mid, jnp.where(row == 2, low, 0.0)))
        send_ref[h, FPAD : 2 * FPAD, :] = jnp.concatenate([g_t[part], dots]).astype(bf16)
        if h % 4 == 3:
            heads = slice(h - 3, h + 1)
            copy = pltpu.make_async_copy(send_ref.at[heads], out_ref.at[heads], out_sems.at[h // 4])
            copy.start()
            outs.append(copy)
    for copy in outs:
        copy.wait()


def keys_kernel(got_ref, out_ref, kv_ref, sem):
    copy = pltpu.make_async_copy(got_ref.at[:, 2 * FPAD : 2 * FPAD + 16], kv_ref, sem)
    copy.start()
    copy.wait()
    kv = kv_ref[...].astype(f32).reshape(HEADS, 2, CELLS, 128)
    k_t = kv[:, 0].reshape(128, 128).T
    v_t = kv[:, 1].reshape(128, 128).T
    out_ref[...] = jnp.concatenate([k_t[0:DH], v_t[0:DH]]).astype(bf16)


def key_rows(kv):
    return jnp.concatenate([kv.astype(f32)[0:DH], jnp.zeros((128 - DH, 128), f32)])


def load_keys(blocks, k_s):
    norms = jnp.zeros((1, 128), f32)
    for b, block in enumerate(blocks):
        k_t = key_rows(block)
        norms = jnp.maximum(norms, jnp.sum(k_t * k_t, axis=0, keepdims=True))
        k_s[b * 128 : (b + 1) * 128] = k_t.T.astype(bf16)
    return jnp.max(norms)


def layouts_kernel(kv_0, kv_1, kv_2, kv_6, kv_37, kv_45, k_odd, kt_odd, v_odd, k_even, kt_even, v_even):
    odd = (kv_1[...], kv_37[0], kv_37[1], kv_45[1]), k_odd, kt_odd, v_odd
    even = (kv_0[...], kv_2[...], kv_6[...], kv_45[0]), k_even, kt_even, v_even
    lane = lax.broadcasted_iota(jnp.int32, (128, 128), 1)
    pad = jnp.zeros((128 - DH, 128), f32)
    for blocks, k_ref, kt_ref, v_ref in (odd, even):
        for b, block in enumerate(blocks):
            keys = slice(b * 128, (b + 1) * 128)
            k_t = key_rows(block)
            k_ref[keys] = k_t.T.astype(bf16)
            kt_ref[:, keys] = k_t[0:FPAD].astype(bf16)
            v = jnp.concatenate([block.astype(f32)[DH:], pad]).T
            v_ref[keys] = jnp.where((lane >= DH) & (lane < DH + 3), 1.0, v).astype(bf16)


def tile_of(qg_refs, row):
    blocks = [qg_ref[n, row : row + FPAD] for qg_ref in qg_refs for n in range(HEADS)]
    return jnp.concatenate(blocks, axis=1)


def log_sums(q_t, k_s, norm):
    exact = q_t.astype(f32)
    bound = jnp.sqrt(jnp.sum(exact * exact, axis=0, keepdims=True) * norm) * (SCALE2 * 1.001)

    def scores(rows):
        return jnp.dot(k_s[rows, 0:FPAD], q_t, preferred_element_type=f32) * SCALE2

    total = jnp.zeros((1, TILE), f32)
    count = k_s.shape[0]
    for at in range(0, count, STEP):
        exps = jnp.exp2(scores(slice(at, at + STEP)) - bound)
        total = total + jnp.sum(exps, axis=0, keepdims=True)

    def again():
        def rows(n):
            return pl.ds(pl.multiple_of(n * 128, 128), 128)

        def largest(n, top):
            return jnp.maximum(top, jnp.max(scores(rows(n)), axis=0, keepdims=True))

        top = lax.fori_loop(0, count // 128, largest, jnp.full((1, TILE), -jnp.inf, f32))

        def add(n, total):
            return total + jnp.sum(jnp.exp2(scores(rows(n)) - top), axis=0, keepdims=True)

        return top + jnp.log2(lax.fori_loop(0, count // 128, add, jnp.zeros((1, TILE), f32)))

    return lax.cond(jnp.min(total) < 2.0**-90, again, lambda: bound + jnp.log2(total))


def put_sums(out_ref, sums):
    rows = [sums[:, n * TOK : (n + 1) * TOK] for n in range(2 * HEADS)]
    out_ref[...] = jnp.concatenate(rows).reshape(2, HEADS, TOK)


def get_sums(sums_ref):
    rows = sums_ref[...].reshape(2 * HEADS, TOK)
    return jnp.concatenate([rows[n : n + 1] for n in range(2 * HEADS)], axis=1)


def added(one, two):
    top = jnp.maximum(one, two)
    return top + jnp.log2(jnp.exp2(one - top) + jnp.exp2(two - top))


def first_sums_kernel(qg_a, qg_b, kv_0, kv_1, kv_2, kv_6, out_ref, k_s):
    norm = load_keys((kv_0[...], kv_1[...], kv_2[...], kv_6[...]), k_s)
    put_sums(out_ref, log_sums(tile_of((qg_a, qg_b), 0), k_s, norm))


def second_sums_kernel(qg_a, qg_b, kv_37, kv_45, first_ref, out_ref, k_s):
    norm = load_keys((kv_37[0], kv_37[1], kv_45[0], kv_45[1]), k_s)
    mine = log_sums(tile_of((qg_a, qg_b), 0), k_s, norm)
    put_sums(out_ref, added(mine, get_sums(first_ref)))


def gradients(sums_ref, qg_refs, put_dq, k_s, kt_s, v_s, dk_s, dv_s):
    q_t = tile_of(qg_refs, 0)
    g_t = tile_of(qg_refs, FPAD)
    sums = get_sums(sums_ref)
    dq = jnp.zeros((FPAD, TILE), f32)
    for at in range(0, HALF, STEP):
        b = slice(at, at + STEP)
        scores = jnp.dot(k_s[b, 0:FPAD], q_t, preferred_element_type=f32)
        probs = jnp.exp2(scores * SCALE2 - sums)
        half_probs = probs.astype(bf16)
        shifted = jnp.dot(v_s[b, 0:FPAD], g_t, preferred_element_type=f32)
        ds = (probs * shifted).astype(bf16)
        dk_s[b, 0:FPAD] = lax.dot_general(ds, q_t, NT, preferred_element_type=f32)
        dv_s[b, 0:FPAD] = lax.dot_general(half_probs, g_t, NT, preferred_element_type=f32)
        dq = dq + jnp.dot(kt_s[:, b], ds, preferred_element_type=f32)
    for n in range(2 * HEADS):
        put_dq(n // HEADS, n % HEADS, dq[:, n * TOK : (n + 1) * TOK])


def put_keys(out_ref, dk_s, dv_s):
    dk_t = dk_s[...].T
    dv_t = dv_s[...].T
    for b in range(4):
        keys = slice(b * 128, (b + 1) * 128)
        block = jnp.concatenate([dk_t[0:DH, keys] * SCALE, dv_t[0:DH, keys]])
        out_ref[b] = block.astype(out_ref.dtype)


def first_kernel(
    qg_a, qg_b, k_s, kt_s, v_s, mine_ref, came_ref, sums_ref, dq_a, dq_b, out_ref, dk_s, dv_s
):
    for at in (0, 1):
        sums_ref[at] = added(mine_ref[at], came_ref[1 - at])

    def put_dq(at, n, dq):
        (dq_a, dq_b)[at][n] = dq

    gradients(sums_ref, (qg_a, qg_b), put_dq, k_s, kt_s, v_s, dk_s, dv_s)
    put_keys(out_ref, dk_s, dv_s)


def edge_rows(dq):
    lane = lax.broadcasted_iota(jnp.int32, (24, TOK), 1)
    edges = pltpu.roll(dq[0:24], COLS, 1)
    for n in (1, 2):
        rolled = pltpu.roll(dq[24 * n : 24 * (n + 1)], COLS + 32 * n, 1)
        edges = jnp.where(lane < 32 * n, edges, rolled)
    return edges


def second_kernel(
    qg_a, qg_b, k_s, kt_s, v_s, sums_ref, in_a, in_b, here_ref, edge_ref, away_ref, out_ref, dk_s, dv_s
):
    def put_dq(at, n, dq):
        dq = (in_a, in_b)[at][n] + dq
        edges = edge_rows(dq)
        if at == 0:
            here_ref[n] = dq[0:DH]
            away_ref[n, DH:] = edges
        else:
            away_ref[n, 0:DH] = dq[0:DH]
            edge_ref[n] = edges

    gradients(sums_ref, (qg_a, qg_b), put_dq, k_s, kt_s, v_s, dk_s, dv_s)
    put_keys(out_ref, dk_s, dv_s)


def keys_sum_kernel(mine_ref, came_a, came_b, came_c, out_ref):
    total = mine_ref[0]
    for came in (came_a, came_b, came_c):
        total = total + came[...].astype(f32)
    out_ref[...] = total.astype(bf16)


def beside(x, first):
    none = jnp.zeros_like(x[0:2])
    above = jnp.where(first, jnp.concatenate([none, x[:-2]]), x)
    below = jnp.where(first, x, jnp.concatenate([x[2:], none]))
    return above, below


def pack_back_kernel(dq_ref, edge_ref, came_ref, keys_ref, other_ref, send_ref):
    first = lax.axis_index("c") == 0
    dq = (dq_ref[...] + came_ref[:, 0:DH]) * SCALE
    above, below = beside((edge_ref[...] + came_ref[:, DH:]) * SCALE, first)
    lane = lax.broadcasted_iota(jnp.int32, (HEADS, 24, 128), 2)
    edges = jnp.where(lane % 32 < COLS, above, below)
    lanes = jnp.zeros((128, 128 - DH), f32)
    row = lax.broadcasted_iota(jnp.int32, (HEADS, CELLS, 128), 1)

    def cells(ref, part):
        rows = ref[...].astype(f32)[part * DH : (part + 1) * DH].T
        return jnp.concatenate([rows, lanes], axis=1).reshape(HEADS, CELLS, 128)

    both = []
    for part in (0, 1):
        above, below = beside(cells(other_ref, part), first)
        half = CELLS // 2
        near = jnp.where(row < half, pltpu.roll(above, half, 1), pltpu.roll(below, half, 1))
        both.append(jnp.concatenate([cells(keys_ref, part), near], axis=1))
    dk, dv = both
    lane = lax.broadcasted_iota(jnp.int32, dk.shape, 2)
    mixed = jnp.where(lane < DH, dk, pltpu.roll(dv, DH, 2))
    rest = pltpu.roll(dv, REST - (128 - DH), 2)
    rest = jnp.concatenate([rest, jnp.zeros((HEADS, 8, 128), f32)], axis=1)
    lane = lax.broadcasted_iota(jnp.int32, edges.shape, 2)
    edges = jnp.where(lane < REST, edges, rest)
    send_ref[...] = jnp.concatenate([dq, edges, mixed], axis=1).astype(bf16)


def weights_kernel(patch_ref, qkv_ref, out_ref):
    for part in range(3):
        cols = slice(part * D, (part + 1) * D)
        both = jnp.dot(patch_ref[...], qkv_ref[:, cols], preferred_element_type=f32)
        both = both.reshape(16, 2, 8, D)
        both = jnp.concatenate([both[:, 0].reshape(128, D), both[:, 1].reshape(128, D)])
        high, low = split(both)
        out_ref[0:256, cols] = high
        out_ref[256:512, cols] = low


def split(x):
    high = x.astype(bf16)
    return high, (x - high.astype(f32)).astype(bf16)


def iota(shape, dim):
    return lax.broadcasted_iota(jnp.int32, shape, dim)


def one_hot(where, value=1.0):
    return jnp.where(where, value, 0.0).astype(bf16)


def embed_kernel(back_ref, weights, turned_ref, near_out, far_out, joined, pooled, sheet):
    for h in range(0, HEADS, 2):
        pair = []
        wide = []
        for n in (h, h + 1):
            pair.append(back_ref[n, 0:TOK].astype(f32)[0:DH])
            edges = back_ref[n, 64 : 64 + 32].astype(f32)[DH - 64 :]
            wide += [edges, pltpu.roll(edges, 96, 1), pltpu.roll(edges, 64, 1)]
        rows = slice(h * DH, (h + 2) * DH)
        joined[rows, 0:TOK] = jnp.concatenate(pair).astype(bf16)
        joined[rows, TOK:] = jnp.concatenate(wide).astype(bf16)
    group = iota((DH, 128), 1) // 16
    fits = 128 - DH
    lane = iota((16, 128), 1)
    for h in range(0, HEADS, 4):
        keys, vals = [], []
        for n in range(h, h + 4):
            rest = back_ref[n, 64 : 64 + 32].astype(f32)[8 : 8 + 16]
            mixed = back_ref[n, 96:112].astype(f32)
            keys.append(mixed)
            vals.append(jnp.where(lane < fits, pltpu.roll(mixed, fits, 1), pltpu.roll(rest, 128 - (REST - fits), 1)))
        cells = keys + vals
        cells = jnp.concatenate(cells).T[0:DH]
        for part in (0, 1):
            for n in (0, 2):
                two = [jnp.where(group == 4 * part + k, cells, 0.0) for k in (n, n + 1)]
                rows = part * D + (h + n) * DH
                pooled[rows : rows + 2 * DH] = jnp.concatenate(two).astype(bf16)
    patch = jnp.dot(weights[:, 0:D], joined[...], preferred_element_type=f32)
    patch = patch[0:256] + patch[256:512]
    cells = jnp.dot(weights[:, D:], pooled[...], preferred_element_type=f32)
    cells = jnp.concatenate(split(cells[0:256] + cells[256:512]), axis=1)
    cell, token = iota((256, 256), 0) % 16, iota((256, 256), 1)
    mine = token // (POOL * COLS) * 4 + token % COLS // POOL
    beyond = CELLS + (token - TOK) // COLS * 4 + token % COLS // POOL
    holds = (cell == jnp.where(token < TOK, mine, beyond)) & (token < EXTENDED)
    patch = patch + jnp.dot(cells, one_hot(holds, 1.0 / POOL**2), preferred_element_type=f32)
    to, token = iota((EXTENDED, 256), 0), iota((EXTENDED, 256), 1)
    source = jnp.where(to < TOK, to % 8 * COLS, TOK + to % 2 * COLS) + column_of(to)
    turned = lax.dot_general(
        one_hot(token == source), jnp.concatenate(split(patch)), NT, preferred_element_type=f32
    )
    turned_ref[...] = turned.astype(bf16)
    whole = turned[:, 0:256] + turned[:, 256:512]
    left, right = whole[:, 0:128], whole[:, 128:256]
    lane = iota((8, 128), 1)
    own = jnp.where(lane % 8 < 4, left[0:ROWS], right[TOK - ROWS : TOK])
    beyond = jnp.where(lane % 8 < 4, left[TOK : TOK + 8], pltpu.roll(right[EXTENDED - 8 :], 2, 0))
    sheet[...] = jnp.zeros_like(sheet)
    for u in range(16):
        sheet[pl.ds(u, ROWS, stride=8), :] += pltpu.roll(own, (128 - 8 * u) % 128, 1)
        if u >= 12:
            sheet[u - 8 : u - 7, :] += pltpu.roll(beyond, 128 - 8 * u, 1)[0:1]
        if u < 4:
            sheet[64 + u : 65 + u, :] += pltpu.roll(beyond, (128 - 8 * u) % 128, 1)[1:2]
    edges = sheet[4:68].T
    begins = lax.axis_index("yl") == 0
    near_out[...] = jnp.where(begins, edges[4:8], edges[0:4])
    far_out[...] = jnp.where(begins, edges[0:4], edges[4:8])


def column_of(row):
    far = row - TOK
    return jnp.where(row < TOK, row // 8, far // 8 * 4 + far % 8 // 2)


def fold_kernel(turned_ref, center_ref, sheet):
    turned = turned_ref[...]
    sheet[...] = jnp.zeros_like(sheet)
    here = iota((EXTENDED, 256), 1) % 128 // 8 == column_of(iota((EXTENDED, 256), 0))
    to, at = iota((256, 256), 1), iota((256, 256), 0) % 128
    for pair in range(8):
        tile = one_hot((to // 128 + 2 * pair == at // 8) & (to % 8 == at % 8))
        for side in (0, 1):
            parts = [turned[:, n * 256 + side * 128 : n * 256 + (side + 1) * 128] for n in (0, 1)]
            wide = jnp.dot(jnp.concatenate(parts, axis=1), tile, preferred_element_type=f32)
            wide = jnp.where(here, wide, 0.0)
            own = jnp.sum(wide[0:TOK].reshape(COLS, ROWS, 256), axis=0)
            edge = jnp.sum(wide[TOK:].reshape(4, 8, 256), axis=0)
            edge = edge + pltpu.roll(edge, 4, 0)
            edge = edge + pltpu.roll(edge, 2, 0)
            for k in (0, 1):
                u = 2 * pair + k
                lanes = slice(k * 128, (k + 1) * 128)
                sheet[side, pl.ds(u, ROWS, stride=8), :] += own[:, lanes]
                if u >= 12:
                    sheet[side, u - 8 : u - 7, :] += edge[0:1, lanes]
                if u < 4:
                    sheet[side, 64 + u : 65 + u, :] += edge[1:2, lanes]
    left = sheet[0, 4:68]
    right = sheet[1, 4:68]
    lane = lax.broadcasted_iota(jnp.int32, left.shape, 1)
    center = jnp.where(lane < 124, pltpu.roll(left, 124, 1), 0.0)
    center_ref[...] = center + jnp.where(lane >= 4, pltpu.roll(right, 4, 1), 0.0)


def cols_kernel(center_ref, near_ref, far_ref, out_ref):
    begins = lax.axis_index("yl") == 0
    left = jnp.where(begins, far_ref[...], near_ref[...])
    right = jnp.where(begins, near_ref[...], far_ref[...])
    quiet = jnp.zeros((120, 64), f32)
    out_ref[...] = center_ref[...] + jnp.concatenate([left, quiet, right]).T


def swapped(x, axis, by):
    peers = lax.axis_size(axis)
    return lax.ppermute(x, axis, [(i, i ^ by) for i in range(peers)])


def neighbours(x, axis):
    peers = lax.axis_size(axis)
    pairs = [(i, i + 1) for i in range(1, peers - 1, 2)]
    return lax.ppermute(x, axis, pairs + [(target, source) for source, target in pairs])


def cost(products):
    flops = products * 4 * QUERIES * HALF * 256
    return pl.CostEstimate(flops=flops, bytes_accessed=2**20, transcendentals=2 * QUERIES * HALF)


def on_device(queries, key_states, values, saved_out, grad_out, w_qkv, w_patch):
    tokens = pltpu.VMEM((TOK, D), bf16)
    cells = pltpu.VMEM((2, 4, D), bf16)
    packed = (HEADS, 2 * FPAD + 16, TOK)
    dma = pltpu.SemaphoreType.DMA
    send = call(
        pack_kernel,
        jax.ShapeDtypeStruct(packed, bf16),
        None,
        [tokens, tokens, tokens, cells, cells, pltpu.VMEM(packed, bf16), dma((14,)), dma((4,))],
        [ANYWHERE] * 5,
        out_specs=ANYWHERE,
    )(
        queries.reshape(TOK, D),
        grad_out.reshape(TOK, D),
        saved_out.reshape(TOK, D),
        key_states,
        values,
    )
    got = lax.all_to_all(send, HEAD_AXES, 0, 0, tiled=True)
    kv = call(
        keys_kernel,
        jax.ShapeDtypeStruct((2 * DH, 128), bf16),
        4,
        [pltpu.VMEM((HEADS, 16, 128), bf16), dma(())],
        [ANYWHERE],
    )(got)
    kv_1, kv_2, kv_6 = [swapped(kv, "z", by) for by in (1, 2, 6)]
    kv_37 = swapped(jnp.stack([kv_2, kv_6]), "z", 1)
    kv_45 = swapped(jnp.stack([kv, kv_1]), "z", 4)
    there = swapped(got, "c", 1)
    sums = jax.ShapeDtypeStruct((2, HEADS, TOK), f32)
    keys = pltpu.VMEM((HALF, 128), bf16)
    mine = call(first_sums_kernel, sums, 24, [keys], cost_estimate=cost(1))(got, there, kv, kv_1, kv_2, kv_6)
    kv_37, kv_45, mine = lax.optimization_barrier((kv_37, kv_45, mine))
    mine = call(second_sums_kernel, sums, 24, [keys], cost_estimate=cost(1))(got, there, kv_37, kv_45, mine)
    mine, kv_45 = lax.optimization_barrier((mine, kv_45))
    came = swapped(mine, "c", 1)
    layout = [jax.ShapeDtypeStruct(shape, bf16) for shape in ((HALF, 128), (FPAD, HALF), (HALF, 128))]
    layouts = call(layouts_kernel, layout * 2, 8, cost_estimate=SMALL)(kv, kv_1, kv_2, kv_6, kv_37, kv_45)
    came, layouts = lax.optimization_barrier((came, layouts))
    scratch = [pltpu.VMEM((HALF, 128), f32)] * 2
    dq = [jax.ShapeDtypeStruct((HEADS, FPAD, TOK), f32)] * 2
    block = (4, 2 * DH, 128)
    sums, dq_here, dq_there, grads = call(
        first_kernel, [sums] + dq + [jax.ShapeDtypeStruct(block, bf16)], 32, scratch, cost_estimate=cost(5)
    )(got, there, *layouts[:3], mine, came)
    came = swapped(grads, "z", 1)
    shapes = [jax.ShapeDtypeStruct((HEADS, rows, TOK), f32) for rows in (DH, 24, DH + 24)]
    *dq, grads = call(
        second_kernel,
        shapes + [jax.ShapeDtypeStruct(block, f32)],
        32,
        scratch,
        cost_estimate=cost(5),
    )(got, there, *layouts[3:], sums, dq_here, dq_there)
    dq, grads, came = lax.optimization_barrier((dq, grads, came))
    dq_here, edges, away = dq
    away = swapped(away, "c", 1)
    mine = grads + came.astype(f32)
    mine, w_qkv, w_patch = lax.optimization_barrier((mine, w_qkv, w_patch))
    came = [swapped(mine[n + 1].astype(bf16), "z", by) for n, by in enumerate(EVEN)]
    weights = call(
        weights_kernel, jax.ShapeDtypeStruct((512, 3 * D), bf16), 24, cost_estimate=SMALL
    )(w_patch, w_qkv)
    came, weights = lax.optimization_barrier((came, weights))
    keys = call(keys_sum_kernel, jax.ShapeDtypeStruct((2 * DH, 128), bf16), 4)(mine[0:1], *came)
    other = swapped(keys, "c", 1)
    send = call(pack_back_kernel, jax.ShapeDtypeStruct((HEADS, 112, TOK), bf16), 16)(
        dq_here, edges, away, keys, other
    )
    back = lax.all_to_all(send, HEAD_AXES, 0, 0, tiled=True)
    strip = jax.ShapeDtypeStruct((4, 64), f32)
    turned, to_near, to_far = call(
        embed_kernel,
        [jax.ShapeDtypeStruct((EXTENDED, 512), bf16), strip, strip],
        28,
        [pltpu.VMEM((D, 2 * TOK), bf16), pltpu.VMEM((2 * D, 128), bf16), pltpu.VMEM((72, 128), f32)],
    )(back, weights)
    near, far = swapped(to_near, "yl", 1), neighbours(to_far, COL)
    center = call(
        fold_kernel,
        jax.ShapeDtypeStruct((64, 128), f32),
        8,
        [pltpu.VMEM((2, 72, 128), f32)],
        cost_estimate=SMALL,
    )(turned)
    near, far, center = lax.optimization_barrier((near, far, center))
    return call(cols_kernel, jax.ShapeDtypeStruct((64, 128), f32), 4)(center, near, far)


def solution(mesh):
    fine = Mesh(mesh.devices.reshape(2, 4, 2, 8, 2), ("yh", "x", "c", "z", "yl"))
    split = P(BLK, COL, None)
    return jax.shard_map(
        on_device,
        mesh=fine,
        in_specs=(split, split, split, split, split, P(), P()),
        out_specs=P(BLK, COL),
        check_vma=False,
    )
```

```python
import math

import jax
import jax.numpy as jnp
from jax import lax
from jax.experimental import pallas as pl
from jax.experimental.pallas import tpu as pltpu
from jax.sharding import Mesh, PartitionSpec as P

D = 1152
HEADS = 16
DH = D // HEADS
POOL = 4
SCALE = DH**-0.5
SCALE2 = SCALE * math.log2(math.e)
ROWS, COLS = 8, 16
TOK = ROWS * COLS
CELLS = TOK // POOL**2
EXTENDED = TOK + 2 * COLS
FPAD = 80
QUERIES = 2048
HALF = 512
TILE = 2 * QUERIES
STEP = 256
HEAD_AXES = ("yh", "x", "yl")
BLK = ("yh", "x", "c")
EVEN = (2, 6, 4)
COL = ("z", "yl")
REST = 96
NT = (((1,), (1,)), ((), ()))
SMALL = pl.CostEstimate(flops=2**20, bytes_accessed=2**16, transcendentals=0)
WHOLE = pl.BlockSpec(memory_space=pltpu.VMEM)
ANYWHERE = pl.BlockSpec(memory_space=pl.ANY)
bf16, f32 = jnp.bfloat16, jnp.float32


def call(kernel, out, mib, scratch=(), specs=None, **more):
    if specs is not None:
        more["in_specs"] = specs
    return pl.pallas_call(
        kernel,
        out_shape=out,
        scratch_shapes=scratch,
        compiler_params=pltpu.CompilerParams(vmem_limit_bytes=mib * 2**20 if mib else None),
        **more,
    )


def pack_kernel(
    q_in, g_in, o_in, k_in, v_in, out_ref, q_ref, g_ref, o_ref, k_ref, v_ref, send_ref, sems, out_sems
):
    pairs = [(k_in, k_ref), (v_in, v_ref)]
    quarter = TOK // 4
    for source, target in ((q_in, q_ref), (g_in, g_ref), (o_in, o_ref)):
        for at in range(0, TOK, quarter):
            pairs.append((source.at[at : at + quarter], target.at[at : at + quarter]))
    copies = [pltpu.make_async_copy(*pair, sems.at[n]) for n, pair in enumerate(pairs)]
    for copy in copies:
        copy.start()
    for copy in copies[:6]:
        copy.wait()
    q_t = q_ref[...].astype(f32).T
    keys = jnp.concatenate([k_ref[0].astype(f32), k_ref[1].astype(f32)])
    vals = jnp.concatenate([v_ref[0].astype(f32), v_ref[1].astype(f32)])
    lanes = jnp.zeros((CELLS, 128 - DH), f32)
    for h in range(HEADS):
        part = slice(h * DH, (h + 1) * DH)
        send_ref[h, 0:FPAD, :] = jnp.concatenate([q_t[part], jnp.zeros((8, TOK), f32)]).astype(bf16)
        k_h = jnp.concatenate([keys[:, part], lanes], axis=1)
        v_h = jnp.concatenate([vals[:, part], lanes], axis=1)
        send_ref[h, 2 * FPAD : 2 * FPAD + 16, :] = jnp.concatenate([k_h, v_h]).astype(bf16)
    for copy in copies[6:]:
        copy.wait()
    g_t = g_ref[...].astype(f32).T
    prod = g_t * o_ref[...].astype(f32).T
    row = lax.broadcasted_iota(jnp.int32, (8, TOK), 0)
    outs = []
    for h in range(HEADS):
        part = slice(h * DH, (h + 1) * DH)
        dot = -jnp.sum(prod[part], axis=0, keepdims=True)
        high = dot.astype(bf16).astype(f32)
        mid = (dot - high).astype(bf16).astype(f32)
        low = dot - high - mid
        dots = jnp.where(row == 0, high, jnp.where(row == 1, mid, jnp.where(row == 2, low, 0.0)))
        send_ref[h, FPAD : 2 * FPAD, :] = jnp.concatenate([g_t[part], dots]).astype(bf16)
        if h % 4 == 3:
            heads = slice(h - 3, h + 1)
            copy = pltpu.make_async_copy(send_ref.at[heads], out_ref.at[heads], out_sems.at[h // 4])
            copy.start()
            outs.append(copy)
    for copy in outs:
        copy.wait()


def keys_kernel(got_ref, out_ref, kv_ref, sem):
    copy = pltpu.make_async_copy(got_ref.at[:, 2 * FPAD : 2 * FPAD + 16], kv_ref, sem)
    copy.start()
    copy.wait()
    kv = kv_ref[...].astype(f32).reshape(HEADS, 2, CELLS, 128)
    k_t = kv[:, 0].reshape(128, 128).T
    v_t = kv[:, 1].reshape(128, 128).T
    out_ref[...] = jnp.concatenate([k_t[0:DH], v_t[0:DH]]).astype(bf16)


def key_rows(kv):
    return jnp.concatenate([kv.astype(f32)[0:DH], jnp.zeros((128 - DH, 128), f32)])


def load_keys(blocks, k_s):
    norms = jnp.zeros((1, 128), f32)
    for b, block in enumerate(blocks):
        k_t = key_rows(block)
        norms = jnp.maximum(norms, jnp.sum(k_t * k_t, axis=0, keepdims=True))
        k_s[b * 128 : (b + 1) * 128] = k_t.T.astype(bf16)
    return jnp.max(norms)


def layouts_kernel(kv_0, kv_1, kv_2, kv_6, kv_37, kv_45, k_odd, kt_odd, v_odd, k_even, kt_even, v_even):
    odd = (kv_1[...], kv_37[0], kv_37[1], kv_45[1]), k_odd, kt_odd, v_odd
    even = (kv_0[...], kv_2[...], kv_6[...], kv_45[0]), k_even, kt_even, v_even
    lane = lax.broadcasted_iota(jnp.int32, (128, 128), 1)
    pad = jnp.zeros((128 - DH, 128), f32)
    for blocks, k_ref, kt_ref, v_ref in (odd, even):
        for b, block in enumerate(blocks):
            keys = slice(b * 128, (b + 1) * 128)
            k_t = key_rows(block)
            k_ref[keys] = k_t.T.astype(bf16)
            kt_ref[:, keys] = k_t[0:FPAD].astype(bf16)
            v = jnp.concatenate([block.astype(f32)[DH:], pad]).T
            v_ref[keys] = jnp.where((lane >= DH) & (lane < DH + 3), 1.0, v).astype(bf16)


def tile_of(qg_refs, row):
    blocks = [qg_ref[n, row : row + FPAD] for qg_ref in qg_refs for n in range(HEADS)]
    return jnp.concatenate(blocks, axis=1)


def log_sums(q_t, k_s, norm):
    exact = q_t.astype(f32)
    bound = jnp.sqrt(jnp.sum(exact * exact, axis=0, keepdims=True) * norm) * (SCALE2 * 1.001)

    def scores(rows):
        return jnp.dot(k_s[rows, 0:FPAD], q_t, preferred_element_type=f32) * SCALE2

    total = jnp.zeros((1, TILE), f32)
    count = k_s.shape[0]
    for at in range(0, count, STEP):
        exps = jnp.exp2(scores(slice(at, at + STEP)) - bound)
        total = total + jnp.sum(exps, axis=0, keepdims=True)

    def again():
        def rows(n):
            return pl.ds(pl.multiple_of(n * 128, 128), 128)

        def largest(n, top):
            return jnp.maximum(top, jnp.max(scores(rows(n)), axis=0, keepdims=True))

        top = lax.fori_loop(0, count // 128, largest, jnp.full((1, TILE), -jnp.inf, f32))

        def add(n, total):
            return total + jnp.sum(jnp.exp2(scores(rows(n)) - top), axis=0, keepdims=True)

        return top + jnp.log2(lax.fori_loop(0, count // 128, add, jnp.zeros((1, TILE), f32)))

    return lax.cond(jnp.min(total) < 2.0**-90, again, lambda: bound + jnp.log2(total))


def put_sums(out_ref, sums):
    rows = [sums[:, n * TOK : (n + 1) * TOK] for n in range(2 * HEADS)]
    out_ref[...] = jnp.concatenate(rows).reshape(2, HEADS, TOK)


def get_sums(sums_ref):
    rows = sums_ref[...].reshape(2 * HEADS, TOK)
    return jnp.concatenate([rows[n : n + 1] for n in range(2 * HEADS)], axis=1)


def added(one, two):
    top = jnp.maximum(one, two)
    return top + jnp.log2(jnp.exp2(one - top) + jnp.exp2(two - top))


def first_sums_kernel(qg_a, qg_b, kv_0, kv_1, kv_2, kv_6, out_ref, k_s):
    norm = load_keys((kv_0[...], kv_1[...], kv_2[...], kv_6[...]), k_s)
    put_sums(out_ref, log_sums(tile_of((qg_a, qg_b), 0), k_s, norm))


def second_sums_kernel(qg_a, qg_b, kv_37, kv_45, first_ref, out_ref, k_s):
    norm = load_keys((kv_37[0], kv_37[1], kv_45[0], kv_45[1]), k_s)
    mine = log_sums(tile_of((qg_a, qg_b), 0), k_s, norm)
    put_sums(out_ref, added(mine, get_sums(first_ref)))


def gradients(sums_ref, qg_refs, put_dq, k_s, kt_s, v_s, dk_s, dv_s):
    q_t = tile_of(qg_refs, 0)
    g_t = tile_of(qg_refs, FPAD)
    sums = get_sums(sums_ref)
    dq = jnp.zeros((FPAD, TILE), f32)
    for at in range(0, HALF, STEP):
        b = slice(at, at + STEP)
        scores = jnp.dot(k_s[b, 0:FPAD], q_t, preferred_element_type=f32)
        probs = jnp.exp2(scores * SCALE2 - sums)
        half_probs = probs.astype(bf16)
        shifted = jnp.dot(v_s[b, 0:FPAD], g_t, preferred_element_type=f32)
        ds = (probs * shifted).astype(bf16)
        dk_s[b, 0:FPAD] = lax.dot_general(ds, q_t, NT, preferred_element_type=f32)
        dv_s[b, 0:FPAD] = lax.dot_general(half_probs, g_t, NT, preferred_element_type=f32)
        dq = dq + jnp.dot(kt_s[:, b], ds, preferred_element_type=f32)
    for n in range(2 * HEADS):
        put_dq(n // HEADS, n % HEADS, dq[:, n * TOK : (n + 1) * TOK])


def put_keys(out_ref, dk_s, dv_s):
    dk_t = dk_s[...].T
    dv_t = dv_s[...].T
    for b in range(4):
        keys = slice(b * 128, (b + 1) * 128)
        block = jnp.concatenate([dk_t[0:DH, keys] * SCALE, dv_t[0:DH, keys]])
        out_ref[b] = block.astype(out_ref.dtype)


def first_kernel(
    qg_a, qg_b, k_s, kt_s, v_s, mine_ref, came_ref, sums_ref, dq_a, dq_b, out_ref, dk_s, dv_s
):
    for at in (0, 1):
        sums_ref[at] = added(mine_ref[at], came_ref[1 - at])

    def put_dq(at, n, dq):
        (dq_a, dq_b)[at][n] = dq

    gradients(sums_ref, (qg_a, qg_b), put_dq, k_s, kt_s, v_s, dk_s, dv_s)
    put_keys(out_ref, dk_s, dv_s)


def edge_rows(dq):
    lane = lax.broadcasted_iota(jnp.int32, (24, TOK), 1)
    edges = pltpu.roll(dq[0:24], COLS, 1)
    for n in (1, 2):
        rolled = pltpu.roll(dq[24 * n : 24 * (n + 1)], COLS + 32 * n, 1)
        edges = jnp.where(lane < 32 * n, edges, rolled)
    return edges


def second_kernel(
    qg_a, qg_b, k_s, kt_s, v_s, sums_ref, in_a, in_b, here_ref, edge_ref, away_ref, out_ref, dk_s, dv_s
):
    def put_dq(at, n, dq):
        dq = (in_a, in_b)[at][n] + dq
        edges = edge_rows(dq)
        if at == 0:
            here_ref[n] = dq[0:DH]
            away_ref[n, DH:] = edges
        else:
            away_ref[n, 0:DH] = dq[0:DH]
            edge_ref[n] = edges

    gradients(sums_ref, (qg_a, qg_b), put_dq, k_s, kt_s, v_s, dk_s, dv_s)
    put_keys(out_ref, dk_s, dv_s)


def keys_sum_kernel(mine_ref, came_a, came_b, came_c, out_ref):
    total = mine_ref[0]
    for came in (came_a, came_b, came_c):
        total = total + came[...].astype(f32)
    out_ref[...] = total.astype(bf16)


def beside(x, first):
    none = jnp.zeros_like(x[0:2])
    above = jnp.where(first, jnp.concatenate([none, x[:-2]]), x)
    below = jnp.where(first, x, jnp.concatenate([x[2:], none]))
    return above, below


def pack_back_kernel(dq_ref, edge_ref, came_ref, keys_ref, other_ref, send_ref):
    first = lax.axis_index("c") == 0
    dq = (dq_ref[...] + came_ref[:, 0:DH]) * SCALE
    above, below = beside((edge_ref[...] + came_ref[:, DH:]) * SCALE, first)
    lane = lax.broadcasted_iota(jnp.int32, (HEADS, 24, 128), 2)
    edges = jnp.where(lane % 32 < COLS, above, below)
    lanes = jnp.zeros((128, 128 - DH), f32)
    row = lax.broadcasted_iota(jnp.int32, (HEADS, CELLS, 128), 1)

    def cells(ref, part):
        rows = ref[...].astype(f32)[part * DH : (part + 1) * DH].T
        return jnp.concatenate([rows, lanes], axis=1).reshape(HEADS, CELLS, 128)

    both = []
    for part in (0, 1):
        above, below = beside(cells(other_ref, part), first)
        half = CELLS // 2
        near = jnp.where(row < half, pltpu.roll(above, half, 1), pltpu.roll(below, half, 1))
        both.append(jnp.concatenate([cells(keys_ref, part), near], axis=1))
    dk, dv = both
    lane = lax.broadcasted_iota(jnp.int32, dk.shape, 2)
    mixed = jnp.where(lane < DH, dk, pltpu.roll(dv, DH, 2))
    rest = pltpu.roll(dv, REST - (128 - DH), 2)
    rest = jnp.concatenate([rest, jnp.zeros((HEADS, 8, 128), f32)], axis=1)
    lane = lax.broadcasted_iota(jnp.int32, edges.shape, 2)
    edges = jnp.where(lane < REST, edges, rest)
    send_ref[...] = jnp.concatenate([dq, edges, mixed], axis=1).astype(bf16)


def weights_kernel(patch_ref, qkv_ref, out_ref):
    for part in range(3):
        cols = slice(part * D, (part + 1) * D)
        both = jnp.dot(patch_ref[...], qkv_ref[:, cols], preferred_element_type=f32)
        both = both.reshape(16, 2, 8, D)
        left, right = both[:, 0].reshape(128, D), both[:, 1].reshape(128, D)
        outer = lax.broadcasted_iota(jnp.int32, (128, D), 0) % 8 < 4
        for at, rows in ((0, jnp.where(outer, left, right)), (256, jnp.where(outer, right, left))):
            high, low = split(rows)
            out_ref[at : at + 128, cols] = high
            out_ref[at + 128 : at + 256, cols] = low


def split(x):
    high = x.astype(bf16)
    return high, (x - high.astype(f32)).astype(bf16)


def iota(shape, dim):
    return lax.broadcasted_iota(jnp.int32, shape, dim)


def one_hot(where, value=1.0):
    return jnp.where(where, value, 0.0).astype(bf16)


def turn(weights, joined, pooled):
    def product(rows, values):
        out = jnp.dot(rows, values, preferred_element_type=f32)
        return out[0:128] + out[128:256]

    patch = product(weights[:, 0:D], joined)
    cells = jnp.concatenate(split(product(weights[:, D:], pooled)), axis=1)
    cell, token = iota((256, 256), 0) % 16, iota((256, 256), 1)
    mine = token // (POOL * COLS) * 4 + token % COLS // POOL
    beyond = CELLS + (token - TOK) // COLS * 4 + token % COLS // POOL
    holds = (cell == jnp.where(token < TOK, mine, beyond)) & (token < EXTENDED)
    patch = patch + jnp.dot(cells, one_hot(holds, 1.0 / POOL**2), preferred_element_type=f32)
    to, token = iota((EXTENDED, 256), 0), iota((EXTENDED, 256), 1)
    source = jnp.where(to < TOK, to % 8 * COLS, TOK + to % 2 * COLS) + column_of(to)
    return lax.dot_general(
        one_hot(token == source), jnp.concatenate(split(patch)), NT, preferred_element_type=f32
    )


def embed_kernel(back_ref, weights, turned_ref, joined, pooled, near_out, far_out, sheet):
    for h in range(0, HEADS, 2):
        pair = []
        wide = []
        for n in (h, h + 1):
            pair.append(back_ref[n, 0:TOK].astype(f32)[0:DH])
            edges = back_ref[n, 64 : 64 + 32].astype(f32)[DH - 64 :]
            wide += [edges, pltpu.roll(edges, 96, 1), pltpu.roll(edges, 64, 1)]
        rows = slice(h * DH, (h + 2) * DH)
        joined[rows, 0:TOK] = jnp.concatenate(pair).astype(bf16)
        joined[rows, TOK:] = jnp.concatenate(wide).astype(bf16)
    group = iota((DH, 128), 1) // 16
    fits = 128 - DH
    lane = iota((16, 128), 1)
    for h in range(0, HEADS, 4):
        keys, vals = [], []
        for n in range(h, h + 4):
            rest = back_ref[n, 64 : 64 + 32].astype(f32)[8 : 8 + 16]
            mixed = back_ref[n, 96:112].astype(f32)
            keys.append(mixed)
            vals.append(jnp.where(lane < fits, pltpu.roll(mixed, fits, 1), pltpu.roll(rest, 128 - (REST - fits), 1)))
        cells = keys + vals
        cells = jnp.concatenate(cells).T[0:DH]
        for part in (0, 1):
            for n in (0, 2):
                two = [jnp.where(group == 4 * part + k, cells, 0.0) for k in (n, n + 1)]
                rows = part * D + (h + n) * DH
                pooled[rows : rows + 2 * DH] = jnp.concatenate(two).astype(bf16)
    turned = turn(weights[0:256], joined[...], pooled[...])
    turned_ref[...] = turned.astype(bf16)
    left = right = turned[:, 0:128] + turned[:, 128:256]
    lane = iota((8, 128), 1)
    own = jnp.where(lane % 8 < 4, left[0:ROWS], right[TOK - ROWS : TOK])
    beyond = jnp.where(lane % 8 < 4, left[TOK : TOK + 8], pltpu.roll(right[EXTENDED - 8 :], 2, 0))
    sheet[...] = jnp.zeros_like(sheet)
    for u in range(16):
        sheet[pl.ds(u, ROWS, stride=8), :] += pltpu.roll(own, (128 - 8 * u) % 128, 1)
        if u >= 12:
            sheet[u - 8 : u - 7, :] += pltpu.roll(beyond, 128 - 8 * u, 1)[0:1]
        if u < 4:
            sheet[64 + u : 65 + u, :] += pltpu.roll(beyond, (128 - 8 * u) % 128, 1)[1:2]
    edges = sheet[4:68].T
    begins = lax.axis_index("yl") == 0
    near_out[...] = jnp.where(begins, edges[4:8], edges[0:4])
    far_out[...] = jnp.where(begins, edges[0:4], edges[4:8])


def column_of(row):
    far = row - TOK
    return jnp.where(row < TOK, row // 8, far // 8 * 4 + far % 8 // 2)


def fold_kernel(outer_ref, weights, joined, pooled, center_ref, sheet):
    outer = outer_ref[...].astype(f32)
    inner = turn(weights[256:512], joined[...], pooled[...])
    low_half = iota(outer.shape, 1) % 8 < 4
    halves = [jnp.where(low_half, outer, inner), jnp.where(low_half, inner, outer)]
    halves = [half.astype(bf16) for half in halves]
    sheet[...] = jnp.zeros_like(sheet)
    here = iota((EXTENDED, 256), 1) % 128 // 8 == column_of(iota((EXTENDED, 256), 0))
    to, at = iota((256, 256), 1), iota((256, 256), 0) % 128
    for pair in range(8):
        tile = one_hot((to // 128 + 2 * pair == at // 8) & (to % 8 == at % 8))
        for side in (0, 1):
            wide = jnp.dot(halves[side], tile, preferred_element_type=f32)
            wide = jnp.where(here, wide, 0.0)
            own = jnp.sum(wide[0:TOK].reshape(COLS, ROWS, 256), axis=0)
            edge = jnp.sum(wide[TOK:].reshape(4, 8, 256), axis=0)
            edge = edge + pltpu.roll(edge, 4, 0)
            edge = edge + pltpu.roll(edge, 2, 0)
            for k in (0, 1):
                u = 2 * pair + k
                lanes = slice(k * 128, (k + 1) * 128)
                sheet[side, pl.ds(u, ROWS, stride=8), :] += own[:, lanes]
                if u >= 12:
                    sheet[side, u - 8 : u - 7, :] += edge[0:1, lanes]
                if u < 4:
                    sheet[side, 64 + u : 65 + u, :] += edge[1:2, lanes]
    left = sheet[0, 4:68]
    right = sheet[1, 4:68]
    lane = lax.broadcasted_iota(jnp.int32, left.shape, 1)
    center = jnp.where(lane < 124, pltpu.roll(left, 124, 1), 0.0)
    center_ref[...] = center + jnp.where(lane >= 4, pltpu.roll(right, 4, 1), 0.0)


def cols_kernel(center_ref, near_ref, far_ref, out_ref):
    begins = lax.axis_index("yl") == 0
    left = jnp.where(begins, far_ref[...], near_ref[...])
    right = jnp.where(begins, near_ref[...], far_ref[...])
    quiet = jnp.zeros((120, 64), f32)
    out_ref[...] = center_ref[...] + jnp.concatenate([left, quiet, right]).T


def swapped(x, axis, by):
    peers = lax.axis_size(axis)
    return lax.ppermute(x, axis, [(i, i ^ by) for i in range(peers)])


def neighbours(x, axis):
    peers = lax.axis_size(axis)
    pairs = [(i, i + 1) for i in range(1, peers - 1, 2)]
    return lax.ppermute(x, axis, pairs + [(target, source) for source, target in pairs])


def cost(products):
    flops = products * 4 * QUERIES * HALF * 256
    return pl.CostEstimate(flops=flops, bytes_accessed=2**20, transcendentals=2 * QUERIES * HALF)


def on_device(queries, key_states, values, saved_out, grad_out, w_qkv, w_patch):
    tokens = pltpu.VMEM((TOK, D), bf16)
    cells = pltpu.VMEM((2, 4, D), bf16)
    packed = (HEADS, 2 * FPAD + 16, TOK)
    dma = pltpu.SemaphoreType.DMA
    send = call(
        pack_kernel,
        jax.ShapeDtypeStruct(packed, bf16),
        None,
        [tokens, tokens, tokens, cells, cells, pltpu.VMEM(packed, bf16), dma((14,)), dma((4,))],
        [ANYWHERE] * 5,
        out_specs=ANYWHERE,
    )(
        queries.reshape(TOK, D),
        grad_out.reshape(TOK, D),
        saved_out.reshape(TOK, D),
        key_states,
        values,
    )
    got = lax.all_to_all(send, HEAD_AXES, 0, 0, tiled=True)
    kv = call(
        keys_kernel,
        jax.ShapeDtypeStruct((2 * DH, 128), bf16),
        4,
        [pltpu.VMEM((HEADS, 16, 128), bf16), dma(())],
        [ANYWHERE],
    )(got)
    kv_1, kv_2, kv_6 = [swapped(kv, "z", by) for by in (1, 2, 6)]
    kv_37 = swapped(jnp.stack([kv_2, kv_6]), "z", 1)
    kv_45 = swapped(jnp.stack([kv, kv_1]), "z", 4)
    there = swapped(got, "c", 1)
    sums = jax.ShapeDtypeStruct((2, HEADS, TOK), f32)
    keys = pltpu.VMEM((HALF, 128), bf16)
    mine = call(first_sums_kernel, sums, 24, [keys], cost_estimate=cost(1))(got, there, kv, kv_1, kv_2, kv_6)
    kv_37, kv_45, mine = lax.optimization_barrier((kv_37, kv_45, mine))
    mine = call(second_sums_kernel, sums, 24, [keys], cost_estimate=cost(1))(got, there, kv_37, kv_45, mine)
    mine, kv_45 = lax.optimization_barrier((mine, kv_45))
    came = swapped(mine, "c", 1)
    layout = [jax.ShapeDtypeStruct(shape, bf16) for shape in ((HALF, 128), (FPAD, HALF), (HALF, 128))]
    layouts = call(layouts_kernel, layout * 2, 8, cost_estimate=SMALL)(kv, kv_1, kv_2, kv_6, kv_37, kv_45)
    came, layouts = lax.optimization_barrier((came, layouts))
    scratch = [pltpu.VMEM((HALF, 128), f32)] * 2
    dq = [jax.ShapeDtypeStruct((HEADS, FPAD, TOK), f32)] * 2
    block = (4, 2 * DH, 128)
    sums, dq_here, dq_there, grads = call(
        first_kernel, [sums] + dq + [jax.ShapeDtypeStruct(block, bf16)], 32, scratch, cost_estimate=cost(5)
    )(got, there, *layouts[:3], mine, came)
    came = swapped(grads, "z", 1)
    shapes = [jax.ShapeDtypeStruct((HEADS, rows, TOK), f32) for rows in (DH, 24, DH + 24)]
    *dq, grads = call(
        second_kernel,
        shapes + [jax.ShapeDtypeStruct(block, f32)],
        32,
        scratch,
        cost_estimate=cost(5),
    )(got, there, *layouts[3:], sums, dq_here, dq_there)
    dq, grads, came = lax.optimization_barrier((dq, grads, came))
    dq_here, edges, away = dq
    away = swapped(away, "c", 1)
    mine = grads + came.astype(f32)
    mine, w_qkv, w_patch = lax.optimization_barrier((mine, w_qkv, w_patch))
    came = [swapped(mine[n + 1].astype(bf16), "z", by) for n, by in enumerate(EVEN)]
    weights = call(
        weights_kernel, jax.ShapeDtypeStruct((512, 3 * D), bf16), 24, cost_estimate=SMALL
    )(w_patch, w_qkv)
    came, weights = lax.optimization_barrier((came, weights))
    keys = call(keys_sum_kernel, jax.ShapeDtypeStruct((2 * DH, 128), bf16), 4)(mine[0:1], *came)
    other = swapped(keys, "c", 1)
    send = call(pack_back_kernel, jax.ShapeDtypeStruct((HEADS, 112, TOK), bf16), 16)(
        dq_here, edges, away, keys, other
    )
    back = lax.all_to_all(send, HEAD_AXES, 0, 0, tiled=True)
    strip = jax.ShapeDtypeStruct((4, 64), f32)
    shapes = [(EXTENDED, 256), (D, 2 * TOK), (2 * D, 128)]
    *parts, to_near, to_far = call(
        embed_kernel,
        [jax.ShapeDtypeStruct(shape, bf16) for shape in shapes] + [strip, strip],
        28,
        [pltpu.VMEM((72, 128), f32)],
    )(back, weights)
    near, far = swapped(to_near, "yl", 1), neighbours(to_far, COL)
    center = call(
        fold_kernel,
        jax.ShapeDtypeStruct((64, 128), f32),
        20,
        [pltpu.VMEM((2, 72, 128), f32)],
        cost_estimate=SMALL,
    )(parts[0], weights, *parts[1:])
    near, far, center = lax.optimization_barrier((near, far, center))
    return call(cols_kernel, jax.ShapeDtypeStruct((64, 128), f32), 4)(center, near, far)


def solution(mesh):
    fine = Mesh(mesh.devices.reshape(2, 4, 2, 8, 2), ("yh", "x", "c", "z", "yl"))
    split = P(BLK, COL, None)
    return jax.shard_map(
        on_device,
        mesh=fine,
        in_specs=(split, split, split, split, split, P(), P()),
        out_specs=P(BLK, COL),
        check_vma=False,
    )
```

```python
import math

import jax
import jax.numpy as jnp
from jax import lax
from jax.experimental import pallas as pl
from jax.experimental.pallas import tpu as pltpu
from jax.sharding import Mesh, PartitionSpec as P

D = 1152
HEADS = 16
DH = D // HEADS
POOL = 4
SCALE = DH**-0.5
SCALE2 = SCALE * math.log2(math.e)
ROWS, COLS = 8, 16
TOK = ROWS * COLS
CELLS = TOK // POOL**2
EXTENDED = TOK + 2 * COLS
FPAD = 80
QUERIES = 2048
HALF = 512
TILE = 2 * QUERIES
STEP = 256
HEAD_AXES = ("yh", "x", "yl")
BLK = ("yh", "x", "c")
EVEN = (2, 6, 4)
COL = ("z", "yl")
REST = 96
NT = (((1,), (1,)), ((), ()))
SMALL = pl.CostEstimate(flops=2**20, bytes_accessed=2**16, transcendentals=0)
WHOLE = pl.BlockSpec(memory_space=pltpu.VMEM)
ANYWHERE = pl.BlockSpec(memory_space=pl.ANY)
bf16, f32 = jnp.bfloat16, jnp.float32


def call(kernel, out, mib, scratch=(), specs=None, **more):
    if specs is not None:
        more["in_specs"] = specs
    return pl.pallas_call(
        kernel,
        out_shape=out,
        scratch_shapes=scratch,
        compiler_params=pltpu.CompilerParams(vmem_limit_bytes=mib * 2**20 if mib else None),
        **more,
    )


def pack_kernel(
    q_in, g_in, o_in, k_in, v_in, out_ref, q_ref, g_ref, o_ref, k_ref, v_ref, send_ref, sems, out_sems
):
    pairs = [(k_in, k_ref), (v_in, v_ref)]
    quarter = TOK // 4
    for source, target in ((q_in, q_ref), (g_in, g_ref), (o_in, o_ref)):
        for at in range(0, TOK, quarter):
            pairs.append((source.at[at : at + quarter], target.at[at : at + quarter]))
    copies = [pltpu.make_async_copy(*pair, sems.at[n]) for n, pair in enumerate(pairs)]
    for copy in copies:
        copy.start()
    for copy in copies[:6]:
        copy.wait()
    q_t = q_ref[...].astype(f32).T
    keys = jnp.concatenate([k_ref[0].astype(f32), k_ref[1].astype(f32)])
    vals = jnp.concatenate([v_ref[0].astype(f32), v_ref[1].astype(f32)])
    lanes = jnp.zeros((CELLS, 128 - DH), f32)
    for h in range(HEADS):
        part = slice(h * DH, (h + 1) * DH)
        send_ref[h, 0:FPAD, :] = jnp.concatenate([q_t[part], jnp.zeros((8, TOK), f32)]).astype(bf16)
        k_h = jnp.concatenate([keys[:, part], lanes], axis=1)
        v_h = jnp.concatenate([vals[:, part], lanes], axis=1)
        send_ref[h, 2 * FPAD : 2 * FPAD + 16, :] = jnp.concatenate([k_h, v_h]).astype(bf16)
    outs = []

    def put(heads, rows):
        place = (heads, rows)
        copy = pltpu.make_async_copy(send_ref.at[place], out_ref.at[place], out_sems.at[len(outs)])
        copy.start()
        outs.append(copy)

    put(slice(0, HEADS), slice(0, FPAD))
    put(slice(0, HEADS), slice(2 * FPAD, 2 * FPAD + 16))
    for copy in copies[6:]:
        copy.wait()
    g_t = g_ref[...].astype(f32).T
    prod = g_t * o_ref[...].astype(f32).T
    row = lax.broadcasted_iota(jnp.int32, (8, TOK), 0)
    for h in range(HEADS):
        part = slice(h * DH, (h + 1) * DH)
        dot = -jnp.sum(prod[part], axis=0, keepdims=True)
        high = dot.astype(bf16).astype(f32)
        mid = (dot - high).astype(bf16).astype(f32)
        low = dot - high - mid
        dots = jnp.where(row == 0, high, jnp.where(row == 1, mid, jnp.where(row == 2, low, 0.0)))
        send_ref[h, FPAD : 2 * FPAD, :] = jnp.concatenate([g_t[part], dots]).astype(bf16)
        if h % 4 == 3:
            put(slice(h - 3, h + 1), slice(FPAD, 2 * FPAD))
    for copy in outs:
        copy.wait()


def keys_kernel(got_ref, out_ref, kv_ref, sem):
    copy = pltpu.make_async_copy(got_ref.at[:, 2 * FPAD : 2 * FPAD + 16], kv_ref, sem)
    copy.start()
    copy.wait()
    kv = kv_ref[...].astype(f32).reshape(HEADS, 2, CELLS, 128)
    k_t = kv[:, 0].reshape(128, 128).T
    v_t = kv[:, 1].reshape(128, 128).T
    out_ref[...] = jnp.concatenate([k_t[0:DH], v_t[0:DH]]).astype(bf16)


def key_rows(kv):
    return jnp.concatenate([kv.astype(f32)[0:DH], jnp.zeros((128 - DH, 128), f32)])


def load_keys(blocks, k_s):
    norms = jnp.zeros((1, 128), f32)
    for b, block in enumerate(blocks):
        k_t = key_rows(block)
        norms = jnp.maximum(norms, jnp.sum(k_t * k_t, axis=0, keepdims=True))
        k_s[b * 128 : (b + 1) * 128] = k_t.T.astype(bf16)
    return jnp.max(norms)


def layouts_kernel(kv_0, kv_1, kv_2, kv_6, kv_37, kv_45, k_odd, kt_odd, v_odd, k_even, kt_even, v_even):
    odd = (kv_1[...], kv_37[0], kv_37[1], kv_45[1]), k_odd, kt_odd, v_odd
    even = (kv_0[...], kv_2[...], kv_6[...], kv_45[0]), k_even, kt_even, v_even
    lane = lax.broadcasted_iota(jnp.int32, (128, 128), 1)
    pad = jnp.zeros((128 - DH, 128), f32)
    for blocks, k_ref, kt_ref, v_ref in (odd, even):
        for b, block in enumerate(blocks):
            keys = slice(b * 128, (b + 1) * 128)
            k_t = key_rows(block)
            k_ref[keys] = k_t.T.astype(bf16)
            kt_ref[:, keys] = k_t[0:FPAD].astype(bf16)
            v = jnp.concatenate([block.astype(f32)[DH:], pad]).T
            v_ref[keys] = jnp.where((lane >= DH) & (lane < DH + 3), 1.0, v).astype(bf16)


def tile_of(qg_refs, row):
    blocks = [qg_ref[n, row : row + FPAD] for qg_ref in qg_refs for n in range(HEADS)]
    return jnp.concatenate(blocks, axis=1)


def log_sums(q_t, k_s, norm):
    exact = q_t.astype(f32)
    bound = jnp.sqrt(jnp.sum(exact * exact, axis=0, keepdims=True) * norm) * (SCALE2 * 1.001)

    def scores(rows):
        return jnp.dot(k_s[rows, 0:FPAD], q_t, preferred_element_type=f32) * SCALE2

    total = jnp.zeros((1, TILE), f32)
    count = k_s.shape[0]
    for at in range(0, count, STEP):
        exps = jnp.exp2(scores(slice(at, at + STEP)) - bound)
        total = total + jnp.sum(exps, axis=0, keepdims=True)

    def again():
        def rows(n):
            return pl.ds(pl.multiple_of(n * 128, 128), 128)

        def largest(n, top):
            return jnp.maximum(top, jnp.max(scores(rows(n)), axis=0, keepdims=True))

        top = lax.fori_loop(0, count // 128, largest, jnp.full((1, TILE), -jnp.inf, f32))

        def add(n, total):
            return total + jnp.sum(jnp.exp2(scores(rows(n)) - top), axis=0, keepdims=True)

        return top + jnp.log2(lax.fori_loop(0, count // 128, add, jnp.zeros((1, TILE), f32)))

    return lax.cond(jnp.min(total) < 2.0**-90, again, lambda: bound + jnp.log2(total))


def put_sums(out_ref, sums):
    rows = [sums[:, n * TOK : (n + 1) * TOK] for n in range(2 * HEADS)]
    out_ref[...] = jnp.concatenate(rows).reshape(2, HEADS, TOK)


def get_sums(sums_ref):
    rows = sums_ref[...].reshape(2 * HEADS, TOK)
    return jnp.concatenate([rows[n : n + 1] for n in range(2 * HEADS)], axis=1)


def added(one, two):
    top = jnp.maximum(one, two)
    return top + jnp.log2(jnp.exp2(one - top) + jnp.exp2(two - top))


def first_sums_kernel(qg_a, qg_b, kv_0, kv_1, kv_2, kv_6, out_ref, k_s):
    norm = load_keys((kv_0[...], kv_1[...], kv_2[...], kv_6[...]), k_s)
    put_sums(out_ref, log_sums(tile_of((qg_a, qg_b), 0), k_s, norm))


def second_sums_kernel(qg_a, qg_b, kv_37, kv_45, first_ref, out_ref, k_s):
    norm = load_keys((kv_37[0], kv_37[1], kv_45[0], kv_45[1]), k_s)
    mine = log_sums(tile_of((qg_a, qg_b), 0), k_s, norm)
    put_sums(out_ref, added(mine, get_sums(first_ref)))


def gradients(sums_ref, qg_refs, put_dq, k_s, kt_s, v_s, dk_s, dv_s):
    q_t = tile_of(qg_refs, 0)
    g_t = tile_of(qg_refs, FPAD)
    sums = get_sums(sums_ref)
    dq = jnp.zeros((FPAD, TILE), f32)
    for at in range(0, HALF, STEP):
        b = slice(at, at + STEP)
        scores = jnp.dot(k_s[b, 0:FPAD], q_t, preferred_element_type=f32)
        probs = jnp.exp2(scores * SCALE2 - sums)
        half_probs = probs.astype(bf16)
        shifted = jnp.dot(v_s[b, 0:FPAD], g_t, preferred_element_type=f32)
        ds = (probs * shifted).astype(bf16)
        dk_s[b, 0:FPAD] = lax.dot_general(ds, q_t, NT, preferred_element_type=f32)
        dv_s[b, 0:FPAD] = lax.dot_general(half_probs, g_t, NT, preferred_element_type=f32)
        dq = dq + jnp.dot(kt_s[:, b], ds, preferred_element_type=f32)
    for n in range(2 * HEADS):
        put_dq(n // HEADS, n % HEADS, dq[:, n * TOK : (n + 1) * TOK])


def put_keys(out_ref, dk_s, dv_s):
    dk_t = dk_s[...].T
    dv_t = dv_s[...].T
    for b in range(4):
        keys = slice(b * 128, (b + 1) * 128)
        block = jnp.concatenate([dk_t[0:DH, keys] * SCALE, dv_t[0:DH, keys]])
        out_ref[b] = block.astype(out_ref.dtype)


def first_kernel(
    qg_a, qg_b, k_s, kt_s, v_s, mine_ref, came_ref, sums_ref, dq_a, dq_b, out_ref, dk_s, dv_s
):
    for at in (0, 1):
        sums_ref[at] = added(mine_ref[at], came_ref[1 - at])

    def put_dq(at, n, dq):
        (dq_a, dq_b)[at][n] = dq

    gradients(sums_ref, (qg_a, qg_b), put_dq, k_s, kt_s, v_s, dk_s, dv_s)
    put_keys(out_ref, dk_s, dv_s)


def edge_rows(dq):
    lane = lax.broadcasted_iota(jnp.int32, (24, TOK), 1)
    edges = pltpu.roll(dq[0:24], COLS, 1)
    for n in (1, 2):
        rolled = pltpu.roll(dq[24 * n : 24 * (n + 1)], COLS + 32 * n, 1)
        edges = jnp.where(lane < 32 * n, edges, rolled)
    return edges


def second_kernel(
    qg_a, qg_b, k_s, kt_s, v_s, sums_ref, in_a, in_b, here_ref, edge_ref, away_ref, out_ref, dk_s, dv_s
):
    def put_dq(at, n, dq):
        dq = (in_a, in_b)[at][n] + dq
        edges = edge_rows(dq)
        if at == 0:
            here_ref[n] = dq[0:DH]
            away_ref[n, DH:] = edges
        else:
            away_ref[n, 0:DH] = dq[0:DH]
            edge_ref[n] = edges

    gradients(sums_ref, (qg_a, qg_b), put_dq, k_s, kt_s, v_s, dk_s, dv_s)
    put_keys(out_ref, dk_s, dv_s)


def keys_sum_kernel(mine_ref, came_a, came_b, came_c, out_ref):
    total = mine_ref[0]
    for came in (came_a, came_b, came_c):
        total = total + came[...].astype(f32)
    out_ref[...] = total.astype(bf16)


def beside(x, first):
    none = jnp.zeros_like(x[0:2])
    above = jnp.where(first, jnp.concatenate([none, x[:-2]]), x)
    below = jnp.where(first, x, jnp.concatenate([x[2:], none]))
    return above, below


def pack_back_kernel(dq_ref, edge_ref, came_ref, keys_ref, other_ref, send_ref):
    first = lax.axis_index("c") == 0
    dq = (dq_ref[...] + came_ref[:, 0:DH]) * SCALE
    above, below = beside((edge_ref[...] + came_ref[:, DH:]) * SCALE, first)
    lane = lax.broadcasted_iota(jnp.int32, (HEADS, 24, 128), 2)
    edges = jnp.where(lane % 32 < COLS, above, below)
    lanes = jnp.zeros((128, 128 - DH), f32)
    row = lax.broadcasted_iota(jnp.int32, (HEADS, CELLS, 128), 1)

    def cells(ref, part):
        rows = ref[...].astype(f32)[part * DH : (part + 1) * DH].T
        return jnp.concatenate([rows, lanes], axis=1).reshape(HEADS, CELLS, 128)

    both = []
    for part in (0, 1):
        above, below = beside(cells(other_ref, part), first)
        half = CELLS // 2
        near = jnp.where(row < half, pltpu.roll(above, half, 1), pltpu.roll(below, half, 1))
        both.append(jnp.concatenate([cells(keys_ref, part), near], axis=1))
    dk, dv = both
    lane = lax.broadcasted_iota(jnp.int32, dk.shape, 2)
    mixed = jnp.where(lane < DH, dk, pltpu.roll(dv, DH, 2))
    rest = pltpu.roll(dv, REST - (128 - DH), 2)
    rest = jnp.concatenate([rest, jnp.zeros((HEADS, 8, 128), f32)], axis=1)
    lane = lax.broadcasted_iota(jnp.int32, edges.shape, 2)
    edges = jnp.where(lane < REST, edges, rest)
    send_ref[...] = jnp.concatenate([dq, edges, mixed], axis=1).astype(bf16)


def weights_kernel(patch_ref, qkv_ref, out_ref):
    for part in range(3):
        cols = slice(part * D, (part + 1) * D)
        both = jnp.dot(patch_ref[...], qkv_ref[:, cols], preferred_element_type=f32)
        both = both.reshape(16, 2, 8, D)
        left, right = both[:, 0].reshape(128, D), both[:, 1].reshape(128, D)
        outer = lax.broadcasted_iota(jnp.int32, (128, D), 0) % 8 < 4
        for at, rows in ((0, jnp.where(outer, left, right)), (256, jnp.where(outer, right, left))):
            high, low = split(rows)
            out_ref[at : at + 128, cols] = high
            out_ref[at + 128 : at + 256, cols] = low


def split(x):
    high = x.astype(bf16)
    return high, (x - high.astype(f32)).astype(bf16)


def iota(shape, dim):
    return lax.broadcasted_iota(jnp.int32, shape, dim)


def one_hot(where, value=1.0):
    return jnp.where(where, value, 0.0).astype(bf16)


def turn(weights, joined, pooled):
    def product(rows, values):
        out = jnp.dot(rows, values, preferred_element_type=f32)
        return out[0:128] + out[128:256]

    patch = product(weights[:, 0:D], joined)
    cells = jnp.concatenate(split(product(weights[:, D:], pooled)), axis=1)
    cell, token = iota((256, 256), 0) % 16, iota((256, 256), 1)
    mine = token // (POOL * COLS) * 4 + token % COLS // POOL
    beyond = CELLS + (token - TOK) // COLS * 4 + token % COLS // POOL
    holds = (cell == jnp.where(token < TOK, mine, beyond)) & (token < EXTENDED)
    patch = patch + jnp.dot(cells, one_hot(holds, 1.0 / POOL**2), preferred_element_type=f32)
    to, token = iota((EXTENDED, 256), 0), iota((EXTENDED, 256), 1)
    source = jnp.where(to < TOK, to % 8 * COLS, TOK + to % 2 * COLS) + column_of(to)
    return lax.dot_general(
        one_hot(token == source), jnp.concatenate(split(patch)), NT, preferred_element_type=f32
    )


def embed_kernel(back_ref, weights, turned_ref, joined, pooled, near_out, far_out, sheet):
    for h in range(0, HEADS, 2):
        pair = []
        wide = []
        for n in (h, h + 1):
            pair.append(back_ref[n, 0:TOK].astype(f32)[0:DH])
            edges = back_ref[n, 64 : 64 + 32].astype(f32)[DH - 64 :]
            wide += [edges, pltpu.roll(edges, 96, 1), pltpu.roll(edges, 64, 1)]
        rows = slice(h * DH, (h + 2) * DH)
        joined[rows, 0:TOK] = jnp.concatenate(pair).astype(bf16)
        joined[rows, TOK:] = jnp.concatenate(wide).astype(bf16)
    group = iota((DH, 128), 1) // 16
    fits = 128 - DH
    lane = iota((16, 128), 1)
    for h in range(0, HEADS, 4):
        keys, vals = [], []
        for n in range(h, h + 4):
            rest = back_ref[n, 64 : 64 + 32].astype(f32)[8 : 8 + 16]
            mixed = back_ref[n, 96:112].astype(f32)
            keys.append(mixed)
            vals.append(jnp.where(lane < fits, pltpu.roll(mixed, fits, 1), pltpu.roll(rest, 128 - (REST - fits), 1)))
        cells = keys + vals
        cells = jnp.concatenate(cells).T[0:DH]
        for part in (0, 1):
            for n in (0, 2):
                two = [jnp.where(group == 4 * part + k, cells, 0.0) for k in (n, n + 1)]
                rows = part * D + (h + n) * DH
                pooled[rows : rows + 2 * DH] = jnp.concatenate(two).astype(bf16)
    turned = turn(weights[0:256], joined[...], pooled[...])
    turned_ref[...] = turned.astype(bf16)
    left = right = turned[:, 0:128] + turned[:, 128:256]
    lane = iota((8, 128), 1)
    own = jnp.where(lane % 8 < 4, left[0:ROWS], right[TOK - ROWS : TOK])
    beyond = jnp.where(lane % 8 < 4, left[TOK : TOK + 8], pltpu.roll(right[EXTENDED - 8 :], 2, 0))
    sheet[...] = jnp.zeros_like(sheet)
    for u in range(16):
        sheet[pl.ds(u, ROWS, stride=8), :] += pltpu.roll(own, (128 - 8 * u) % 128, 1)
        if u >= 12:
            sheet[u - 8 : u - 7, :] += pltpu.roll(beyond, 128 - 8 * u, 1)[0:1]
        if u < 4:
            sheet[64 + u : 65 + u, :] += pltpu.roll(beyond, (128 - 8 * u) % 128, 1)[1:2]
    edges = sheet[4:68].T
    begins = lax.axis_index("yl") == 0
    near_out[...] = jnp.where(begins, edges[4:8], edges[0:4])
    far_out[...] = jnp.where(begins, edges[0:4], edges[4:8])


def column_of(row):
    far = row - TOK
    return jnp.where(row < TOK, row // 8, far // 8 * 4 + far % 8 // 2)


def fold_kernel(outer_ref, weights, joined, pooled, center_ref, sheet):
    outer = outer_ref[...].astype(f32)
    inner = turn(weights[256:512], joined[...], pooled[...])
    low_half = iota(outer.shape, 1) % 8 < 4
    halves = [jnp.where(low_half, outer, inner), jnp.where(low_half, inner, outer)]
    halves = [half.astype(bf16) for half in halves]
    sheet[...] = jnp.zeros_like(sheet)
    here = iota((EXTENDED, 256), 1) % 128 // 8 == column_of(iota((EXTENDED, 256), 0))
    to, at = iota((256, 256), 1), iota((256, 256), 0) % 128
    for pair in range(8):
        tile = one_hot((to // 128 + 2 * pair == at // 8) & (to % 8 == at % 8))
        for side in (0, 1):
            wide = jnp.dot(halves[side], tile, preferred_element_type=f32)
            wide = jnp.where(here, wide, 0.0)
            own = jnp.sum(wide[0:TOK].reshape(COLS, ROWS, 256), axis=0)
            edge = jnp.sum(wide[TOK:].reshape(4, 8, 256), axis=0)
            edge = edge + pltpu.roll(edge, 4, 0)
            edge = edge + pltpu.roll(edge, 2, 0)
            for k in (0, 1):
                u = 2 * pair + k
                lanes = slice(k * 128, (k + 1) * 128)
                sheet[side, pl.ds(u, ROWS, stride=8), :] += own[:, lanes]
                if u >= 12:
                    sheet[side, u - 8 : u - 7, :] += edge[0:1, lanes]
                if u < 4:
                    sheet[side, 64 + u : 65 + u, :] += edge[1:2, lanes]
    left = sheet[0, 4:68]
    right = sheet[1, 4:68]
    lane = lax.broadcasted_iota(jnp.int32, left.shape, 1)
    center = jnp.where(lane < 124, pltpu.roll(left, 124, 1), 0.0)
    center_ref[...] = center + jnp.where(lane >= 4, pltpu.roll(right, 4, 1), 0.0)


def cols_kernel(center_ref, near_ref, far_ref, out_ref):
    begins = lax.axis_index("yl") == 0
    left = jnp.where(begins, far_ref[...], near_ref[...])
    right = jnp.where(begins, near_ref[...], far_ref[...])
    quiet = jnp.zeros((120, 64), f32)
    out_ref[...] = center_ref[...] + jnp.concatenate([left, quiet, right]).T


def swapped(x, axis, by):
    peers = lax.axis_size(axis)
    return lax.ppermute(x, axis, [(i, i ^ by) for i in range(peers)])


def neighbours(x, axis):
    peers = lax.axis_size(axis)
    pairs = [(i, i + 1) for i in range(1, peers - 1, 2)]
    return lax.ppermute(x, axis, pairs + [(target, source) for source, target in pairs])


def cost(products):
    flops = products * 4 * QUERIES * HALF * 256
    return pl.CostEstimate(flops=flops, bytes_accessed=2**20, transcendentals=2 * QUERIES * HALF)


def on_device(queries, key_states, values, saved_out, grad_out, w_qkv, w_patch):
    tokens = pltpu.VMEM((TOK, D), bf16)
    cells = pltpu.VMEM((2, 4, D), bf16)
    packed = (HEADS, 2 * FPAD + 16, TOK)
    dma = pltpu.SemaphoreType.DMA
    send = call(
        pack_kernel,
        jax.ShapeDtypeStruct(packed, bf16),
        None,
        [tokens, tokens, tokens, cells, cells, pltpu.VMEM(packed, bf16), dma((14,)), dma((6,))],
        [ANYWHERE] * 5,
        out_specs=ANYWHERE,
    )(
        queries.reshape(TOK, D),
        grad_out.reshape(TOK, D),
        saved_out.reshape(TOK, D),
        key_states,
        values,
    )
    got = lax.all_to_all(send, HEAD_AXES, 0, 0, tiled=True)
    kv = call(
        keys_kernel,
        jax.ShapeDtypeStruct((2 * DH, 128), bf16),
        4,
        [pltpu.VMEM((HEADS, 16, 128), bf16), dma(())],
        [ANYWHERE],
    )(got)
    kv_1, kv_2, kv_6 = [swapped(kv, "z", by) for by in (1, 2, 6)]
    kv_37 = swapped(jnp.stack([kv_2, kv_6]), "z", 1)
    kv_45 = swapped(jnp.stack([kv, kv_1]), "z", 4)
    there = swapped(got, "c", 1)
    sums = jax.ShapeDtypeStruct((2, HEADS, TOK), f32)
    keys = pltpu.VMEM((HALF, 128), bf16)
    mine = call(first_sums_kernel, sums, 24, [keys], cost_estimate=cost(1))(got, there, kv, kv_1, kv_2, kv_6)
    kv_37, kv_45, mine = lax.optimization_barrier((kv_37, kv_45, mine))
    mine = call(second_sums_kernel, sums, 24, [keys], cost_estimate=cost(1))(got, there, kv_37, kv_45, mine)
    mine, kv_45 = lax.optimization_barrier((mine, kv_45))
    came = swapped(mine, "c", 1)
    layout = [jax.ShapeDtypeStruct(shape, bf16) for shape in ((HALF, 128), (FPAD, HALF), (HALF, 128))]
    layouts = call(layouts_kernel, layout * 2, 8, cost_estimate=SMALL)(kv, kv_1, kv_2, kv_6, kv_37, kv_45)
    came, layouts = lax.optimization_barrier((came, layouts))
    scratch = [pltpu.VMEM((HALF, 128), f32)] * 2
    dq = [jax.ShapeDtypeStruct((HEADS, FPAD, TOK), f32)] * 2
    block = (4, 2 * DH, 128)
    sums, dq_here, dq_there, grads = call(
        first_kernel, [sums] + dq + [jax.ShapeDtypeStruct(block, bf16)], 32, scratch, cost_estimate=cost(5)
    )(got, there, *layouts[:3], mine, came)
    came = swapped(grads, "z", 1)
    shapes = [jax.ShapeDtypeStruct((HEADS, rows, TOK), f32) for rows in (DH, 24, DH + 24)]
    *dq, grads = call(
        second_kernel,
        shapes + [jax.ShapeDtypeStruct(block, f32)],
        32,
        scratch,
        cost_estimate=cost(5),
    )(got, there, *layouts[3:], sums, dq_here, dq_there)
    dq, grads, came = lax.optimization_barrier((dq, grads, came))
    dq_here, edges, away = dq
    away = swapped(away, "c", 1)
    mine = grads + came.astype(f32)
    mine, w_qkv, w_patch = lax.optimization_barrier((mine, w_qkv, w_patch))
    came = [swapped(mine[n + 1].astype(bf16), "z", by) for n, by in enumerate(EVEN)]
    weights = call(
        weights_kernel, jax.ShapeDtypeStruct((512, 3 * D), bf16), 24, cost_estimate=SMALL
    )(w_patch, w_qkv)
    came, weights = lax.optimization_barrier((came, weights))
    keys = call(keys_sum_kernel, jax.ShapeDtypeStruct((2 * DH, 128), bf16), 4)(mine[0:1], *came)
    other = swapped(keys, "c", 1)
    send = call(pack_back_kernel, jax.ShapeDtypeStruct((HEADS, 112, TOK), bf16), 16)(
        dq_here, edges, away, keys, other
    )
    back = lax.all_to_all(send, HEAD_AXES, 0, 0, tiled=True)
    strip = jax.ShapeDtypeStruct((4, 64), f32)
    shapes = [(EXTENDED, 256), (D, 2 * TOK), (2 * D, 128)]
    *parts, to_near, to_far = call(
        embed_kernel,
        [jax.ShapeDtypeStruct(shape, bf16) for shape in shapes] + [strip, strip],
        28,
        [pltpu.VMEM((72, 128), f32)],
    )(back, weights)
    near, far = swapped(to_near, "yl", 1), neighbours(to_far, COL)
    center = call(
        fold_kernel,
        jax.ShapeDtypeStruct((64, 128), f32),
        20,
        [pltpu.VMEM((2, 72, 128), f32)],
        cost_estimate=SMALL,
    )(parts[0], weights, *parts[1:])
    near, far, center = lax.optimization_barrier((near, far, center))
    return call(cols_kernel, jax.ShapeDtypeStruct((64, 128), f32), 4)(center, near, far)


def solution(mesh):
    fine = Mesh(mesh.devices.reshape(2, 4, 2, 8, 2), ("yh", "x", "c", "z", "yl"))
    split = P(BLK, COL, None)
    return jax.shard_map(
        on_device,
        mesh=fine,
        in_specs=(split, split, split, split, split, P(), P()),
        out_specs=P(BLK, COL),
        check_vma=False,
    )
```

```python
import math

import jax
import jax.numpy as jnp
from jax import lax
from jax.experimental import pallas as pl
from jax.experimental.pallas import tpu as pltpu
from jax.sharding import Mesh, PartitionSpec as P

D = 1152
HEADS = 16
DH = D // HEADS
POOL = 4
SCALE = DH**-0.5
SCALE2 = SCALE * math.log2(math.e)
ROWS, COLS = 8, 16
TOK = ROWS * COLS
CELLS = TOK // POOL**2
EXTENDED = TOK + 2 * COLS
FPAD = 80
QUERIES = 2048
HALF = 512
TILE = 2 * QUERIES
STEP = 256
HEAD_AXES = ("yh", "x", "yl")
BLK = ("yh", "x", "c")
EVEN = (2, 6, 4)
COL = ("z", "yl")
REST = 96
NT = (((1,), (1,)), ((), ()))
SMALL = pl.CostEstimate(flops=2**20, bytes_accessed=2**16, transcendentals=0)
WHOLE = pl.BlockSpec(memory_space=pltpu.VMEM)
ANYWHERE = pl.BlockSpec(memory_space=pl.ANY)
bf16, f32 = jnp.bfloat16, jnp.float32


def call(kernel, out, mib, scratch=(), specs=None, **more):
    if specs is not None:
        more["in_specs"] = specs
    return pl.pallas_call(
        kernel,
        out_shape=out,
        scratch_shapes=scratch,
        compiler_params=pltpu.CompilerParams(vmem_limit_bytes=mib * 2**20 if mib else None),
        **more,
    )


def pack_kernel(
    q_in, g_in, o_in, k_in, v_in, out_ref, q_ref, g_ref, o_ref, k_ref, v_ref, send_ref, sems, out_sems
):
    pairs = []
    quarter = TOK // 4
    for source, target in ((q_in, q_ref), (g_in, g_ref), (o_in, o_ref)):
        for at in range(0, TOK, quarter):
            pairs.append((source.at[at : at + quarter], target.at[at : at + quarter]))
    pairs[4:4] = [(k_in, k_ref), (v_in, v_ref)]
    copies = [pltpu.make_async_copy(*pair, sems.at[n]) for n, pair in enumerate(pairs)]
    for copy in copies:
        copy.start()
    for copy in copies[:6]:
        copy.wait()
    q_t = q_ref[...].astype(f32).T
    keys = jnp.concatenate([k_ref[0].astype(f32), k_ref[1].astype(f32)])
    vals = jnp.concatenate([v_ref[0].astype(f32), v_ref[1].astype(f32)])
    lanes = jnp.zeros((CELLS, 128 - DH), f32)
    for h in range(HEADS):
        part = slice(h * DH, (h + 1) * DH)
        send_ref[h, 0:FPAD, :] = jnp.concatenate([q_t[part], jnp.zeros((8, TOK), f32)]).astype(bf16)
        k_h = jnp.concatenate([keys[:, part], lanes], axis=1)
        v_h = jnp.concatenate([vals[:, part], lanes], axis=1)
        send_ref[h, 2 * FPAD : 2 * FPAD + 16, :] = jnp.concatenate([k_h, v_h]).astype(bf16)
    outs = []

    def put(heads, rows):
        place = (heads, rows)
        copy = pltpu.make_async_copy(send_ref.at[place], out_ref.at[place], out_sems.at[len(outs)])
        copy.start()
        outs.append(copy)

    put(slice(0, HEADS), slice(0, FPAD))
    put(slice(0, HEADS), slice(2 * FPAD, 2 * FPAD + 16))
    for copy in copies[6:]:
        copy.wait()
    g_t = g_ref[...].astype(f32).T
    prod = g_t * o_ref[...].astype(f32).T
    row = lax.broadcasted_iota(jnp.int32, (8, TOK), 0)
    for h in range(HEADS):
        part = slice(h * DH, (h + 1) * DH)
        dot = -jnp.sum(prod[part], axis=0, keepdims=True)
        high = dot.astype(bf16).astype(f32)
        mid = (dot - high).astype(bf16).astype(f32)
        low = dot - high - mid
        dots = jnp.where(row == 0, high, jnp.where(row == 1, mid, jnp.where(row == 2, low, 0.0)))
        send_ref[h, FPAD : 2 * FPAD, :] = jnp.concatenate([g_t[part], dots]).astype(bf16)
        if h % 4 == 3:
            put(slice(h - 3, h + 1), slice(FPAD, 2 * FPAD))
    for copy in outs:
        copy.wait()


def keys_kernel(got_ref, out_ref, kv_ref, sem):
    copy = pltpu.make_async_copy(got_ref.at[:, 2 * FPAD : 2 * FPAD + 16], kv_ref, sem)
    copy.start()
    copy.wait()
    kv = kv_ref[...].astype(f32).reshape(HEADS, 2, CELLS, 128)
    k_t = kv[:, 0].reshape(128, 128).T
    v_t = kv[:, 1].reshape(128, 128).T
    out_ref[...] = jnp.concatenate([k_t[0:DH], v_t[0:DH]]).astype(bf16)


def key_rows(kv):
    return jnp.concatenate([kv.astype(f32)[0:DH], jnp.zeros((128 - DH, 128), f32)])


def load_keys(blocks, k_s):
    norms = jnp.zeros((1, 128), f32)
    for b, block in enumerate(blocks):
        k_t = key_rows(block)
        norms = jnp.maximum(norms, jnp.sum(k_t * k_t, axis=0, keepdims=True))
        k_s[b * 128 : (b + 1) * 128] = k_t.T.astype(bf16)
    return jnp.max(norms)


def layouts_kernel(kv_0, kv_1, kv_2, kv_6, kv_37, kv_45, k_odd, kt_odd, v_odd, k_even, kt_even, v_even):
    odd = (kv_1[...], kv_37[0], kv_37[1], kv_45[1]), k_odd, kt_odd, v_odd
    even = (kv_0[...], kv_2[...], kv_6[...], kv_45[0]), k_even, kt_even, v_even
    lane = lax.broadcasted_iota(jnp.int32, (128, 128), 1)
    pad = jnp.zeros((128 - DH, 128), f32)
    for blocks, k_ref, kt_ref, v_ref in (odd, even):
        for b, block in enumerate(blocks):
            keys = slice(b * 128, (b + 1) * 128)
            k_t = key_rows(block)
            k_ref[keys] = k_t.T.astype(bf16)
            kt_ref[:, keys] = k_t[0:FPAD].astype(bf16)
            v = jnp.concatenate([block.astype(f32)[DH:], pad]).T
            v_ref[keys] = jnp.where((lane >= DH) & (lane < DH + 3), 1.0, v).astype(bf16)


def tile_of(qg_refs, row):
    blocks = [qg_ref[n, row : row + FPAD] for qg_ref in qg_refs for n in range(HEADS)]
    return jnp.concatenate(blocks, axis=1)


def log_sums(q_t, k_s, norm):
    exact = q_t.astype(f32)
    bound = jnp.sqrt(jnp.sum(exact * exact, axis=0, keepdims=True) * norm) * (SCALE2 * 1.001)

    def scores(rows):
        return jnp.dot(k_s[rows, 0:FPAD], q_t, preferred_element_type=f32) * SCALE2

    total = jnp.zeros((1, TILE), f32)
    count = k_s.shape[0]
    for at in range(0, count, HALF):
        exps = jnp.exp2(scores(slice(at, at + HALF)) - bound)
        total = total + jnp.sum(exps, axis=0, keepdims=True)

    def again():
        def rows(n):
            return pl.ds(pl.multiple_of(n * 128, 128), 128)

        def largest(n, top):
            return jnp.maximum(top, jnp.max(scores(rows(n)), axis=0, keepdims=True))

        top = lax.fori_loop(0, count // 128, largest, jnp.full((1, TILE), -jnp.inf, f32))

        def add(n, total):
            return total + jnp.sum(jnp.exp2(scores(rows(n)) - top), axis=0, keepdims=True)

        return top + jnp.log2(lax.fori_loop(0, count // 128, add, jnp.zeros((1, TILE), f32)))

    return lax.cond(jnp.min(total) < 2.0**-90, again, lambda: bound + jnp.log2(total))


def put_sums(out_ref, sums):
    rows = [sums[:, n * TOK : (n + 1) * TOK] for n in range(2 * HEADS)]
    out_ref[...] = jnp.concatenate(rows).reshape(2, HEADS, TOK)


def get_sums(sums_ref):
    rows = sums_ref[...].reshape(2 * HEADS, TOK)
    return jnp.concatenate([rows[n : n + 1] for n in range(2 * HEADS)], axis=1)


def added(one, two):
    top = jnp.maximum(one, two)
    return top + jnp.log2(jnp.exp2(one - top) + jnp.exp2(two - top))


def first_sums_kernel(qg_a, qg_b, kv_0, kv_1, kv_2, kv_6, out_ref, k_s):
    norm = load_keys((kv_0[...], kv_1[...], kv_2[...], kv_6[...]), k_s)
    put_sums(out_ref, log_sums(tile_of((qg_a, qg_b), 0), k_s, norm))


def second_sums_kernel(qg_a, qg_b, kv_37, kv_45, first_ref, out_ref, k_s):
    norm = load_keys((kv_37[0], kv_37[1], kv_45[0], kv_45[1]), k_s)
    mine = log_sums(tile_of((qg_a, qg_b), 0), k_s, norm)
    put_sums(out_ref, added(mine, get_sums(first_ref)))


def gradients(sums_ref, qg_refs, put_dq, k_s, kt_s, v_s, dk_s, dv_s):
    q_t = tile_of(qg_refs, 0)
    g_t = tile_of(qg_refs, FPAD)
    sums = get_sums(sums_ref)
    dq = jnp.zeros((FPAD, TILE), f32)
    for at in range(0, HALF, STEP):
        b = slice(at, at + STEP)
        scores = jnp.dot(k_s[b, 0:FPAD], q_t, preferred_element_type=f32)
        probs = jnp.exp2(scores * SCALE2 - sums)
        half_probs = probs.astype(bf16)
        shifted = jnp.dot(v_s[b, 0:FPAD], g_t, preferred_element_type=f32)
        ds = (probs * shifted).astype(bf16)
        dk_s[b, 0:FPAD] = lax.dot_general(ds, q_t, NT, preferred_element_type=f32)
        dv_s[b, 0:FPAD] = lax.dot_general(half_probs, g_t, NT, preferred_element_type=f32)
        dq = dq + jnp.dot(kt_s[:, b], ds, preferred_element_type=f32)
    for n in range(2 * HEADS):
        put_dq(n // HEADS, n % HEADS, dq[:, n * TOK : (n + 1) * TOK])


def put_keys(out_ref, dk_s, dv_s):
    dk_t = dk_s[...].T
    dv_t = dv_s[...].T
    for b in range(4):
        keys = slice(b * 128, (b + 1) * 128)
        block = jnp.concatenate([dk_t[0:DH, keys] * SCALE, dv_t[0:DH, keys]])
        out_ref[b] = block.astype(out_ref.dtype)


def first_kernel(
    qg_a, qg_b, k_s, kt_s, v_s, mine_ref, came_ref, sums_ref, dq_a, dq_b, out_ref, dk_s, dv_s
):
    for at in (0, 1):
        sums_ref[at] = added(mine_ref[at], came_ref[1 - at])

    def put_dq(at, n, dq):
        (dq_a, dq_b)[at][n] = dq

    gradients(sums_ref, (qg_a, qg_b), put_dq, k_s, kt_s, v_s, dk_s, dv_s)
    put_keys(out_ref, dk_s, dv_s)


def edge_rows(dq):
    lane = lax.broadcasted_iota(jnp.int32, (24, TOK), 1)
    edges = pltpu.roll(dq[0:24], COLS, 1)
    for n in (1, 2):
        rolled = pltpu.roll(dq[24 * n : 24 * (n + 1)], COLS + 32 * n, 1)
        edges = jnp.where(lane < 32 * n, edges, rolled)
    return edges


def second_kernel(
    qg_a, qg_b, k_s, kt_s, v_s, sums_ref, in_a, in_b, here_ref, edge_ref, away_ref, out_ref, dk_s, dv_s
):
    def put_dq(at, n, dq):
        dq = (in_a, in_b)[at][n] + dq
        edges = edge_rows(dq)
        if at == 0:
            here_ref[n] = dq[0:DH]
            away_ref[n, DH:] = edges
        else:
            away_ref[n, 0:DH] = dq[0:DH]
            edge_ref[n] = edges

    gradients(sums_ref, (qg_a, qg_b), put_dq, k_s, kt_s, v_s, dk_s, dv_s)
    put_keys(out_ref, dk_s, dv_s)


def keys_sum_kernel(mine_ref, came_a, came_b, came_c, out_ref):
    total = mine_ref[0]
    for came in (came_a, came_b, came_c):
        total = total + came[...].astype(f32)
    out_ref[...] = total.astype(bf16)


def beside(x, first):
    none = jnp.zeros_like(x[0:2])
    above = jnp.where(first, jnp.concatenate([none, x[:-2]]), x)
    below = jnp.where(first, x, jnp.concatenate([x[2:], none]))
    return above, below


def pack_back_kernel(dq_ref, edge_ref, came_ref, keys_ref, other_ref, send_ref):
    first = lax.axis_index("c") == 0
    dq = (dq_ref[...] + came_ref[:, 0:DH]) * SCALE
    above, below = beside((edge_ref[...] + came_ref[:, DH:]) * SCALE, first)
    lane = lax.broadcasted_iota(jnp.int32, (HEADS, 24, 128), 2)
    edges = jnp.where(lane % 32 < COLS, above, below)
    lanes = jnp.zeros((128, 128 - DH), f32)
    row = lax.broadcasted_iota(jnp.int32, (HEADS, CELLS, 128), 1)

    def cells(ref, part):
        rows = ref[...].astype(f32)[part * DH : (part + 1) * DH].T
        return jnp.concatenate([rows, lanes], axis=1).reshape(HEADS, CELLS, 128)

    both = []
    for part in (0, 1):
        above, below = beside(cells(other_ref, part), first)
        half = CELLS // 2
        near = jnp.where(row < half, pltpu.roll(above, half, 1), pltpu.roll(below, half, 1))
        both.append(jnp.concatenate([cells(keys_ref, part), near], axis=1))
    dk, dv = both
    lane = lax.broadcasted_iota(jnp.int32, dk.shape, 2)
    mixed = jnp.where(lane < DH, dk, pltpu.roll(dv, DH, 2))
    rest = pltpu.roll(dv, REST - (128 - DH), 2)
    rest = jnp.concatenate([rest, jnp.zeros((HEADS, 8, 128), f32)], axis=1)
    lane = lax.broadcasted_iota(jnp.int32, edges.shape, 2)
    edges = jnp.where(lane < REST, edges, rest)
    send_ref[...] = jnp.concatenate([dq, edges, mixed], axis=1).astype(bf16)


def weights_kernel(patch_ref, qkv_ref, out_ref):
    for part in range(3):
        cols = slice(part * D, (part + 1) * D)
        both = jnp.dot(patch_ref[...], qkv_ref[:, cols], preferred_element_type=f32)
        both = both.reshape(16, 2, 8, D)
        left, right = both[:, 0].reshape(128, D), both[:, 1].reshape(128, D)
        outer = lax.broadcasted_iota(jnp.int32, (128, D), 0) % 8 < 4
        for at, rows in ((0, jnp.where(outer, left, right)), (256, jnp.where(outer, right, left))):
            high, low = split(rows)
            out_ref[at : at + 128, cols] = high
            out_ref[at + 128 : at + 256, cols] = low


def split(x):
    high = x.astype(bf16)
    return high, (x - high.astype(f32)).astype(bf16)


def iota(shape, dim):
    return lax.broadcasted_iota(jnp.int32, shape, dim)


def one_hot(where, value=1.0):
    return jnp.where(where, value, 0.0).astype(bf16)


def turn(weights, joined, pooled):
    def product(rows, values):
        out = jnp.dot(rows, values, preferred_element_type=f32)
        return out[0:128] + out[128:256]

    patch = product(weights[:, 0:D], joined)
    cells = jnp.concatenate(split(product(weights[:, D:], pooled)), axis=1)
    cell, token = iota((256, 256), 0) % 16, iota((256, 256), 1)
    mine = token // (POOL * COLS) * 4 + token % COLS // POOL
    beyond = CELLS + (token - TOK) // COLS * 4 + token % COLS // POOL
    holds = (cell == jnp.where(token < TOK, mine, beyond)) & (token < EXTENDED)
    patch = patch + jnp.dot(cells, one_hot(holds, 1.0 / POOL**2), preferred_element_type=f32)
    to, token = iota((EXTENDED, 256), 0), iota((EXTENDED, 256), 1)
    source = jnp.where(to < TOK, to % 8 * COLS, TOK + to % 2 * COLS) + column_of(to)
    return lax.dot_general(
        one_hot(token == source), jnp.concatenate(split(patch)), NT, preferred_element_type=f32
    )


def embed_kernel(back_ref, weights, turned_ref, joined, pooled, near_out, far_out, sheet):
    for h in range(0, HEADS, 2):
        pair = []
        wide = []
        for n in (h, h + 1):
            pair.append(back_ref[n, 0:TOK].astype(f32)[0:DH])
            edges = back_ref[n, 64 : 64 + 32].astype(f32)[DH - 64 :]
            wide += [edges, pltpu.roll(edges, 96, 1), pltpu.roll(edges, 64, 1)]
        rows = slice(h * DH, (h + 2) * DH)
        joined[rows, 0:TOK] = jnp.concatenate(pair).astype(bf16)
        joined[rows, TOK:] = jnp.concatenate(wide).astype(bf16)
    group = iota((DH, 128), 1) // 16
    fits = 128 - DH
    lane = iota((16, 128), 1)
    for h in range(0, HEADS, 4):
        keys, vals = [], []
        for n in range(h, h + 4):
            rest = back_ref[n, 64 : 64 + 32].astype(f32)[8 : 8 + 16]
            mixed = back_ref[n, 96:112].astype(f32)
            keys.append(mixed)
            vals.append(jnp.where(lane < fits, pltpu.roll(mixed, fits, 1), pltpu.roll(rest, 128 - (REST - fits), 1)))
        cells = keys + vals
        cells = jnp.concatenate(cells).T[0:DH]
        for part in (0, 1):
            for n in (0, 2):
                two = [jnp.where(group == 4 * part + k, cells, 0.0) for k in (n, n + 1)]
                rows = part * D + (h + n) * DH
                pooled[rows : rows + 2 * DH] = jnp.concatenate(two).astype(bf16)
    turned = turn(weights[0:256], joined[...], pooled[...])
    turned_ref[...] = turned.astype(bf16)
    left = right = turned[:, 0:128] + turned[:, 128:256]
    lane = iota((8, 128), 1)
    own = jnp.where(lane % 8 < 4, left[0:ROWS], right[TOK - ROWS : TOK])
    beyond = jnp.where(lane % 8 < 4, left[TOK : TOK + 8], pltpu.roll(right[EXTENDED - 8 :], 2, 0))
    sheet[...] = jnp.zeros_like(sheet)
    for u in range(16):
        sheet[pl.ds(u, ROWS, stride=8), :] += pltpu.roll(own, (128 - 8 * u) % 128, 1)
        if u >= 12:
            sheet[u - 8 : u - 7, :] += pltpu.roll(beyond, 128 - 8 * u, 1)[0:1]
        if u < 4:
            sheet[64 + u : 65 + u, :] += pltpu.roll(beyond, (128 - 8 * u) % 128, 1)[1:2]
    edges = sheet[4:68].T
    begins = lax.axis_index("yl") == 0
    near_out[...] = jnp.where(begins, edges[4:8], edges[0:4])
    far_out[...] = jnp.where(begins, edges[0:4], edges[4:8])


def column_of(row):
    far = row - TOK
    return jnp.where(row < TOK, row // 8, far // 8 * 4 + far % 8 // 2)


def fold_kernel(outer_ref, weights, joined, pooled, center_ref, sheet):
    outer = outer_ref[...].astype(f32)
    inner = turn(weights[256:512], joined[...], pooled[...])
    low_half = iota(outer.shape, 1) % 8 < 4
    halves = [jnp.where(low_half, outer, inner), jnp.where(low_half, inner, outer)]
    halves = [half.astype(bf16) for half in halves]
    sheet[...] = jnp.zeros_like(sheet)
    here = iota((EXTENDED, 256), 1) % 128 // 8 == column_of(iota((EXTENDED, 256), 0))
    to, at = iota((256, 256), 1), iota((256, 256), 0) % 128
    for pair in range(8):
        tile = one_hot((to // 128 + 2 * pair == at // 8) & (to % 8 == at % 8))
        for side in (0, 1):
            wide = jnp.dot(halves[side], tile, preferred_element_type=f32)
            wide = jnp.where(here, wide, 0.0)
            own = jnp.sum(wide[0:TOK].reshape(COLS, ROWS, 256), axis=0)
            edge = jnp.sum(wide[TOK:].reshape(4, 8, 256), axis=0)
            edge = edge + pltpu.roll(edge, 4, 0)
            edge = edge + pltpu.roll(edge, 2, 0)
            for k in (0, 1):
                u = 2 * pair + k
                lanes = slice(k * 128, (k + 1) * 128)
                sheet[side, pl.ds(u, ROWS, stride=8), :] += own[:, lanes]
                if u >= 12:
                    sheet[side, u - 8 : u - 7, :] += edge[0:1, lanes]
                if u < 4:
                    sheet[side, 64 + u : 65 + u, :] += edge[1:2, lanes]
    left = sheet[0, 4:68]
    right = sheet[1, 4:68]
    lane = lax.broadcasted_iota(jnp.int32, left.shape, 1)
    center = jnp.where(lane < 124, pltpu.roll(left, 124, 1), 0.0)
    center_ref[...] = center + jnp.where(lane >= 4, pltpu.roll(right, 4, 1), 0.0)


def cols_kernel(center_ref, near_ref, far_ref, out_ref):
    begins = lax.axis_index("yl") == 0
    left = jnp.where(begins, far_ref[...], near_ref[...])
    right = jnp.where(begins, near_ref[...], far_ref[...])
    quiet = jnp.zeros((120, 64), f32)
    out_ref[...] = center_ref[...] + jnp.concatenate([left, quiet, right]).T


def swapped(x, axis, by):
    peers = lax.axis_size(axis)
    return lax.ppermute(x, axis, [(i, i ^ by) for i in range(peers)])


def neighbours(x, axis):
    peers = lax.axis_size(axis)
    pairs = [(i, i + 1) for i in range(1, peers - 1, 2)]
    return lax.ppermute(x, axis, pairs + [(target, source) for source, target in pairs])


def cost(products):
    flops = products * 4 * QUERIES * HALF * 256
    return pl.CostEstimate(flops=flops, bytes_accessed=2**20, transcendentals=2 * QUERIES * HALF)


def on_device(queries, key_states, values, saved_out, grad_out, w_qkv, w_patch):
    tokens = pltpu.VMEM((TOK, D), bf16)
    cells = pltpu.VMEM((2, 4, D), bf16)
    packed = (HEADS, 2 * FPAD + 16, TOK)
    dma = pltpu.SemaphoreType.DMA
    send = call(
        pack_kernel,
        jax.ShapeDtypeStruct(packed, bf16),
        None,
        [tokens, tokens, tokens, cells, cells, pltpu.VMEM(packed, bf16), dma((14,)), dma((6,))],
        [ANYWHERE] * 5,
        out_specs=ANYWHERE,
    )(
        queries.reshape(TOK, D),
        grad_out.reshape(TOK, D),
        saved_out.reshape(TOK, D),
        key_states,
        values,
    )
    got = lax.all_to_all(send, HEAD_AXES, 0, 0, tiled=True)
    kv = call(
        keys_kernel,
        jax.ShapeDtypeStruct((2 * DH, 128), bf16),
        4,
        [pltpu.VMEM((HEADS, 16, 128), bf16), dma(())],
        [ANYWHERE],
    )(got)
    kv_1, kv_2, kv_6 = [swapped(kv, "z", by) for by in (1, 2, 6)]
    kv_37 = swapped(jnp.stack([kv_2, kv_6]), "z", 1)
    kv_45 = swapped(jnp.stack([kv, kv_1]), "z", 4)
    there = swapped(got, "c", 1)
    sums = jax.ShapeDtypeStruct((2, HEADS, TOK), f32)
    keys = pltpu.VMEM((HALF, 128), bf16)
    mine = call(first_sums_kernel, sums, 24, [keys], cost_estimate=cost(1))(got, there, kv, kv_1, kv_2, kv_6)
    kv_37, kv_45, mine = lax.optimization_barrier((kv_37, kv_45, mine))
    mine = call(second_sums_kernel, sums, 24, [keys], cost_estimate=cost(1))(got, there, kv_37, kv_45, mine)
    mine, kv_45 = lax.optimization_barrier((mine, kv_45))
    came = swapped(mine, "c", 1)
    layout = [jax.ShapeDtypeStruct(shape, bf16) for shape in ((HALF, 128), (FPAD, HALF), (HALF, 128))]
    layouts = call(layouts_kernel, layout * 2, 8, cost_estimate=SMALL)(kv, kv_1, kv_2, kv_6, kv_37, kv_45)
    came, layouts = lax.optimization_barrier((came, layouts))
    scratch = [pltpu.VMEM((HALF, 128), f32)] * 2
    dq = [jax.ShapeDtypeStruct((HEADS, FPAD, TOK), f32)] * 2
    block = (4, 2 * DH, 128)
    sums, dq_here, dq_there, grads = call(
        first_kernel, [sums] + dq + [jax.ShapeDtypeStruct(block, bf16)], 32, scratch, cost_estimate=cost(5)
    )(got, there, *layouts[:3], mine, came)
    came = swapped(grads, "z", 1)
    shapes = [jax.ShapeDtypeStruct((HEADS, rows, TOK), f32) for rows in (DH, 24, DH + 24)]
    *dq, grads = call(
        second_kernel,
        shapes + [jax.ShapeDtypeStruct(block, f32)],
        32,
        scratch,
        cost_estimate=cost(5),
    )(got, there, *layouts[3:], sums, dq_here, dq_there)
    dq, grads, came = lax.optimization_barrier((dq, grads, came))
    dq_here, edges, away = dq
    away = swapped(away, "c", 1)
    mine = grads + came.astype(f32)
    mine, w_qkv, w_patch = lax.optimization_barrier((mine, w_qkv, w_patch))
    came = [swapped(mine[n + 1].astype(bf16), "z", by) for n, by in enumerate(EVEN)]
    weights = call(
        weights_kernel, jax.ShapeDtypeStruct((512, 3 * D), bf16), 24, cost_estimate=SMALL
    )(w_patch, w_qkv)
    came, weights = lax.optimization_barrier((came, weights))
    keys = call(keys_sum_kernel, jax.ShapeDtypeStruct((2 * DH, 128), bf16), 4)(mine[0:1], *came)
    other = swapped(keys, "c", 1)
    send = call(pack_back_kernel, jax.ShapeDtypeStruct((HEADS, 112, TOK), bf16), 16)(
        dq_here, edges, away, keys, other
    )
    back = lax.all_to_all(send, HEAD_AXES, 0, 0, tiled=True)
    strip = jax.ShapeDtypeStruct((4, 64), f32)
    shapes = [(EXTENDED, 256), (D, 2 * TOK), (2 * D, 128)]
    *parts, to_near, to_far = call(
        embed_kernel,
        [jax.ShapeDtypeStruct(shape, bf16) for shape in shapes] + [strip, strip],
        28,
        [pltpu.VMEM((72, 128), f32)],
    )(back, weights)
    near, far = swapped(to_near, "yl", 1), neighbours(to_far, COL)
    center = call(
        fold_kernel,
        jax.ShapeDtypeStruct((64, 128), f32),
        20,
        [pltpu.VMEM((2, 72, 128), f32)],
        cost_estimate=SMALL,
    )(parts[0], weights, *parts[1:])
    near, far, center = lax.optimization_barrier((near, far, center))
    return call(cols_kernel, jax.ShapeDtypeStruct((64, 128), f32), 4)(center, near, far)


def solution(mesh):
    fine = Mesh(mesh.devices.reshape(2, 4, 2, 8, 2), ("yh", "x", "c", "z", "yl"))
    split = P(BLK, COL, None)
    return jax.shard_map(
        on_device,
        mesh=fine,
        in_specs=(split, split, split, split, split, P(), P()),
        out_specs=P(BLK, COL),
        check_vma=False,
    )
```
